128 devices in a mesh: blk: 8 (over x_lo, y), feat: 16 (over x_hi, z, core).
Axes of the slice: x: 4 (x_hi: 2, x_lo: 2; x = x_hi * 2 + x_lo), y: 4, z: 4, core: 2. Of those that a mesh axis runs over, the one named last changes fastest.
Arguments:
- node_feats: bfloat16 [256, 65536], P('feat', 'blk'), may hold values from -6 to 6
- weight: bfloat16 [256, 256], P('feat'), may hold values from -0.375 to 0.375
- tiles: bfloat16 [512, 32, 128, 128], P('blk'), may hold values from -0.09375 to 0.09375
- block_cols: int32 [512, 32], P('blk'), may hold values from 0 to 511, all different within a row
- cotangent: bfloat16 [256, 65536], P('feat', 'blk'), may hold values from -6 to 6
Outputs:
- hidden: bfloat16 [256, 65536], P('feat', 'blk')
- weight_grad: float32 [256, 256], P('feat')
- feats_grad: bfloat16 [256, 65536], P('feat', 'blk')
The draws below stay inside these ranges and needn't reach their ends.
Inputs may be any that keep to these rules, and one draw needn't show every extreme that they name: `block_cols`: within a block row the 32 source blocks differ; every source block is named by some block row.
All inputs are finite; a program needn't handle non-finite values.
Results may differ from the reference program's by a relative error of at most 0.02.
Values may be sent and summed in bfloat16 or wider, within the bound.
No kernel may reach another device: no remote copies, remote signals or barrier semaphores. Data moves between devices by JAX's collectives and lax.ppermute only.
A program may use at most 192 MiB of HBM per device.

```python
import jax
import jax.numpy as jnp
from jax import lax

D = 256
P_SIZE = 32
NODES = 65536
COL_BLOCKS = 512


def block_scale(key, shape, cuts, smallest, largest):
    def one(dim, blocks):
        heights = jax.random.uniform(jax.random.fold_in(jax.random.fold_in(key, 6), dim), (blocks,), jnp.float32, smallest / len(cuts), largest / len(cuts))
        return jnp.repeat(jnp.exp(heights), shape[dim] // blocks).reshape((-1,) + (1,) * (len(shape) - dim - 1))

    factor_of = one(*cuts[0])
    for cut in cuts[1:]:
        factor_of = factor_of * one(*cut)
    return factor_of


def picks_of(stream_key, rows, number_of, top, lift):
    sequence = jax.random.permutation(jax.random.fold_in(stream_key, 1), number_of)
    boost = sequence
    for power in range(3):
        boost = boost * boost // number_of
    boost = boost * lift // number_of
    tickets = jax.random.randint(jax.random.fold_in(stream_key, 2), (rows, number_of), 0, 4096) + boost
    holders = jax.random.permutation(jax.random.fold_in(stream_key, 3), rows)[jnp.arange(number_of) % rows]
    tickets = jnp.where(jnp.arange(rows)[:, None] == holders[None, :], 1 << 14, tickets)
    priority = tickets * number_of + jnp.arange(number_of)
    return lax.top_k(priority.astype(jnp.int32), top)[1].astype(jnp.int32)


def centred(stream_key, extent, spread, limit, cuts=(), kind=jnp.bfloat16):
    gain = block_scale(stream_key, extent, cuts, -0.22, 0.18) if cuts else 1.0
    result = jax.random.normal(stream_key, extent, jnp.float32) * spread * gain
    return jnp.minimum(jnp.maximum(result, -limit), limit).astype(kind)


def setup_inputs(seed: int = 0) -> dict:
    seeds = jax.random.split(jax.random.key(seed), 6)
    node_feats = centred(seeds[0], (D, NODES), 1.0, 6.0, ((0, 16), (1, 8)))
    weight = centred(seeds[1], (D, D), D ** -0.5, 0.375, ((0, 16),))
    tiles = centred(seeds[2], (COL_BLOCKS, P_SIZE, 128, 128), (P_SIZE * 128) ** -0.5, 0.09375, ((0, 8),))
    block_cols = picks_of(seeds[3], COL_BLOCKS, COL_BLOCKS, P_SIZE, 512)
    cotangent = centred(seeds[4], (D, NODES), 1.0, 6.0, ((0, 16), (1, 8)))
    return {"node_feats": node_feats, "weight": weight, "tiles": tiles, "block_cols": block_cols, "cotangent": cotangent}


def reference(node_feats, weight, tiles, block_cols, cotangent):
    width, total = node_feats.shape
    nblocks = total // 128
    blocked = node_feats.reshape(width, nblocks, 128)

    def aggregate(item):
        cols, tile_row = item
        picked = jnp.take(blocked, cols.astype(jnp.int32), axis=1)
        return jnp.einsum('dpk,pjk->dj', picked.astype(jnp.float32), tile_row.astype(jnp.float32))

    agg_blocks = lax.map(aggregate, (block_cols, tiles))
    aggregated = jnp.transpose(agg_blocks, (1, 0, 2)).reshape(width, total).astype(jnp.bfloat16)
    pre = jnp.dot(weight.T, aggregated, preferred_element_type=jnp.float32)
    hidden = jax.nn.silu(pre).astype(jnp.bfloat16)
    sig = jax.nn.sigmoid(pre)
    pre_grad = (cotangent.astype(jnp.float32) * sig * (1.0 + pre * (1.0 - sig))).astype(jnp.bfloat16)
    weight_grad = jnp.dot(aggregated, pre_grad.T, preferred_element_type=jnp.float32)
    agg_grad = jnp.dot(weight, pre_grad, preferred_element_type=jnp.float32).astype(jnp.bfloat16)
    grad_blocks = jnp.transpose(agg_grad.reshape(width, nblocks, 128), (1, 0, 2))

    def scatter_step(accum, item):
        grad_row, cols, tile_row = item
        contrib = jnp.einsum('dj,pjk->dpk', grad_row.astype(jnp.float32), tile_row.astype(jnp.float32))
        return accum.at[:, cols.astype(jnp.int32)].add(contrib), None

    start = jnp.zeros((width, nblocks, 128), jnp.float32)
    accum, unused = lax.scan(scatter_step, start, (grad_blocks, block_cols, tiles))
    feats_grad = accum.reshape(width, total).astype(jnp.bfloat16)
    return hidden, weight_grad, feats_grad
```

```python
import functools

import jax
import jax.numpy as jnp
from jax import lax
from jax.experimental import pallas as pl
from jax.experimental.pallas import tpu as pltpu
from jax.sharding import PartitionSpec as P

BF16 = jnp.bfloat16
F32 = jnp.float32
ANY = pl.BlockSpec(memory_space=pl.ANY)
VMEM = pl.BlockSpec(memory_space=pltpu.VMEM)
SMEM = pl.BlockSpec(memory_space=pltpu.SMEM)

STEPS = ((0, 0), (0, 1), (0, 3), (1, 0), (0, 2), (1, 1), (1, 3), (1, 2))
SLABS = 8
HALF = 16
PAIR = 32
LOCAL = 8192
NODES = 65536
SLOTS = 32
ROWS = 32


def _index(x, y):
    return x * 4 + y


def _from_step(step):
    dx, dy = step
    return [(_index(x ^ dx, (y + dy) % 4), _index(x, y)) for x in range(2) for y in range(4)]


def _to_step(step):
    return [(b, a) for a, b in _from_step(step)]


CORE_SWAP = [(f, f ^ 1) for f in range(16)]
SAME_CORE = [list(range(0, 16, 2)), list(range(1, 16, 2))]


def swap(a):
    return lax.ppermute(a, "feat", CORE_SWAP)


def load_kernel(info, tiles, out, sems):
    core = info[0]
    copies = []
    for g in range(8):
        copies.append(
            pltpu.make_async_copy(
                tiles.at[pl.ds(8 * g + 4 * core, 4)], out.at[pl.ds(4 * g, 4)], sems.at[g]
            )
        )
    for c in copies:
        c.start()
    for c in copies:
        c.wait()


def load_tiles(info, tiles):
    return pl.pallas_call(
        load_kernel,
        out_shape=pltpu.VMEM((ROWS, SLOTS, 128, 128), BF16),
        in_specs=[SMEM, ANY],
        out_specs=VMEM,
        scratch_shapes=[pltpu.SemaphoreType.DMA((8,))],
        compiler_params=pltpu.CompilerParams(vmem_limit_bytes=2 << 20),
        cost_estimate=pl.CostEstimate(flops=0, bytes_accessed=64 << 20, transcendentals=0),
        name="load_tiles",
    )(info, tiles)


def row_of(core, local):
    return 8 * (local // 4) + 4 * core + local % 4


def lanes_of(block):
    return pl.ds(pl.multiple_of(block * 128, 128), 128)


def forward_kernel(info, cols, tiles, *refs):
    pieces, (out, feats, sems) = refs[:16], refs[16:]
    core = info[0]
    copies = []
    for d in range(SLABS):
        lanes = pl.ds(pl.multiple_of(info[1 + d] * LOCAL, LOCAL), LOCAL)
        for h in range(2):
            copies.append(
                pltpu.make_async_copy(
                    pieces[2 * d + h], feats.at[pl.ds(HALF * h, HALF), lanes], sems.at[2 * d + h]
                )
            )
    for c in copies:
        c.start()
    for c in copies:
        c.wait()

    def row(local, carry):
        r = row_of(core, local)
        total = jnp.zeros((PAIR, 128), F32)
        for p in range(0, SLOTS, 2):
            picked = jnp.concatenate(
                [feats[:, lanes_of(cols[r, p + i])] for i in range(2)], axis=1
            )
            pair = jnp.concatenate([tiles[local, p + i] for i in range(2)], axis=1)
            total += lax.dot_general(
                picked, pair, (((1,), (1,)), ((), ())), preferred_element_type=F32
            )
        out[local // 4, :, lanes_of(local % 4)] = total.astype(BF16)
        return carry

    lax.fori_loop(0, ROWS, row, 0)


def forward(info, cols, tiles, pieces):
    return pl.pallas_call(
        forward_kernel,
        out_shape=jax.ShapeDtypeStruct((8, PAIR, 512), BF16),
        in_specs=[SMEM, SMEM, VMEM] + [ANY] * 16,
        out_specs=VMEM,
        scratch_shapes=[pltpu.VMEM((PAIR, NODES), BF16), pltpu.SemaphoreType.DMA((16,))],
        compiler_params=pltpu.CompilerParams(vmem_limit_bytes=12 << 20),
        cost_estimate=pl.CostEstimate(
            flops=8 * 2 * 1024 * 128 * 128 * 32, bytes_accessed=8 << 20, transcendentals=0
        ),
        name="forward",
    )(info, cols, tiles, *pieces)


def flip_halves(value, core):
    parts = []
    for g in range(8):
        a = value[PAIR * g : PAIR * g + HALF]
        b = value[PAIR * g + HALF : PAIR * (g + 1)]
        parts += [jnp.where(core == 1, b, a), jnp.where(core == 1, a, b)]
    return jnp.concatenate(parts, axis=0)


def dense_kernel(info, agg_ref, side_ref, grad_ref, tail_ref):
    core = info[0]
    agg = agg_ref[...]
    weight = flip_halves(side_ref[:, 512:], core)
    pre = lax.dot_general(weight, agg, (((0,), (0,)), ((), ())), preferred_element_type=F32)
    sig = 1.0 / (1.0 + jnp.exp(-pre))
    tail_ref[:, :512] = (pre * sig).astype(BF16)
    pre_grad = (side_ref[:, :512].astype(F32) * sig * (1.0 + pre * (1.0 - sig))).astype(BF16)
    grad_ref[...] = jnp.dot(weight, pre_grad, preferred_element_type=F32).astype(BF16)
    wgrad = lax.dot_general(agg, pre_grad, (((1,), (1,)), ((), ())), preferred_element_type=F32)
    tail_ref[:, 512:] = flip_halves(wgrad, core).astype(BF16)


def dense(info, agg, side):
    return pl.pallas_call(
        dense_kernel,
        out_shape=(
            jax.ShapeDtypeStruct((256, 512), BF16),
            jax.ShapeDtypeStruct((256, 768), BF16),
        ),
        in_specs=[SMEM, VMEM, VMEM],
        out_specs=(VMEM, VMEM),
        compiler_params=pltpu.CompilerParams(vmem_limit_bytes=8 << 20),
        cost_estimate=pl.CostEstimate(
            flops=3 * 2 * 256 * 256 * 512, bytes_accessed=2 << 20, transcendentals=256 * 512
        ),
        name="dense",
    )(info, agg, side)


def backward_kernel(info, cols, tiles, grad, *refs):
    outs, (total, staged, sems) = refs[:16], refs[16:]
    core = info[0]

    def clear(i, carry):
        total[:, pl.ds(pl.multiple_of(i * 2048, 2048), 2048)] = jnp.zeros((PAIR, 2048), F32)
        return carry

    lax.fori_loop(0, NODES // 2048, clear, 0)

    def row(local, carry):
        r = row_of(core, local)
        g = grad[local // 4, :, lanes_of(local % 4)]
        for first in range(0, SLOTS, 8):
            blocks = [lanes_of(cols[r, first + i]) for i in range(8)]
            terms = []
            for i in range(0, 8, 2):
                pair = jnp.concatenate([tiles[local, first + i + k] for k in range(2)], axis=1)
                both = jnp.dot(g, pair, preferred_element_type=F32)
                terms += [both[:, :128], both[:, 128:]]
            sums = [total[:, blocks[i]] + terms[i] for i in range(8)]
            for i in range(8):
                total[:, blocks[i]] = sums[i]
        return carry

    lax.fori_loop(0, ROWS, row, 0)

    copies = []
    for h in (1, 0):
        rows = pl.ds(HALF * h, HALF)
        for d in range(SLABS):
            base = info[1 + d] * LOCAL
            lanes = pl.ds(pl.multiple_of(base, LOCAL), LOCAL)
            staged[rows, lanes] = total[rows, lanes].astype(BF16)
            copy = pltpu.make_async_copy(
                staged.at[rows, lanes], outs[8 * h + d], sems.at[8 * h + d]
            )
            copy.start()
            copies.append(copy)
    for c in copies:
        c.wait()


def backward(info, cols, tiles, grad):
    return pl.pallas_call(
        backward_kernel,
        out_shape=[jax.ShapeDtypeStruct((HALF, LOCAL), BF16)] * 16,
        in_specs=[SMEM, SMEM, VMEM, VMEM],
        out_specs=[ANY] * 16,
        scratch_shapes=[
            pltpu.VMEM((PAIR, NODES), F32),
            pltpu.VMEM((PAIR, NODES), BF16),
            pltpu.SemaphoreType.DMA((16,)),
        ],
        compiler_params=pltpu.CompilerParams(vmem_limit_bytes=20 << 20),
        cost_estimate=pl.CostEstimate(
            flops=8 * 2 * 1024 * 128 * 128 * 32, bytes_accessed=8 << 20, transcendentals=0
        ),
        name="backward",
    )(info, cols, tiles, grad)


def per_device(node_feats, weight, tiles, block_cols, cotangent):
    core = lax.axis_index("feat") % 2
    slab = lax.axis_index("blk")
    x, y = slab // 4, slab % 4
    info = jnp.stack([core] + [(x ^ dx) * 4 + (y + dy) % 4 for dx, dy in STEPS]).astype(jnp.int32)

    blocks = [node_feats] + [
        lax.ppermute(node_feats, "blk", _from_step(step)) for step in STEPS[1:]
    ]
    pieces = []
    for block in blocks:
        pieces += [block, swap(block)]
    held = pltpu.with_memory_space_constraint(load_tiles(info, tiles), pltpu.VMEM)

    side = jnp.concatenate(
        [
            jnp.transpose(cotangent.reshape(HALF, 16, 512), (1, 0, 2)),
            jnp.broadcast_to(weight[None], (16, HALF, 256)),
        ],
        axis=2,
    )
    side = lax.all_to_all(side, "feat", 0, 0, tiled=True).reshape(256, 768)

    agg = forward(info, block_cols, held, pieces)
    agg = lax.all_to_all(agg, "feat", 0, 0, axis_index_groups=SAME_CORE, tiled=True)
    grad, tail = dense(info, agg.reshape(256, 512), side)
    grad = lax.all_to_all(
        grad.reshape(8, PAIR, 512), "feat", 0, 0, axis_index_groups=SAME_CORE, tiled=True
    )
    parts = backward(info, block_cols, held, grad)
    own, other = parts[:8], parts[8:]
    summed = [own[d].astype(F32) + swap(other[d]).astype(F32) for d in range(SLABS)]
    total = summed[0]
    for d in range(1, SLABS):
        total = total + lax.ppermute(summed[d].astype(BF16), "blk", _to_step(STEPS[d])).astype(F32)
    feats_grad = total.astype(BF16)

    tail = lax.all_to_all(tail.reshape(16, HALF, 768), "feat", 0, 0, tiled=True)
    hidden = jnp.transpose(tail[:, :, :512], (1, 0, 2)).reshape(HALF, LOCAL)
    wgrad = jnp.sum(tail[:, :, 512:].astype(F32), axis=0)
    wgrad = lax.all_to_all(
        jnp.broadcast_to(wgrad[None], (SLABS, HALF, 256)), "blk", 0, 0, tiled=True
    )
    weight_grad = jnp.sum(wgrad, axis=0)
    return hidden, weight_grad, feats_grad


def solution(mesh):
    placed = (
        P("feat", "blk"),
        P("feat", None),
        P("blk", None, None, None),
        P("blk", None),
        P("feat", "blk"),
    )
    return jax.shard_map(
        per_device,
        mesh=mesh,
        in_specs=placed,
        out_specs=(P("feat", "blk"), P("feat", None), P("feat", "blk")),
        check_vma=False,
    )
```

```python
import functools

import jax
import jax.numpy as jnp
from jax import lax
from jax.experimental import pallas as pl
from jax.experimental.pallas import tpu as pltpu
from jax.sharding import PartitionSpec as P

BF16 = jnp.bfloat16
F32 = jnp.float32
ANY = pl.BlockSpec(memory_space=pl.ANY)
VMEM = pl.BlockSpec(memory_space=pltpu.VMEM)
SMEM = pl.BlockSpec(memory_space=pltpu.SMEM)

STEPS = ((0, 0), (0, 1), (0, 3), (1, 0), (0, 2), (1, 1), (1, 3), (1, 2))
SLABS = 8
HALF = 16
PAIR = 32
LOCAL = 8192
NODES = 65536
SLOTS = 32
ROWS = 32
HELD = 16
RING = 6


def _index(x, y):
    return x * 4 + y


def _from_step(step):
    dx, dy = step
    return [(_index(x ^ dx, (y + dy) % 4), _index(x, y)) for x in range(2) for y in range(4)]


def _to_step(step):
    return [(b, a) for a, b in _from_step(step)]


CORE_SWAP = [(f, f ^ 1) for f in range(16)]
SAME_CORE = [list(range(0, 16, 2)), list(range(1, 16, 2))]


def swap(a):
    return lax.ppermute(a, "feat", CORE_SWAP)


def row_of(core, local):
    return 8 * (local // 4) + 4 * core + local % 4


def lanes_of(block):
    return pl.ds(pl.multiple_of(block * 128, 128), 128)


def prepare_kernel(info, first, second, ship, rest):
    core = info[0]
    low = jnp.where(core == 0, first[...], second[...])
    high = jnp.where(core == 0, second[...], first[...])
    both = jnp.concatenate([low, high], axis=0)
    tiles = []
    for m in range(16):
        stacked = jnp.concatenate(
            [both[:, 128 * q : 128 * (q + 1)] for q in range(4 * m, 4 * m + 4)], axis=0
        )
        tiles.append(stacked.T)
    for m in range(8):
        lanes = slice(128 * m, 128 * (m + 1))
        ship[:, lanes] = jnp.where(core == 0, tiles[m], tiles[8 + m])
        rest[:, lanes] = jnp.where(core == 0, tiles[8 + m], tiles[m])


def prepare(info, first, second):
    return pl.pallas_call(
        prepare_kernel,
        out_shape=[jax.ShapeDtypeStruct((128, 1024), BF16)] * 2,
        in_specs=[SMEM, VMEM, VMEM],
        out_specs=[VMEM, VMEM],
        compiler_params=pltpu.CompilerParams(vmem_limit_bytes=8 << 20),
        cost_estimate=pl.CostEstimate(flops=0, bytes_accessed=1 << 20, transcendentals=0),
        name="prepare",
    )(info, first, second)


def load_kernel(info, tiles, out, sems):
    core = info[0]
    copies = []
    for g in range(HELD // 4):
        copies.append(
            pltpu.make_async_copy(
                tiles.at[pl.ds(8 * g + 4 * core, 4)], out.at[pl.ds(4 * g, 4)], sems.at[g]
            )
        )
    for c in copies:
        c.start()
    for c in copies:
        c.wait()


def load_tiles(info, tiles):
    return pl.pallas_call(
        load_kernel,
        out_shape=pltpu.VMEM((HELD, SLOTS, 128, 128), BF16),
        in_specs=[SMEM, ANY],
        out_specs=VMEM,
        scratch_shapes=[pltpu.SemaphoreType.DMA((HELD // 4,))],
        compiler_params=pltpu.CompilerParams(vmem_limit_bytes=2 << 20),
        cost_estimate=pl.CostEstimate(flops=0, bytes_accessed=32 << 20, transcendentals=0),
        name="load_tiles",
    )(info, tiles)


class Stream:
    def __init__(self, core, tiles, ring, sems):
        self.core, self.tiles, self.ring, self.sems = core, tiles, ring, sems

    def copy(self, i):
        return pltpu.make_async_copy(
            self.tiles.at[row_of(self.core, HELD + i)],
            self.ring.at[lax.rem(i, RING)],
            self.sems.at[lax.rem(i, RING)],
        )

    def begin(self):
        for i in range(RING):
            self.copy(jnp.int32(i)).start()

    def next(self, i):
        @pl.when(i + RING < ROWS - HELD)
        def _():
            self.copy(i + RING).start()


def forward_kernel(info, cols, held, tiles, *refs):
    pieces, (out, feats, masks, ring, sems, ring_sems) = refs[:16], refs[16:]
    core = info[0]
    stream = Stream(core, tiles, ring, ring_sems)
    copies = []
    for d in range(SLABS):
        for h in range(2):
            half = jnp.where(core == h, 0, 1)
            at = pl.multiple_of(info[1 + d] * 2048 + half * 1024, 1024)
            copies.append(
                pltpu.make_async_copy(
                    pieces[2 * d + h], feats.at[:, pl.ds(at, 1024)], sems.at[2 * d + h]
                )
            )
    for c in copies:
        c.start()
    stream.begin()
    group = lax.broadcasted_iota(jnp.int32, (16, 128), 1) // PAIR
    for g in range(4):
        masks[g] = jnp.where(group == g, 1.0, 0.0).astype(BF16)
    for c in copies:
        c.wait()

    def picked(block):
        lanes = lanes_of(block // 4)
        mask = masks[lax.rem(block, 4)]
        return [feats[pl.ds(16 * i, 16), lanes] * mask for i in range(8)]

    def row(local, tile_of):
        r = row_of(core, local)
        total = jnp.zeros((128, 128), F32)
        for p in range(0, SLOTS, 2):
            right = jnp.concatenate(picked(cols[r, p]) + picked(cols[r, p + 1]), axis=0)
            left = jnp.concatenate([tile_of(p), tile_of(p + 1)], axis=1)
            total += jnp.dot(left, right, preferred_element_type=F32)
        turned = total.T
        folded = turned[0:32] + turned[32:64] + turned[64:96] + turned[96:128]
        out[local // 4, :, lanes_of(lax.rem(local, 4))] = folded.astype(BF16)

    def step(i, carry):
        stream.copy(i).wait()
        slot = lax.rem(i, RING)
        row(i, lambda p: held[i, p])
        row(HELD + i, lambda p: ring[slot, p])
        stream.next(i)
        return carry

    lax.fori_loop(0, HELD, step, 0)


def forward(info, cols, held, tiles, pieces):
    return pl.pallas_call(
        forward_kernel,
        out_shape=jax.ShapeDtypeStruct((8, PAIR, 512), BF16),
        in_specs=[SMEM, SMEM, VMEM, ANY] + [ANY] * 16,
        out_specs=VMEM,
        scratch_shapes=[
            pltpu.VMEM((128, NODES * PAIR // 128), BF16),
            pltpu.VMEM((4, 16, 128), BF16),
            pltpu.VMEM((RING, SLOTS, 128, 128), BF16),
            pltpu.SemaphoreType.DMA((16,)),
            pltpu.SemaphoreType.DMA((RING,)),
        ],
        compiler_params=pltpu.CompilerParams(vmem_limit_bytes=14 << 20),
        cost_estimate=pl.CostEstimate(
            flops=8 * 2 * 1024 * 128 * 128 * 32, bytes_accessed=8 << 20, transcendentals=0
        ),
        name="forward",
    )(info, cols, held, tiles, *pieces)


def dense_kernel(agg_ref, side_ref, grad_ref, tail_ref):
    agg = agg_ref[...]
    weight = side_ref[:, 512:]
    pre = lax.dot_general(weight, agg, (((0,), (0,)), ((), ())), preferred_element_type=F32)
    sig = 1.0 / (1.0 + jnp.exp(-pre))
    tail_ref[:, :512] = (pre * sig).astype(BF16)
    pre_grad = (side_ref[:, :512].astype(F32) * sig * (1.0 + pre * (1.0 - sig))).astype(BF16)
    grad_ref[...] = jnp.dot(weight, pre_grad, preferred_element_type=F32).astype(BF16)
    wgrad = lax.dot_general(agg, pre_grad, (((1,), (1,)), ((), ())), preferred_element_type=F32)
    tail_ref[:, 512:] = wgrad.astype(BF16)


def dense(agg, side):
    return pl.pallas_call(
        dense_kernel,
        out_shape=(
            jax.ShapeDtypeStruct((256, 512), BF16),
            jax.ShapeDtypeStruct((256, 768), BF16),
        ),
        in_specs=[VMEM, VMEM],
        out_specs=(VMEM, VMEM),
        compiler_params=pltpu.CompilerParams(vmem_limit_bytes=8 << 20),
        cost_estimate=pl.CostEstimate(
            flops=3 * 2 * 256 * 256 * 512, bytes_accessed=2 << 20, transcendentals=256 * 512
        ),
        name="dense",
    )(agg, side)


def backward_kernel(info, cols, held, tiles, grad, *refs):
    outs, (total, ring, ring_sems) = refs[:16], refs[16:]
    core = info[0]
    stream = Stream(core, tiles, ring, ring_sems)
    stream.begin()

    def clear(i, carry):
        total[:, pl.ds(pl.multiple_of(i * 2048, 2048), 2048)] = jnp.zeros((PAIR, 2048), F32)
        return carry

    lax.fori_loop(0, NODES // 2048, clear, 0)

    def row(local, tile_of):
        r = row_of(core, local)
        g = grad[local // 4, :, lanes_of(lax.rem(local, 4))]
        for first in range(0, SLOTS, 8):
            blocks = [lanes_of(cols[r, first + i]) for i in range(8)]
            terms = []
            for i in range(first, first + 8, 2):
                pair = jnp.concatenate([tile_of(i), tile_of(i + 1)], axis=1)
                both = jnp.dot(g, pair, preferred_element_type=F32)
                terms += [both[:, :128], both[:, 128:]]
            sums = [total[:, blocks[i]] + terms[i] for i in range(8)]
            for i in range(8):
                total[:, blocks[i]] = sums[i]

    def step(i, carry):
        stream.copy(i).wait()
        slot = lax.rem(i, RING)
        row(i, lambda p: held[i, p])
        row(HELD + i, lambda p: ring[slot, p])
        stream.next(i)
        return carry

    lax.fori_loop(0, HELD, step, 0)

    own = pl.ds(pl.multiple_of(HALF * core, HALF), HALF)
    other = pl.ds(pl.multiple_of(HALF * (1 - core), HALF), HALF)
    for d in range(SLABS):
        lanes = pl.ds(pl.multiple_of(info[1 + d] * LOCAL, LOCAL), LOCAL)
        outs[d][...] = total[own, lanes].astype(BF16)
        outs[8 + d][...] = total[other, lanes].astype(BF16)


def backward(info, cols, held, tiles, grad):
    return pl.pallas_call(
        backward_kernel,
        out_shape=[jax.ShapeDtypeStruct((HALF, LOCAL), BF16)] * 16,
        in_specs=[SMEM, SMEM, VMEM, ANY, VMEM],
        out_specs=[VMEM] * 16,
        scratch_shapes=[
            pltpu.VMEM((PAIR, NODES), F32),
            pltpu.VMEM((RING, SLOTS, 128, 128), BF16),
            pltpu.SemaphoreType.DMA((RING,)),
        ],
        compiler_params=pltpu.CompilerParams(vmem_limit_bytes=20 << 20),
        cost_estimate=pl.CostEstimate(
            flops=8 * 2 * 1024 * 128 * 128 * 32, bytes_accessed=8 << 20, transcendentals=0
        ),
        name="backward",
    )(info, cols, held, tiles, grad)


def per_device(node_feats, weight, tiles, block_cols, cotangent):
    core = lax.axis_index("feat") % 2
    slab = lax.axis_index("blk")
    x, y = slab // 4, slab % 4
    info = jnp.stack([core] + [(x ^ dx) * 4 + (y + dy) % 4 for dx, dy in STEPS]).astype(jnp.int32)

    ship, rest = prepare(info, node_feats, swap(node_feats))
    pieces = [ship, rest]
    for step in STEPS[1:]:
        block = lax.ppermute(ship, "blk", _from_step(step))
        pieces += [block, swap(block)]
    held = pltpu.with_memory_space_constraint(load_tiles(info, tiles), pltpu.VMEM)

    side = jnp.concatenate(
        [
            jnp.transpose(cotangent.reshape(HALF, 16, 512), (1, 0, 2)),
            jnp.broadcast_to(weight[None], (16, HALF, 256)),
        ],
        axis=2,
    )
    side = lax.all_to_all(side, "feat", 0, 0, tiled=True).reshape(256, 768)

    agg = forward(info, block_cols, held, tiles, pieces)
    agg = lax.all_to_all(agg, "feat", 0, 0, axis_index_groups=SAME_CORE, tiled=True)
    grad, tail = dense(agg.reshape(256, 512), side)
    grad = lax.all_to_all(
        grad.reshape(8, PAIR, 512), "feat", 0, 0, axis_index_groups=SAME_CORE, tiled=True
    )
    parts = backward(info, block_cols, held, tiles, grad)
    own, other = parts[:8], parts[8:]
    summed = [own[d].astype(F32) + swap(other[d]).astype(F32) for d in range(SLABS)]
    total = summed[0]
    for d in range(1, SLABS):
        total = total + lax.ppermute(summed[d].astype(BF16), "blk", _to_step(STEPS[d])).astype(F32)
    feats_grad = total.astype(BF16)

    tail = lax.all_to_all(tail.reshape(16, HALF, 768), "feat", 0, 0, tiled=True)
    hidden = jnp.transpose(tail[:, :, :512], (1, 0, 2)).reshape(HALF, LOCAL)
    wgrad = jnp.sum(tail[:, :, 512:].astype(F32), axis=0)
    wgrad = lax.all_to_all(
        jnp.broadcast_to(wgrad[None], (SLABS, HALF, 256)), "blk", 0, 0, tiled=True
    )
    weight_grad = jnp.sum(wgrad, axis=0)
    return hidden, weight_grad, feats_grad


def solution(mesh):
    placed = (
        P("feat", "blk"),
        P("feat", None),
        P("blk", None, None, None),
        P("blk", None),
        P("feat", "blk"),
    )
    return jax.shard_map(
        per_device,
        mesh=mesh,
        in_specs=placed,
        out_specs=(P("feat", "blk"), P("feat", None), P("feat", "blk")),
        check_vma=False,
    )
```

```python
import functools

import jax
import jax.numpy as jnp
from jax import lax
from jax.experimental import pallas as pl
from jax.experimental.pallas import tpu as pltpu
from jax.sharding import PartitionSpec as P

BF16 = jnp.bfloat16
F32 = jnp.float32
ANY = pl.BlockSpec(memory_space=pl.ANY)
VMEM = pl.BlockSpec(memory_space=pltpu.VMEM)
SMEM = pl.BlockSpec(memory_space=pltpu.SMEM)

STEPS = ((0, 0), (0, 1), (0, 3), (1, 0), (0, 2), (1, 1), (1, 3), (1, 2))
UP, DOWN, ACROSS = (0, 1), (0, 3), (1, 0)
PIECES = tuple((d, 0, 8192) for d in range(7)) + ((7, 0, 4096), (7, 4096, 4096))
SLABS = 8
HALF = 16
PAIR = 32
LOCAL = 8192
NODES = 65536
SLOTS = 32
ROWS = 32
HELD = 16
RING = 16


def _index(x, y):
    return x * 4 + y


def _from_step(step):
    dx, dy = step
    return [(_index(x ^ dx, (y + dy) % 4), _index(x, y)) for x in range(2) for y in range(4)]


def _to_step(step):
    return [(b, a) for a, b in _from_step(step)]


CORE_SWAP = [(f, f ^ 1) for f in range(16)]
SAME_CORE = [list(range(0, 16, 2)), list(range(1, 16, 2))]


def swap(a):
    return lax.ppermute(a, "feat", CORE_SWAP)


def receive(a, step):
    return lax.ppermute(a, "blk", _from_step(step))


def send(a, step):
    return lax.ppermute(a, "blk", _to_step(step))


def after(a, *others):
    return lax.optimization_barrier((a, *others))[0]


def row_of(core, local):
    return 8 * (local // 4) + 4 * core + local % 4


def lanes_of(block):
    return pl.ds(pl.multiple_of(block * 128, 128), 128)


def load_kernel(info, tiles, out, token, sems):
    core = info[0]
    copies = []
    for g in range(HELD // 4):
        copies.append(
            pltpu.make_async_copy(
                tiles.at[pl.ds(8 * g + 4 * core, 4)], out.at[pl.ds(4 * g, 4)], sems.at[g]
            )
        )
    for c in copies:
        c.start()
    token[...] = jnp.zeros_like(token)
    for c in copies:
        c.wait()


def load_tiles(info, tiles):
    return pl.pallas_call(
        load_kernel,
        out_shape=(
            pltpu.VMEM((HELD, SLOTS, 128, 128), BF16),
            jax.ShapeDtypeStruct((8, 128), F32),
        ),
        in_specs=[SMEM, ANY],
        out_specs=(VMEM, VMEM),
        scratch_shapes=[pltpu.SemaphoreType.DMA((HELD // 4,))],
        compiler_params=pltpu.CompilerParams(vmem_limit_bytes=2 << 20),
        cost_estimate=pl.CostEstimate(flops=0, bytes_accessed=32 << 20, transcendentals=0),
        name="load_tiles",
    )(info, tiles)


WIDE = 1280


def unpack_kernel(info, message, mine, other, wgrad_mine, wgrad_other):
    core = info[0]
    own = pl.ds(pl.multiple_of(HALF * core, HALF), HALF)
    sibling = pl.ds(pl.multiple_of(HALF * (1 - core), HALF), HALF)
    for rows, nodes, wgrad in ((own, mine, wgrad_mine), (sibling, other, wgrad_other)):
        total = jnp.zeros((HALF, 256), F32)
        for g in range(8):
            nodes[:, 512 * g : 512 * (g + 1)] = message[g, rows, 512:1024]
            total += message[g, rows, 1024:].astype(F32)
        wgrad[...] = total


def unpack(info, message):
    return pl.pallas_call(
        unpack_kernel,
        out_shape=(
            jax.ShapeDtypeStruct((HALF, 4096), BF16),
            jax.ShapeDtypeStruct((HALF, 4096), BF16),
            jax.ShapeDtypeStruct((HALF, 256), F32),
            jax.ShapeDtypeStruct((HALF, 256), F32),
        ),
        in_specs=[SMEM, VMEM],
        out_specs=(VMEM,) * 4,
        compiler_params=pltpu.CompilerParams(vmem_limit_bytes=4 << 20),
        cost_estimate=pl.CostEstimate(flops=0, bytes_accessed=1 << 20, transcendentals=0),
        name="unpack",
    )(info, message)


def join_kernel(info, mine, received, hidden):
    core = info[0]
    for g in range(8):
        chunk = slice(512 * g, 512 * (g + 1))
        a, b = mine[:, chunk], received[:, chunk]
        hidden[:, 1024 * g : 1024 * g + 512] = jnp.where(core == 0, a, b)
        hidden[:, 1024 * g + 512 : 1024 * (g + 1)] = jnp.where(core == 0, b, a)


def join(info, mine, received):
    return pl.pallas_call(
        join_kernel,
        out_shape=jax.ShapeDtypeStruct((HALF, LOCAL), BF16),
        in_specs=[SMEM, VMEM, VMEM],
        out_specs=VMEM,
        compiler_params=pltpu.CompilerParams(vmem_limit_bytes=4 << 20),
        cost_estimate=pl.CostEstimate(flops=0, bytes_accessed=1 << 20, transcendentals=0),
        name="join",
    )(info, mine, received)


def forward_kernel(info, cols, held, tiles, *refs):
    pieces, sides, (out, feats, ring, sems, ring_sems) = refs[:18], refs[18:22], refs[22:]
    core = info[0]
    copies = []
    for i, (d, first, count) in enumerate(PIECES):
        at = pl.multiple_of(info[1 + d] * LOCAL + first, 4096)
        for h in range(2):
            rows = pl.ds(pl.multiple_of(jnp.where(core == h, 0, HALF), HALF), HALF)
            copies.append(
                pltpu.make_async_copy(
                    pieces[2 * i + h], feats.at[rows, pl.ds(at, count)], sems.at[2 * i + h]
                )
            )
    stream = [
        pltpu.make_async_copy(tiles.at[row_of(core, HELD + i)], ring.at[i], ring_sems.at[i])
        for i in range(ROWS - HELD)
    ]
    for c in copies + stream:
        c.start()
    for h in range(2):
        rows = pl.ds(pl.multiple_of(jnp.where(core == h, 0, HALF), HALF), HALF)
        cot, weight = sides[2 * h], sides[2 * h + 1]
        for g in range(8):
            nodes = pl.ds(pl.multiple_of(1024 * g + 512 * core, 512), 512)
            out[g, rows, 512:1024] = cot[:, nodes]
            out[g, rows, 1024:] = weight[...]
    for c in copies:
        c.wait()

    def four_rows(first, source, offset, sums):
        rows = [row_of(core, first + k) for k in range(4)]

        def push(unit, p, register):
            right = [
                jnp.concatenate([source[first - offset + k, p + e] for e in range(2)], axis=1)
                for k in (2 * unit, 2 * unit + 1)
            ]
            pltpu.matmul_push_rhs(
                jnp.concatenate(right, axis=0), register, unit, transpose=True
            )

        def multiply(unit, p, register):
            left = [
                jnp.concatenate([feats[:, lanes_of(cols[p + e, r])] for e in range(2)], axis=1)
                for r in rows[2 * unit : 2 * unit + 2]
            ]
            pltpu.matmul_acc_lhs(
                sums[unit], jnp.concatenate(left, axis=0), load_staged_rhs=register
            )

        for unit in range(2):
            push(unit, 0, 0)
        for p in range(0, SLOTS, 2):
            if p + 2 < SLOTS:
                for unit in range(2):
                    push(unit, p + 2, (p // 2 + 1) % 2)
            for unit in range(2):
                multiply(unit, p, (p // 2) % 2)
        for unit in range(2):
            got = pltpu.matmul_pop(sums[unit])
            for k in range(2):
                value = got[PAIR * k : PAIR * (k + 1), 128 * k : 128 * (k + 1)]
                j = 2 * unit + k
                out[first // 4, :, 128 * j : 128 * (j + 1)] = value.astype(BF16)

    def held_rows(i, carry):
        pl.run_scoped(
            lambda *sums: four_rows(4 * i, held, 0, sums),
            *[pltpu.ACC(unit)((2 * PAIR, 256), F32) for unit in range(2)],
        )
        return carry

    lax.fori_loop(0, HELD // 4, held_rows, 0)
    for c in stream:
        c.wait()

    def streamed_rows(i, carry):
        pl.run_scoped(
            lambda *sums: four_rows(HELD + 4 * i, ring, HELD, sums),
            *[pltpu.ACC(unit)((2 * PAIR, 256), F32) for unit in range(2)],
        )
        return carry

    lax.fori_loop(0, (ROWS - HELD) // 4, streamed_rows, 0)


def forward(info, cols, held, tiles, pieces, sides):
    return pl.pallas_call(
        forward_kernel,
        out_shape=jax.ShapeDtypeStruct((8, PAIR, WIDE), BF16),
        in_specs=[SMEM, SMEM, VMEM, ANY] + [ANY] * 18 + [VMEM] * 4,
        out_specs=VMEM,
        scratch_shapes=[
            pltpu.VMEM((PAIR, NODES), BF16),
            pltpu.VMEM((ROWS - HELD, SLOTS, 128, 128), BF16),
            pltpu.SemaphoreType.DMA((18,)),
            pltpu.SemaphoreType.DMA((ROWS - HELD,)),
        ],
        compiler_params=pltpu.CompilerParams(vmem_limit_bytes=24 << 20),
        cost_estimate=pl.CostEstimate(
            flops=8 * 2 * 1024 * 128 * 128 * 32, bytes_accessed=8 << 20, transcendentals=0
        ),
        name="forward",
    )(info, cols, held, tiles, *pieces, *sides)


def dense_kernel(message, out):
    agg = message[:, :512]
    weight = message[:, 1024:]
    pre = lax.dot_general(weight, agg, (((0,), (0,)), ((), ())), preferred_element_type=F32)
    sig = 1.0 / (1.0 + jnp.exp(-pre))
    out[:, 512:1024] = (pre * sig).astype(BF16)
    cot = message[:, 512:1024].astype(F32)
    pre_grad = (cot * sig * (1.0 + pre * (1.0 - sig))).astype(BF16)
    out[:, :512] = jnp.dot(weight, pre_grad, preferred_element_type=F32).astype(BF16)
    wgrad = lax.dot_general(agg, pre_grad, (((1,), (1,)), ((), ())), preferred_element_type=F32)
    out[:, 1024:] = wgrad.astype(BF16)


def dense(message):
    return pl.pallas_call(
        dense_kernel,
        out_shape=jax.ShapeDtypeStruct((256, WIDE), BF16),
        in_specs=[VMEM],
        out_specs=VMEM,
        compiler_params=pltpu.CompilerParams(vmem_limit_bytes=8 << 20),
        cost_estimate=pl.CostEstimate(
            flops=3 * 2 * 256 * 256 * 512, bytes_accessed=2 << 20, transcendentals=256 * 512
        ),
        name="dense",
    )(message)


def backward_kernel(info, cols, tiles, grad, *refs):
    outs, (total, ring, sems) = refs[:18], refs[18:]
    core = info[0]

    def copy(i):
        slot = lax.rem(i, RING)
        return pltpu.make_async_copy(tiles.at[row_of(core, i)], ring.at[slot], sems.at[slot])

    for i in range(RING):
        copy(jnp.int32(i)).start()

    def clear(i, carry):
        total[:, pl.ds(pl.multiple_of(i * 2048, 2048), 2048)] = jnp.zeros((PAIR, 2048), F32)
        return carry

    lax.fori_loop(0, NODES // 2048, clear, 0)

    def row(local):
        r = row_of(core, local)
        slot = lax.rem(local, RING)
        g = grad[local // 4, :, lanes_of(lax.rem(local, 4))]
        for first in range(0, SLOTS, 8):
            blocks = [lanes_of(cols[first + i, r]) for i in range(8)]
            terms = []
            for i in range(first, first + 8, 2):
                pair = jnp.concatenate([ring[slot, i], ring[slot, i + 1]], axis=1)
                both = jnp.dot(g, pair, preferred_element_type=F32)
                terms += [both[:, :128], both[:, 128:]]
            sums = [total[:, blocks[i]] + terms[i] for i in range(8)]
            for i in range(8):
                total[:, blocks[i]] = sums[i]

    def step(i, carry):
        for k in range(2):
            copy(2 * i + k).wait()
        for k in range(2):
            row(2 * i + k)

        @pl.when(2 * i + RING < ROWS)
        def _():
            for k in range(2):
                copy(2 * i + k + RING).start()

        return carry

    lax.fori_loop(0, ROWS // 2, step, 0)

    own = pl.ds(pl.multiple_of(HALF * core, HALF), HALF)
    other = pl.ds(pl.multiple_of(HALF * (1 - core), HALF), HALF)
    for i, (d, first, count) in enumerate(PIECES):
        lanes = pl.ds(pl.multiple_of(info[1 + d] * LOCAL + first, 4096), count)
        outs[i][...] = total[own, lanes].astype(BF16)
        outs[9 + i][...] = total[other, lanes].astype(BF16)


def backward(info, cols, tiles, grad):
    return pl.pallas_call(
        backward_kernel,
        out_shape=[jax.ShapeDtypeStruct((HALF, n), BF16) for _, _, n in PIECES] * 2,
        in_specs=[SMEM, SMEM, ANY, VMEM],
        out_specs=[VMEM] * 18,
        scratch_shapes=[
            pltpu.VMEM((PAIR, NODES), F32),
            pltpu.VMEM((RING, SLOTS, 128, 128), BF16),
            pltpu.SemaphoreType.DMA((RING,)),
        ],
        compiler_params=pltpu.CompilerParams(vmem_limit_bytes=32 << 20),
        cost_estimate=pl.CostEstimate(
            flops=8 * 2 * 1024 * 128 * 128 * 32, bytes_accessed=8 << 20, transcendentals=0
        ),
        name="backward",
    )(info, cols, tiles, grad)


def per_device(node_feats, weight, tiles, block_cols, cotangent):
    core = lax.axis_index("feat") % 2
    slab = lax.axis_index("blk")
    x, y = slab // 4, slab % 4
    info = jnp.stack([core] + [(x ^ dx) * 4 + (y + dy) % 4 for dx, dy in STEPS]).astype(jnp.int32)
    cols = block_cols.T

    up, down, across = (receive(node_feats, s) for s in (UP, DOWN, ACROSS))
    held, token = load_tiles(info, tiles)
    up2, across2 = after(up, token), after(across, token)
    far = receive(up2, UP)
    across_up = receive(up2, ACROSS)
    across_down = receive(across2, DOWN)
    corner = [receive(across_up[:, :4096], UP), receive(across_down[:, 4096:], DOWN)]
    pieces = []
    for block in (node_feats, up, down, across, far, across_up, across_down, *corner):
        pieces += [block, swap(block)]
    sides = [cotangent, weight, swap(cotangent), swap(weight)]
    held = pltpu.with_memory_space_constraint(held, pltpu.VMEM)

    message = forward(info, cols, held, tiles, pieces, sides)
    message = lax.all_to_all(message, "feat", 0, 0, axis_index_groups=SAME_CORE, tiled=True)
    message = dense(message.reshape(256, WIDE)).reshape(8, PAIR, WIDE)
    message = lax.all_to_all(message, "feat", 0, 0, axis_index_groups=SAME_CORE, tiled=True)
    parts = backward(info, cols, tiles, message)

    def mine(i):
        return parts[i].astype(F32) + swap(parts[9 + i]).astype(F32)

    def widen(a, low, high):
        return lax.pad(a, jnp.zeros((), a.dtype), ((0, 0, 0), (low, high, 0))).astype(F32)

    corner_up = send(mine(7).astype(BF16), UP)
    corner_down = send(mine(8).astype(BF16), DOWN)
    hidden, hidden_other, wgrad, wgrad_other = unpack(info, after(message, parts[0]))
    hidden = join(info, hidden, swap(hidden_other))
    wgrad = wgrad + swap(wgrad_other)
    wgrad = wgrad + receive(wgrad, ACROSS)
    across_up = (mine(5) + widen(corner_up, 0, 4096)).astype(BF16)
    across_down = (mine(6) + widen(corner_down, 4096, 0)).astype(BF16)
    across_up, across_down, wgrad, hidden = lax.optimization_barrier(
        (across_up, across_down, wgrad, hidden)
    )
    from_across = send(across_up, ACROSS)
    from_up = send(across_down, DOWN)
    from_down = send(mine(4).astype(BF16), UP)
    wgrad = wgrad + lax.ppermute(wgrad, "blk", [(b, b ^ 1) for b in range(8)])
    up = (mine(1) + from_across.astype(F32) + from_down.astype(F32)).astype(BF16)
    across = (mine(3) + from_up.astype(F32)).astype(BF16)
    up, across, down, wgrad = lax.optimization_barrier((up, across, mine(2).astype(BF16), wgrad))
    weight_grad = wgrad + lax.ppermute(wgrad, "blk", [(b, b ^ 2) for b in range(8)])
    last = [send(up, UP), send(down, DOWN), send(across, ACROSS)]
    total = mine(0)
    for a in last:
        total = total + a.astype(F32)
    return hidden, weight_grad, total.astype(BF16)


def solution(mesh):
    placed = (
        P("feat", "blk"),
        P("feat", None),
        P("blk", None, None, None),
        P("blk", None),
        P("feat", "blk"),
    )
    return jax.shard_map(
        per_device,
        mesh=mesh,
        in_specs=placed,
        out_specs=(P("feat", "blk"), P("feat", None), P("feat", "blk")),
        check_vma=False,
    )
```

```python
import functools

import jax
import jax.numpy as jnp
from jax import lax
from jax.experimental import pallas as pl
from jax.experimental.pallas import tpu as pltpu
from jax.sharding import PartitionSpec as P

BF16 = jnp.bfloat16
F32 = jnp.float32
ANY = pl.BlockSpec(memory_space=pl.ANY)
VMEM = pl.BlockSpec(memory_space=pltpu.VMEM)
SMEM = pl.BlockSpec(memory_space=pltpu.SMEM)

STEPS = ((0, 0), (0, 1), (0, 3), (1, 0), (0, 2), (1, 1), (1, 3), (1, 2))
UP, DOWN, ACROSS = (0, 1), (0, 3), (1, 0)
GROUPS = ((7,), (5, 6, 4), (1, 3, 2, 0))
PIECES = tuple((d, 0, 8192) for d in range(7)) + ((7, 0, 4096), (7, 4096, 4096))
SLABS = 8
HALF = 16
PAIR = 32
LOCAL = 8192
NODES = 65536
SLOTS = 32
ROWS = 32
HELD = 16
RING = 16


def _index(x, y):
    return x * 4 + y


def _from_step(step):
    dx, dy = step
    return [(_index(x ^ dx, (y + dy) % 4), _index(x, y)) for x in range(2) for y in range(4)]


def _to_step(step):
    return [(b, a) for a, b in _from_step(step)]


CORE_SWAP = [(f, f ^ 1) for f in range(16)]
SAME_CORE = [list(range(0, 16, 2)), list(range(1, 16, 2))]


def swap(a):
    return lax.ppermute(a, "feat", CORE_SWAP)


def receive(a, step):
    return lax.ppermute(a, "blk", _from_step(step))


def send(a, step):
    return lax.ppermute(a, "blk", _to_step(step))


def after(a, *others):
    return lax.optimization_barrier((a, *others))[0]


def row_of(core, local):
    return 8 * (local // 4) + 4 * core + local % 4


def lanes_of(block):
    return pl.ds(pl.multiple_of(block * 128, 128), 128)


def load_kernel(first, info, tiles, out, token, sems):
    core = info[0]
    copies = []
    for g in range(HELD // 4):
        copies.append(
            pltpu.make_async_copy(
                tiles.at[pl.ds(8 * (first + g) + 4 * core, 4)],
                out.at[pl.ds(4 * g, 4)],
                sems.at[g],
            )
        )
    for c in copies:
        c.start()
    token[...] = jnp.zeros_like(token)
    for c in copies:
        c.wait()


def load_tiles(info, tiles, first):
    held, token = pl.pallas_call(
        functools.partial(load_kernel, first),
        out_shape=(
            pltpu.VMEM((HELD, SLOTS, 128, 128), BF16),
            jax.ShapeDtypeStruct((8, 128), F32),
        ),
        in_specs=[SMEM, ANY],
        out_specs=(VMEM, VMEM),
        scratch_shapes=[pltpu.SemaphoreType.DMA((HELD // 4,))],
        compiler_params=pltpu.CompilerParams(vmem_limit_bytes=2 << 20),
        cost_estimate=pl.CostEstimate(flops=0, bytes_accessed=32 << 20, transcendentals=0),
        name="load_tiles",
    )(info, tiles)
    return pltpu.with_memory_space_constraint(held, pltpu.VMEM), token


WIDE = 1280


def unpack_kernel(info, message, mine, other, wgrad_mine, wgrad_other):
    core = info[0]
    own = pl.ds(pl.multiple_of(HALF * core, HALF), HALF)
    sibling = pl.ds(pl.multiple_of(HALF * (1 - core), HALF), HALF)
    for rows, nodes, wgrad in ((own, mine, wgrad_mine), (sibling, other, wgrad_other)):
        total = jnp.zeros((HALF, 256), F32)
        for g in range(8):
            nodes[:, 512 * g : 512 * (g + 1)] = message[g, rows, 512:1024]
            total += message[g, rows, 1024:].astype(F32)
        wgrad[...] = total


def unpack(info, message):
    return pl.pallas_call(
        unpack_kernel,
        out_shape=(
            jax.ShapeDtypeStruct((HALF, 4096), BF16),
            jax.ShapeDtypeStruct((HALF, 4096), BF16),
            jax.ShapeDtypeStruct((HALF, 256), F32),
            jax.ShapeDtypeStruct((HALF, 256), F32),
        ),
        in_specs=[SMEM, VMEM],
        out_specs=(VMEM,) * 4,
        compiler_params=pltpu.CompilerParams(vmem_limit_bytes=4 << 20),
        cost_estimate=pl.CostEstimate(flops=0, bytes_accessed=1 << 20, transcendentals=0),
        name="unpack",
    )(info, message)


def join_kernel(info, mine, received, hidden):
    core = info[0]
    for g in range(8):
        chunk = slice(512 * g, 512 * (g + 1))
        a, b = mine[:, chunk], received[:, chunk]
        hidden[:, 1024 * g : 1024 * g + 512] = jnp.where(core == 0, a, b)
        hidden[:, 1024 * g + 512 : 1024 * (g + 1)] = jnp.where(core == 0, b, a)


def join(info, mine, received):
    return pl.pallas_call(
        join_kernel,
        out_shape=jax.ShapeDtypeStruct((HALF, LOCAL), BF16),
        in_specs=[SMEM, VMEM, VMEM],
        out_specs=VMEM,
        compiler_params=pltpu.CompilerParams(vmem_limit_bytes=4 << 20),
        cost_estimate=pl.CostEstimate(flops=0, bytes_accessed=1 << 20, transcendentals=0),
        name="join",
    )(info, mine, received)


def forward_kernel(info, cols, low_tiles, high_tiles, *refs):
    pieces, sides, (out, feats, sems) = refs[:18], refs[18:22], refs[22:]
    core = info[0]
    copies = []
    for i, (d, first, count) in enumerate(PIECES):
        at = pl.multiple_of(info[1 + d] * LOCAL + first, 4096)
        for h in range(2):
            rows = pl.ds(pl.multiple_of(jnp.where(core == h, 0, HALF), HALF), HALF)
            copies.append(
                pltpu.make_async_copy(
                    pieces[2 * i + h], feats.at[rows, pl.ds(at, count)], sems.at[2 * i + h]
                )
            )
    for c in copies:
        c.start()
    for h in range(2):
        rows = pl.ds(pl.multiple_of(jnp.where(core == h, 0, HALF), HALF), HALF)
        cot, weight = sides[2 * h], sides[2 * h + 1]
        for g in range(8):
            nodes = pl.ds(pl.multiple_of(1024 * g + 512 * core, 512), 512)
            out[g, rows, 512:1024] = cot[:, nodes]
            out[g, rows, 1024:] = weight[...]
    for c in copies:
        c.wait()

    def four_rows(first, source, offset, sums):
        rows = [row_of(core, first + k) for k in range(4)]

        def push(unit, p, register):
            right = [
                jnp.concatenate([source[first - offset + k, p + e] for e in range(2)], axis=1)
                for k in (2 * unit, 2 * unit + 1)
            ]
            pltpu.matmul_push_rhs(
                jnp.concatenate(right, axis=0), register, unit, transpose=True
            )

        def multiply(unit, p, register):
            left = [
                jnp.concatenate([feats[:, lanes_of(cols[p + e, r])] for e in range(2)], axis=1)
                for r in rows[2 * unit : 2 * unit + 2]
            ]
            pltpu.matmul_acc_lhs(
                sums[unit], jnp.concatenate(left, axis=0), load_staged_rhs=register
            )

        for unit in range(2):
            push(unit, 0, 0)
        for p in range(0, SLOTS, 2):
            if p + 2 < SLOTS:
                for unit in range(2):
                    push(unit, p + 2, (p // 2 + 1) % 2)
            for unit in range(2):
                multiply(unit, p, (p // 2) % 2)
        for unit in range(2):
            got = pltpu.matmul_pop(sums[unit])
            for k in range(2):
                value = got[PAIR * k : PAIR * (k + 1), 128 * k : 128 * (k + 1)]
                j = 2 * unit + k
                out[first // 4, :, 128 * j : 128 * (j + 1)] = value.astype(BF16)

    for source, offset in ((low_tiles, 0), (high_tiles, HELD)):

        def step(i, carry, source=source, offset=offset):
            pl.run_scoped(
                lambda *sums: four_rows(offset + 4 * i, source, offset, sums),
                *[pltpu.ACC(unit)((2 * PAIR, 256), F32) for unit in range(2)],
            )
            return carry

        lax.fori_loop(0, HELD // 4, step, 0)


def forward(info, cols, held, pieces, sides):
    return pl.pallas_call(
        forward_kernel,
        out_shape=jax.ShapeDtypeStruct((8, PAIR, WIDE), BF16),
        in_specs=[SMEM, SMEM, VMEM, VMEM] + [ANY] * 18 + [VMEM] * 4,
        out_specs=VMEM,
        scratch_shapes=[
            pltpu.VMEM((PAIR, NODES), BF16),
            pltpu.SemaphoreType.DMA((18,)),
        ],
        compiler_params=pltpu.CompilerParams(vmem_limit_bytes=8 << 20),
        cost_estimate=pl.CostEstimate(
            flops=8 * 2 * 1024 * 128 * 128 * 32, bytes_accessed=8 << 20, transcendentals=0
        ),
        name="forward",
    )(info, cols, *held, *pieces, *sides)


def dense_kernel(message, out):
    agg = message[:, :512]
    weight = message[:, 1024:]
    pre = lax.dot_general(weight, agg, (((0,), (0,)), ((), ())), preferred_element_type=F32)
    sig = 1.0 / (1.0 + jnp.exp(-pre))
    out[:, 512:1024] = (pre * sig).astype(BF16)
    cot = message[:, 512:1024].astype(F32)
    pre_grad = (cot * sig * (1.0 + pre * (1.0 - sig))).astype(BF16)
    out[:, :512] = jnp.dot(weight, pre_grad, preferred_element_type=F32).astype(BF16)
    wgrad = lax.dot_general(agg, pre_grad, (((1,), (1,)), ((), ())), preferred_element_type=F32)
    out[:, 1024:] = wgrad.astype(BF16)


def dense(message):
    return pl.pallas_call(
        dense_kernel,
        out_shape=jax.ShapeDtypeStruct((256, WIDE), BF16),
        in_specs=[VMEM],
        out_specs=VMEM,
        compiler_params=pltpu.CompilerParams(vmem_limit_bytes=8 << 20),
        cost_estimate=pl.CostEstimate(
            flops=3 * 2 * 256 * 256 * 512, bytes_accessed=2 << 20, transcendentals=256 * 512
        ),
        name="dense",
    )(message)


def backward_kernel(info, cols, tiles, grad, *refs):
    outs, (total, ring, sems) = refs[:6], refs[6:]
    core = info[0]

    def copy(i):
        slot = lax.rem(i, RING)
        return pltpu.make_async_copy(tiles.at[row_of(core, i)], ring.at[slot], sems.at[slot])

    for i in range(RING):
        copy(jnp.int32(i)).start()

    def clear(i, carry):
        total[:, pl.ds(pl.multiple_of(i * 2048, 2048), 2048)] = jnp.zeros((PAIR, 2048), F32)
        return carry

    lax.fori_loop(0, NODES // 2048, clear, 0)

    def row(local):
        r = row_of(core, local)
        slot = lax.rem(local, RING)
        g = grad[local // 4, :, lanes_of(lax.rem(local, 4))]
        for first in range(0, SLOTS, 8):
            blocks = [lanes_of(cols[first + i, r]) for i in range(8)]
            terms = []
            for i in range(first, first + 8, 2):
                pair = jnp.concatenate([ring[slot, i], ring[slot, i + 1]], axis=1)
                both = jnp.dot(g, pair, preferred_element_type=F32)
                terms += [both[:, :128], both[:, 128:]]
            sums = [total[:, blocks[i]] + terms[i] for i in range(8)]
            for i in range(8):
                total[:, blocks[i]] = sums[i]

    def step(i, carry):
        for k in range(2):
            copy(2 * i + k).wait()
        for k in range(2):
            row(2 * i + k)

        @pl.when(2 * i + RING < ROWS)
        def _():
            for k in range(2):
                copy(2 * i + k + RING).start()

        return carry

    lax.fori_loop(0, ROWS // 2, step, 0)

    own = pl.ds(pl.multiple_of(HALF * core, HALF), HALF)
    other = pl.ds(pl.multiple_of(HALF * (1 - core), HALF), HALF)
    for phase, group in enumerate(GROUPS):
        for i, d in enumerate(group):
            lanes = pl.ds(pl.multiple_of(info[1 + d] * LOCAL, LOCAL), LOCAL)
            place = slice(LOCAL * i, LOCAL * (i + 1))
            outs[phase][:, place] = total[own, lanes].astype(BF16)
            outs[3 + phase][:, place] = total[other, lanes].astype(BF16)


def backward(info, cols, tiles, grad):
    return pl.pallas_call(
        backward_kernel,
        out_shape=[jax.ShapeDtypeStruct((HALF, LOCAL * len(g)), BF16) for g in GROUPS] * 2,
        in_specs=[SMEM, SMEM, ANY, VMEM],
        out_specs=[VMEM] * 6,
        scratch_shapes=[
            pltpu.VMEM((PAIR, NODES), F32),
            pltpu.VMEM((RING, SLOTS, 128, 128), BF16),
            pltpu.SemaphoreType.DMA((RING,)),
        ],
        compiler_params=pltpu.CompilerParams(vmem_limit_bytes=32 << 20),
        cost_estimate=pl.CostEstimate(
            flops=8 * 2 * 1024 * 128 * 128 * 32, bytes_accessed=8 << 20, transcendentals=0
        ),
        name="backward",
    )(info, cols, tiles, grad)


def cut_kernel(across_up, across_down, far, token, up_half, down_half):
    up_half[...] = across_up[:, :4096]
    down_half[...] = across_down[:, 4096:]


def cut(across_up, across_down, far, token):
    return pl.pallas_call(
        cut_kernel,
        out_shape=[jax.ShapeDtypeStruct((HALF, 4096), BF16)] * 2,
        in_specs=[VMEM, VMEM, ANY, ANY],
        out_specs=[VMEM] * 2,
        compiler_params=pltpu.CompilerParams(vmem_limit_bytes=4 << 20),
        cost_estimate=pl.CostEstimate(flops=0, bytes_accessed=1 << 19, transcendentals=0),
        name="cut",
    )(across_up, across_down, far, token)


def sum_call(kernel, shapes, args, name):
    return pl.pallas_call(
        kernel,
        out_shape=[jax.ShapeDtypeStruct(s, t) for s, t in shapes],
        in_specs=[VMEM] * len(args),
        out_specs=[VMEM] * len(shapes),
        compiler_params=pltpu.CompilerParams(vmem_limit_bytes=8 << 20),
        cost_estimate=pl.CostEstimate(flops=0, bytes_accessed=2 << 20, transcendentals=0),
        name=name,
    )(*args)


def corner_kernel(own, other, low, high):
    total = own[...].astype(F32) + other[...].astype(F32)
    low[...] = total[:, :4096].astype(BF16)
    high[...] = total[:, 4096:].astype(BF16)


def middle_kernel(own, other, low, high, across_up, across_down, far):
    def mine(i, first, count):
        lanes = slice(LOCAL * i + first, LOCAL * i + first + count)
        return own[:, lanes].astype(F32) + other[:, lanes].astype(F32)

    across_up[:, :4096] = (mine(0, 0, 4096) + low[...].astype(F32)).astype(BF16)
    across_up[:, 4096:] = mine(0, 4096, 4096).astype(BF16)
    across_down[:, :4096] = mine(1, 0, 4096).astype(BF16)
    across_down[:, 4096:] = (mine(1, 4096, 4096) + high[...].astype(F32)).astype(BF16)
    far[...] = mine(2, 0, LOCAL).astype(BF16)


def near_kernel(own, other, from_across, from_up, from_down, up, across, down, base):
    def mine(i):
        lanes = slice(LOCAL * i, LOCAL * (i + 1))
        return own[:, lanes].astype(F32) + other[:, lanes].astype(F32)

    up[...] = (mine(0) + from_across[...].astype(F32) + from_down[...].astype(F32)).astype(BF16)
    across[...] = (mine(1) + from_up[...].astype(F32)).astype(BF16)
    down[...] = mine(2).astype(BF16)
    base[...] = mine(3)


def last_kernel(base, a, b, c, out):
    total = base[...] + a[...].astype(F32) + b[...].astype(F32) + c[...].astype(F32)
    out[...] = total.astype(BF16)


def per_device(node_feats, weight, tiles, block_cols, cotangent):
    core = lax.axis_index("feat") % 2
    slab = lax.axis_index("blk")
    x, y = slab // 4, slab % 4
    info = jnp.stack([core] + [(x ^ dx) * 4 + (y + dy) % 4 for dx, dy in STEPS]).astype(jnp.int32)
    cols = block_cols.T

    up, down, across = (receive(node_feats, s) for s in (UP, DOWN, ACROSS))
    low_tiles, token = load_tiles(info, tiles, 0)
    feats_swapped, cot_swapped = swap(node_feats), swap(cotangent)
    up2, across2 = after(up, token, feats_swapped, cot_swapped), after(across, token, down)
    far = receive(up2, UP)
    across_up = receive(up2, ACROSS)
    across_down = receive(across2, DOWN)
    high_tiles, token = load_tiles(info, after(tiles, up2, across2), HELD // 4)
    weight_swapped = swap(after(weight, up2))
    up_half, down_half = cut(across_up, across_down, far, token)
    corner = [receive(up_half, UP), receive(down_half, DOWN)]
    pieces = [node_feats, feats_swapped]
    for block in (up, down, across, far, across_up, across_down):
        pieces += [block, swap(after(block, up_half, down_half))]
    for block in corner:
        pieces += [block, swap(block)]
    sides = [cotangent, weight, cot_swapped, weight_swapped]

    message = forward(info, cols, (low_tiles, high_tiles), pieces, sides)
    message = lax.all_to_all(message, "feat", 0, 0, axis_index_groups=SAME_CORE, tiled=True)
    message = dense(message.reshape(256, WIDE)).reshape(8, PAIR, WIDE)
    message = lax.all_to_all(message, "feat", 0, 0, axis_index_groups=SAME_CORE, tiled=True)

    own_a, own_b, own_c, other_a, other_b, other_c = backward(info, cols, tiles, message)
    half, whole = ((HALF, 4096), BF16), ((HALF, LOCAL), BF16)
    low, high = sum_call(corner_kernel, [half] * 2, (own_a, swap(other_a)), "sum_corner")
    corner_up, corner_down = send(low, UP), send(high, DOWN)
    hidden, hidden_other, wgrad, wgrad_other = unpack(info, after(message, low, high))
    across_up, across_down, far = sum_call(
        middle_kernel, [whole] * 3, (own_b, swap(other_b), corner_up, corner_down), "sum_middle"
    )
    from_across = send(across_up, ACROSS)
    from_up = send(across_down, DOWN)
    from_down = send(far, UP)
    hidden_other, wgrad_other = after(hidden_other, far), after(wgrad_other, far)
    hidden = join(info, hidden, swap(hidden_other))
    wgrad = wgrad + swap(wgrad_other)
    wgrad = wgrad + receive(wgrad, ACROSS)
    wgrad = wgrad + lax.ppermute(wgrad, "blk", [(b, b ^ 1) for b in range(8)])
    from_across, wgrad, hidden = lax.optimization_barrier((from_across, wgrad, hidden))
    up, across, down, base = sum_call(
        near_kernel,
        [whole] * 3 + [((HALF, LOCAL), F32)],
        (own_c, swap(other_c), from_across, from_up, from_down),
        "sum_near",
    )
    last = [send(up, UP), send(across, ACROSS), send(down, DOWN)]
    wgrad = after(wgrad, down)
    weight_grad = wgrad + lax.ppermute(wgrad, "blk", [(b, b ^ 2) for b in range(8)])
    (feats_grad,) = sum_call(last_kernel, [whole], (base, *last), "sum_last")
    return hidden, weight_grad, feats_grad


def solution(mesh):
    placed = (
        P("feat", "blk"),
        P("feat", None),
        P("blk", None, None, None),
        P("blk", None),
        P("feat", "blk"),
    )
    return jax.shard_map(
        per_device,
        mesh=mesh,
        in_specs=placed,
        out_specs=(P("feat", "blk"), P("feat", None), P("feat", "blk")),
        check_vma=False,
    )
```

```python
import functools

import jax
import jax.numpy as jnp
from jax import lax
from jax.experimental import pallas as pl
from jax.experimental.pallas import tpu as pltpu
from jax.sharding import PartitionSpec as P

BF16 = jnp.bfloat16
F32 = jnp.float32
ANY = pl.BlockSpec(memory_space=pl.ANY)
VMEM = pl.BlockSpec(memory_space=pltpu.VMEM)
SMEM = pl.BlockSpec(memory_space=pltpu.SMEM)

STEPS = ((0, 0), (0, 1), (0, 3), (1, 0), (0, 2), (1, 1), (1, 3), (1, 2))
UP, DOWN, ACROSS = (0, 1), (0, 3), (1, 0)
GROUPS = ((7,), (5, 6, 4), (1, 3, 2, 0))
PIECES = tuple((d, 0, 8192) for d in range(7)) + ((7, 0, 4096), (7, 4096, 4096))
SLABS = 8
HALF = 16
PAIR = 32
LOCAL = 8192
NODES = 65536
SLOTS = 32
ROWS = 32
HELD = 16
RING = 16


def _index(x, y):
    return x * 4 + y


def _from_step(step):
    dx, dy = step
    return [(_index(x ^ dx, (y + dy) % 4), _index(x, y)) for x in range(2) for y in range(4)]


def _to_step(step):
    return [(b, a) for a, b in _from_step(step)]


CORE_SWAP = [(f, f ^ 1) for f in range(16)]
SAME_CORE = [list(range(0, 16, 2)), list(range(1, 16, 2))]


def swap(a):
    return lax.ppermute(a, "feat", CORE_SWAP)


def receive(a, step):
    return lax.ppermute(a, "blk", _from_step(step))


def send(a, step):
    return lax.ppermute(a, "blk", _to_step(step))


def after(a, *others):
    return lax.optimization_barrier((a, *others))[0]


def row_of(core, local):
    return 8 * (local // 4) + 4 * core + local % 4


def lanes_of(block):
    return pl.ds(pl.multiple_of(block * 128, 128), 128)


def load_kernel(first, info, tiles, out, token, sems):
    core = info[0]
    copies = []
    for g in range(HELD // 4):
        copies.append(
            pltpu.make_async_copy(
                tiles.at[pl.ds(8 * (first + g) + 4 * core, 4)],
                out.at[pl.ds(4 * g, 4)],
                sems.at[g],
            )
        )
    for c in copies:
        c.start()
    token[...] = jnp.zeros_like(token)
    for c in copies:
        c.wait()


def load_tiles(info, tiles, first):
    held, token = pl.pallas_call(
        functools.partial(load_kernel, first),
        out_shape=(
            pltpu.VMEM((HELD, SLOTS, 128, 128), BF16),
            jax.ShapeDtypeStruct((8, 128), F32),
        ),
        in_specs=[SMEM, ANY],
        out_specs=(VMEM, VMEM),
        scratch_shapes=[pltpu.SemaphoreType.DMA((HELD // 4,))],
        compiler_params=pltpu.CompilerParams(vmem_limit_bytes=2 << 20),
        cost_estimate=pl.CostEstimate(flops=0, bytes_accessed=32 << 20, transcendentals=0),
        name="load_tiles",
    )(info, tiles)
    return pltpu.with_memory_space_constraint(held, pltpu.VMEM), token


WIDE = 1280


def unpack_kernel(info, message, mine, other, wgrad_mine, wgrad_other):
    core = info[0]
    own = pl.ds(pl.multiple_of(HALF * core, HALF), HALF)
    sibling = pl.ds(pl.multiple_of(HALF * (1 - core), HALF), HALF)
    for rows, nodes, wgrad in ((own, mine, wgrad_mine), (sibling, other, wgrad_other)):
        total = jnp.zeros((HALF, 256), F32)
        for g in range(8):
            nodes[:, 512 * g : 512 * (g + 1)] = message[g, rows, 512:1024]
            total += message[g, rows, 1024:].astype(F32)
        wgrad[...] = total


def unpack(info, message):
    return pl.pallas_call(
        unpack_kernel,
        out_shape=(
            jax.ShapeDtypeStruct((HALF, 4096), BF16),
            jax.ShapeDtypeStruct((HALF, 4096), BF16),
            jax.ShapeDtypeStruct((HALF, 256), F32),
            jax.ShapeDtypeStruct((HALF, 256), F32),
        ),
        in_specs=[SMEM, VMEM],
        out_specs=(VMEM,) * 4,
        compiler_params=pltpu.CompilerParams(vmem_limit_bytes=4 << 20),
        cost_estimate=pl.CostEstimate(flops=0, bytes_accessed=1 << 20, transcendentals=0),
        name="unpack",
    )(info, message)


def join_kernel(info, mine, received, hidden):
    core = info[0]
    for g in range(8):
        chunk = slice(512 * g, 512 * (g + 1))
        a, b = mine[:, chunk], received[:, chunk]
        hidden[:, 1024 * g : 1024 * g + 512] = jnp.where(core == 0, a, b)
        hidden[:, 1024 * g + 512 : 1024 * (g + 1)] = jnp.where(core == 0, b, a)


def join(info, mine, received):
    return pl.pallas_call(
        join_kernel,
        out_shape=jax.ShapeDtypeStruct((HALF, LOCAL), BF16),
        in_specs=[SMEM, VMEM, VMEM],
        out_specs=VMEM,
        compiler_params=pltpu.CompilerParams(vmem_limit_bytes=4 << 20),
        cost_estimate=pl.CostEstimate(flops=0, bytes_accessed=1 << 20, transcendentals=0),
        name="join",
    )(info, mine, received)


def forward_kernel(info, cols, low_tiles, high_tiles, *refs):
    pieces, sides, (out, feats, sems) = refs[:18], refs[18:22], refs[22:]
    core = info[0]
    copies = []
    for i, (d, first, count) in enumerate(PIECES):
        at = pl.multiple_of(info[1 + d] * LOCAL + first, 4096)
        for h in range(2):
            rows = pl.ds(pl.multiple_of(jnp.where(core == h, 0, HALF), HALF), HALF)
            copies.append(
                pltpu.make_async_copy(
                    pieces[2 * i + h], feats.at[rows, pl.ds(at, count)], sems.at[2 * i + h]
                )
            )
    for c in copies:
        c.start()
    for h in range(2):
        rows = pl.ds(pl.multiple_of(jnp.where(core == h, 0, HALF), HALF), HALF)
        cot, weight = sides[2 * h], sides[2 * h + 1]
        for g in range(8):
            nodes = pl.ds(pl.multiple_of(1024 * g + 512 * core, 512), 512)
            out[g, rows, 512:1024] = cot[:, nodes]
            out[g, rows, 1024:] = weight[...]
    for c in copies:
        c.wait()

    def four_rows(first, source, offset, sums):
        rows = [row_of(core, first + k) for k in range(4)]

        def push(unit, p, register):
            right = [
                jnp.concatenate([source[first - offset + k, p + e] for e in range(2)], axis=1)
                for k in (2 * unit, 2 * unit + 1)
            ]
            pltpu.matmul_push_rhs(
                jnp.concatenate(right, axis=0), register, unit, transpose=True
            )

        def multiply(unit, p, register):
            left = [
                jnp.concatenate([feats[:, lanes_of(cols[p + e, r])] for e in range(2)], axis=1)
                for r in rows[2 * unit : 2 * unit + 2]
            ]
            pltpu.matmul_acc_lhs(
                sums[unit], jnp.concatenate(left, axis=0), load_staged_rhs=register
            )

        for unit in range(2):
            push(unit, 0, 0)
        for p in range(0, SLOTS, 2):
            if p + 2 < SLOTS:
                for unit in range(2):
                    push(unit, p + 2, (p // 2 + 1) % 2)
            for unit in range(2):
                multiply(unit, p, (p // 2) % 2)
        for unit in range(2):
            got = pltpu.matmul_pop(sums[unit])
            for k in range(2):
                value = got[PAIR * k : PAIR * (k + 1), 128 * k : 128 * (k + 1)]
                j = 2 * unit + k
                out[first // 4, :, 128 * j : 128 * (j + 1)] = value.astype(BF16)

    for source, offset in ((low_tiles, 0), (high_tiles, HELD)):

        def step(i, carry, source=source, offset=offset):
            pl.run_scoped(
                lambda *sums: four_rows(offset + 4 * i, source, offset, sums),
                *[pltpu.ACC(unit)((2 * PAIR, 256), F32) for unit in range(2)],
            )
            return carry

        lax.fori_loop(0, HELD // 4, step, 0)


def forward(info, cols, held, pieces, sides):
    return pl.pallas_call(
        forward_kernel,
        out_shape=jax.ShapeDtypeStruct((8, PAIR, WIDE), BF16),
        in_specs=[SMEM, SMEM, VMEM, VMEM] + [ANY] * 18 + [VMEM] * 4,
        out_specs=VMEM,
        scratch_shapes=[
            pltpu.VMEM((PAIR, NODES), BF16),
            pltpu.SemaphoreType.DMA((18,)),
        ],
        compiler_params=pltpu.CompilerParams(vmem_limit_bytes=8 << 20),
        cost_estimate=pl.CostEstimate(
            flops=8 * 2 * 1024 * 128 * 128 * 32, bytes_accessed=8 << 20, transcendentals=0
        ),
        name="forward",
    )(info, cols, *held, *pieces, *sides)


def dense_kernel(message, out):
    agg = message[:, :512]
    weight = message[:, 1024:]
    pre = lax.dot_general(weight, agg, (((0,), (0,)), ((), ())), preferred_element_type=F32)
    sig = 1.0 / (1.0 + jnp.exp(-pre))
    out[:, 512:1024] = (pre * sig).astype(BF16)
    cot = message[:, 512:1024].astype(F32)
    pre_grad = (cot * sig * (1.0 + pre * (1.0 - sig))).astype(BF16)
    out[:, :512] = jnp.dot(weight, pre_grad, preferred_element_type=F32).astype(BF16)
    wgrad = lax.dot_general(agg, pre_grad, (((1,), (1,)), ((), ())), preferred_element_type=F32)
    out[:, 1024:] = wgrad.astype(BF16)


def dense(message):
    return pl.pallas_call(
        dense_kernel,
        out_shape=jax.ShapeDtypeStruct((256, WIDE), BF16),
        in_specs=[VMEM],
        out_specs=VMEM,
        compiler_params=pltpu.CompilerParams(vmem_limit_bytes=8 << 20),
        cost_estimate=pl.CostEstimate(
            flops=3 * 2 * 256 * 256 * 512, bytes_accessed=2 << 20, transcendentals=256 * 512
        ),
        name="dense",
    )(message)


def backward_kernel(info, cols, tiles, grad, *refs):
    outs, (total, ring, sems) = refs[:6], refs[6:]
    core = info[0]

    def copy(i):
        slot = lax.rem(i, RING)
        return pltpu.make_async_copy(tiles.at[row_of(core, i)], ring.at[slot], sems.at[slot])

    for i in range(RING):
        copy(jnp.int32(i)).start()

    def clear(i, carry):
        total[:, pl.ds(pl.multiple_of(i * 2048, 2048), 2048)] = jnp.zeros((PAIR, 2048), F32)
        return carry

    lax.fori_loop(0, NODES // 2048, clear, 0)

    def row(local):
        r = row_of(core, local)
        slot = lax.rem(local, RING)
        g = grad[local // 4, :, lanes_of(lax.rem(local, 4))]
        for first in range(0, SLOTS, 8):
            blocks = [lanes_of(cols[first + i, r]) for i in range(8)]
            terms = []
            for i in range(first, first + 8, 2):
                pair = jnp.concatenate([ring[slot, i], ring[slot, i + 1]], axis=1)
                both = jnp.dot(g, pair, preferred_element_type=F32)
                terms += [both[:, :128], both[:, 128:]]
            sums = [total[:, blocks[i]] + terms[i] for i in range(8)]
            for i in range(8):
                total[:, blocks[i]] = sums[i]

    def step(i, carry):
        for k in range(2):
            copy(2 * i + k).wait()
        for k in range(2):
            row(2 * i + k)

        @pl.when(2 * i + RING < ROWS)
        def _():
            for k in range(2):
                copy(2 * i + k + RING).start()

        return carry

    lax.fori_loop(0, ROWS // 2, step, 0)

    own = pl.ds(pl.multiple_of(HALF * core, HALF), HALF)
    other = pl.ds(pl.multiple_of(HALF * (1 - core), HALF), HALF)
    for phase, group in enumerate(GROUPS):
        for i, d in enumerate(group):
            lanes = pl.ds(pl.multiple_of(info[1 + d] * LOCAL, LOCAL), LOCAL)
            place = slice(LOCAL * i, LOCAL * (i + 1))
            outs[phase][:, place] = total[own, lanes].astype(BF16)
            outs[3 + phase][:, place] = total[other, lanes].astype(BF16)


def backward(info, cols, tiles, grad):
    return pl.pallas_call(
        backward_kernel,
        out_shape=[jax.ShapeDtypeStruct((HALF, LOCAL * len(g)), BF16) for g in GROUPS] * 2,
        in_specs=[SMEM, SMEM, ANY, VMEM],
        out_specs=[VMEM] * 6,
        scratch_shapes=[
            pltpu.VMEM((PAIR, NODES), F32),
            pltpu.VMEM((RING, SLOTS, 128, 128), BF16),
            pltpu.SemaphoreType.DMA((RING,)),
        ],
        compiler_params=pltpu.CompilerParams(vmem_limit_bytes=32 << 20),
        cost_estimate=pl.CostEstimate(
            flops=8 * 2 * 1024 * 128 * 128 * 32, bytes_accessed=8 << 20, transcendentals=0
        ),
        name="backward",
    )(info, cols, tiles, grad)


def cut_kernel(across_up, across_down, far, token, up_half, down_half):
    up_half[...] = across_up[:, :4096]
    down_half[...] = across_down[:, 4096:]


def cut(across_up, across_down, far, token):
    return pl.pallas_call(
        cut_kernel,
        out_shape=[jax.ShapeDtypeStruct((HALF, 4096), BF16)] * 2,
        in_specs=[VMEM, VMEM, ANY, ANY],
        out_specs=[VMEM] * 2,
        compiler_params=pltpu.CompilerParams(vmem_limit_bytes=4 << 20),
        cost_estimate=pl.CostEstimate(flops=0, bytes_accessed=1 << 19, transcendentals=0),
        name="cut",
    )(across_up, across_down, far, token)


def sum_call(kernel, shapes, args, name, before=()):
    def body(*refs):
        kernel(*refs[: len(args)], *refs[len(args) + len(before) :])

    return pl.pallas_call(
        body,
        out_shape=[jax.ShapeDtypeStruct(s, t) for s, t in shapes],
        in_specs=[VMEM] * len(args) + [ANY] * len(before),
        out_specs=[VMEM] * len(shapes),
        compiler_params=pltpu.CompilerParams(vmem_limit_bytes=8 << 20),
        cost_estimate=pl.CostEstimate(flops=0, bytes_accessed=2 << 20, transcendentals=0),
        name=name,
    )(*args, *before)


def corner_kernel(own, other, low, high):
    total = own[...].astype(F32) + other[...].astype(F32)
    low[...] = total[:, :4096].astype(BF16)
    high[...] = total[:, 4096:].astype(BF16)


def middle_kernel(own, other, low, high, across_up, across_down, far):
    def mine(i, first, count):
        lanes = slice(LOCAL * i + first, LOCAL * i + first + count)
        return own[:, lanes].astype(F32) + other[:, lanes].astype(F32)

    across_up[:, :4096] = (mine(0, 0, 4096) + low[...].astype(F32)).astype(BF16)
    across_up[:, 4096:] = mine(0, 4096, 4096).astype(BF16)
    across_down[:, :4096] = mine(1, 0, 4096).astype(BF16)
    across_down[:, 4096:] = (mine(1, 4096, 4096) + high[...].astype(F32)).astype(BF16)
    far[...] = mine(2, 0, LOCAL).astype(BF16)


def near_kernel(own, other, from_across, from_up, from_down, up, across, down, base):
    def mine(i):
        lanes = slice(LOCAL * i, LOCAL * (i + 1))
        return own[:, lanes].astype(F32) + other[:, lanes].astype(F32)

    up[...] = (mine(0) + from_across[...].astype(F32) + from_down[...].astype(F32)).astype(BF16)
    across[...] = (mine(1) + from_up[...].astype(F32)).astype(BF16)
    down[...] = mine(2).astype(BF16)
    base[...] = mine(3)


def last_kernel(base, a, b, c, out):
    total = base[...] + a[...].astype(F32) + b[...].astype(F32) + c[...].astype(F32)
    out[...] = total.astype(BF16)


def per_device(node_feats, weight, tiles, block_cols, cotangent):
    core = lax.axis_index("feat") % 2
    slab = lax.axis_index("blk")
    x, y = slab // 4, slab % 4
    info = jnp.stack([core] + [(x ^ dx) * 4 + (y + dy) % 4 for dx, dy in STEPS]).astype(jnp.int32)
    cols = block_cols.T

    up, down, across = (receive(node_feats, s) for s in (UP, DOWN, ACROSS))
    low_tiles, token = load_tiles(info, tiles, 0)
    feats_swapped, cot_swapped = swap(node_feats), swap(cotangent)
    up2, across2 = after(up, token, feats_swapped, cot_swapped), after(across, token, down)
    far = receive(up2, UP)
    across_up = receive(up2, ACROSS)
    across_down = receive(across2, DOWN)
    high_tiles, token = load_tiles(info, after(tiles, up2, across2), HELD // 4)
    weight_swapped = swap(after(weight, up2))
    up_half, down_half = cut(across_up, across_down, far, token)
    corner = [receive(up_half, UP), receive(down_half, DOWN)]
    pieces = [node_feats, feats_swapped]
    for block in (up, down, across, far, across_up, across_down):
        pieces += [block, swap(after(block, up_half, down_half))]
    for block in corner:
        pieces += [block, swap(block)]
    sides = [cotangent, weight, cot_swapped, weight_swapped]

    message = forward(info, cols, (low_tiles, high_tiles), pieces, sides)
    message = lax.all_to_all(message, "feat", 0, 0, axis_index_groups=SAME_CORE, tiled=True)
    message = dense(message.reshape(256, WIDE)).reshape(8, PAIR, WIDE)
    message = lax.all_to_all(message, "feat", 0, 0, axis_index_groups=SAME_CORE, tiled=True)

    own_a, own_b, own_c, other_a, other_b, other_c = backward(info, cols, tiles, message)
    half, whole = ((HALF, 4096), BF16), ((HALF, LOCAL), BF16)
    low, high = sum_call(corner_kernel, [half] * 2, (own_a, swap(other_a)), "sum_corner")
    corner_up, corner_down = send(low, UP), send(high, DOWN)
    hidden, hidden_other, wgrad, wgrad_other = unpack(info, after(message, low, high))
    wgrad_other, hidden_other = swap(wgrad_other), swap(hidden_other)
    across_up, across_down, far = sum_call(
        middle_kernel,
        [whole] * 3,
        (own_b, swap(after(other_b, low, high)), corner_up, corner_down),
        "sum_middle",
        before=(wgrad_other, hidden_other),
    )
    from_across = send(across_up, ACROSS)
    from_up = send(across_down, DOWN)
    from_down = send(far, UP)
    wgrad = wgrad + after(wgrad_other, far)
    wgrad = wgrad + receive(wgrad, ACROSS)
    up, across, down, base = sum_call(
        near_kernel,
        [whole] * 3 + [((HALF, LOCAL), F32)],
        (own_c, swap(after(other_c, far)), from_across, from_up, from_down),
        "sum_near",
        before=(wgrad,),
    )
    last = [send(up, UP), send(across, ACROSS), send(down, DOWN)]
    wgrad = after(wgrad, down)
    wgrad = wgrad + lax.ppermute(wgrad, "blk", [(b, b ^ 1) for b in range(8)])
    weight_grad = wgrad + lax.ppermute(wgrad, "blk", [(b, b ^ 2) for b in range(8)])
    hidden = join(info, after(hidden, down), hidden_other)
    (feats_grad,) = sum_call(last_kernel, [whole], (base, *last), "sum_last")
    return hidden, weight_grad, feats_grad


def solution(mesh):
    placed = (
        P("feat", "blk"),
        P("feat", None),
        P("blk", None, None, None),
        P("blk", None),
        P("feat", "blk"),
    )
    return jax.shard_map(
        per_device,
        mesh=mesh,
        in_specs=placed,
        out_specs=(P("feat", "blk"), P("feat", None), P("feat", "blk")),
        check_vma=False,
    )
```

```python
import functools

import jax
import jax.numpy as jnp
from jax import lax
from jax.experimental import pallas as pl
from jax.experimental.pallas import tpu as pltpu
from jax.sharding import PartitionSpec as P

BF16 = jnp.bfloat16
F32 = jnp.float32
ANY = pl.BlockSpec(memory_space=pl.ANY)
VMEM = pl.BlockSpec(memory_space=pltpu.VMEM)
SMEM = pl.BlockSpec(memory_space=pltpu.SMEM)

STEPS = ((0, 0), (0, 1), (0, 3), (1, 0), (0, 2), (1, 1), (1, 3), (1, 2))
UP, DOWN, ACROSS = (0, 1), (0, 3), (1, 0)
GROUPS = ((7,), (5, 6, 4), (1, 3, 2, 0))
SLABS = 8
HALF = 16
PAIR = 32
LOCAL = 8192
NODES = 65536
SLOTS = 32
ROWS = 32
CHUNK = 32
RING = 4
LIST = 1152


def _index(x, y):
    return x * 4 + y


def _from_step(step):
    dx, dy = step
    return [(_index(x ^ dx, (y + dy) % 4), _index(x, y)) for x in range(2) for y in range(4)]


def _to_step(step):
    return [(b, a) for a, b in _from_step(step)]


CORE_SWAP = [(f, f ^ 1) for f in range(16)]
SAME_CORE = [list(range(0, 16, 2)), list(range(1, 16, 2))]


def swap(a):
    return lax.ppermute(a, "feat", CORE_SWAP)


def receive(a, step):
    return lax.ppermute(a, "blk", _from_step(step))


def send(a, step):
    return lax.ppermute(a, "blk", _to_step(step))


def after(a, *others):
    return lax.optimization_barrier((a, *others))[0]


def row_of(core, local):
    return 8 * (local // 4) + 4 * core + local % 4


def lanes_of(block):
    return pl.ds(pl.multiple_of(block * 128, 128), 128)


def list_kernel(info, cols, first, second, third, counts, place):
    core = info[0]
    lists = (first, second, third)
    for group, members in enumerate(GROUPS):
        for i, d in enumerate(members):
            place[info[1 + d]] = (group << 16) + 64 * i

    def row(local, ends):
        r = row_of(core, local)
        for p in range(SLOTS):
            block = cols[p, r]
            entry = place[block // 64]
            group = entry // 65536
            value = local * 65536 + p * 256 + lax.rem(entry, 65536) + lax.rem(block, 64)
            for i in range(3):
                lists[i][ends[i]] = value
            ends = tuple(e + (group == i).astype(jnp.int32) for i, e in enumerate(ends))
        return ends

    ends = lax.fori_loop(0, ROWS, row, (jnp.int32(0),) * 3)
    for i in range(3):
        counts[i] = ends[i]

        def pad(k, carry, i=i):
            lists[i][ends[i] + k] = jnp.int32(ROWS * 65536)
            return carry

        lax.fori_loop(0, CHUNK, pad, 0)


def make_lists(info, cols):
    *lists, counts = pl.pallas_call(
        list_kernel,
        out_shape=[jax.ShapeDtypeStruct((LIST,), jnp.int32)] * 3
        + [jax.ShapeDtypeStruct((3,), jnp.int32)],
        in_specs=[SMEM, SMEM],
        out_specs=[SMEM] * 4,
        scratch_shapes=[pltpu.SMEM((8,), jnp.int32)],
        cost_estimate=pl.CostEstimate(flops=0, bytes_accessed=24 << 20, transcendentals=0),
        name="lists",
    )(info, cols)
    return lists, counts


def each_chunk(core, entries, count, tiles, ring, sems, work):
    chunks = (count + CHUNK - 1) // CHUNK

    def fetch(i):
        slot = lax.rem(i, RING)
        for t in range(CHUNK):
            entry = entries[i * CHUNK + t]
            local = jnp.minimum(entry // 65536, ROWS - 1)
            p = lax.rem(entry // 256, 256)
            pltpu.make_async_copy(
                tiles.at[row_of(core, local), p], ring.at[slot, t], sems.at[slot]
            ).start()

    def fetch_if(i):
        @pl.when(i < chunks)
        def _():
            fetch(i)

    lax.fori_loop(0, RING - 1, lambda i, c: (fetch_if(i), c)[1], 0)

    def step(i, carry):
        fetch_if(i + RING - 1)
        slot = lax.rem(i, RING)
        pltpu.make_async_copy(ring.at[slot], ring.at[slot], sems.at[slot]).wait()
        work(i, slot)
        return carry

    lax.fori_loop(0, chunks, step, 0)


RING_SCRATCH = [
    pltpu.VMEM((RING, CHUNK, 128, 128), BF16),
    pltpu.SemaphoreType.DMA((RING,)),
]


WIDE = 1280


def unpack_kernel(info, message, mine, other, wgrad_mine, wgrad_other):
    core = info[0]
    own = pl.ds(pl.multiple_of(HALF * core, HALF), HALF)
    sibling = pl.ds(pl.multiple_of(HALF * (1 - core), HALF), HALF)
    for rows, nodes, wgrad in ((own, mine, wgrad_mine), (sibling, other, wgrad_other)):
        total = jnp.zeros((HALF, 256), F32)
        for g in range(8):
            nodes[:, 512 * g : 512 * (g + 1)] = message[g, rows, 512:1024]
            total += message[g, rows, 1024:].astype(F32)
        wgrad[...] = total


def unpack(info, message):
    return pl.pallas_call(
        unpack_kernel,
        out_shape=(
            jax.ShapeDtypeStruct((HALF, 4096), BF16),
            jax.ShapeDtypeStruct((HALF, 4096), BF16),
            jax.ShapeDtypeStruct((HALF, 256), F32),
            jax.ShapeDtypeStruct((HALF, 256), F32),
        ),
        in_specs=[SMEM, VMEM],
        out_specs=(VMEM,) * 4,
        compiler_params=pltpu.CompilerParams(vmem_limit_bytes=4 << 20),
        cost_estimate=pl.CostEstimate(flops=0, bytes_accessed=1 << 20, transcendentals=0),
        name="unpack",
    )(info, message)


def join_kernel(info, mine, received, hidden):
    core = info[0]
    for g in range(8):
        chunk = slice(512 * g, 512 * (g + 1))
        a, b = mine[:, chunk], received[:, chunk]
        hidden[:, 1024 * g : 1024 * g + 512] = jnp.where(core == 0, a, b)
        hidden[:, 1024 * g + 512 : 1024 * (g + 1)] = jnp.where(core == 0, b, a)


def join(info, mine, received):
    return pl.pallas_call(
        join_kernel,
        out_shape=jax.ShapeDtypeStruct((HALF, LOCAL), BF16),
        in_specs=[SMEM, VMEM, VMEM],
        out_specs=VMEM,
        compiler_params=pltpu.CompilerParams(vmem_limit_bytes=4 << 20),
        cost_estimate=pl.CostEstimate(flops=0, bytes_accessed=1 << 20, transcendentals=0),
        name="join",
    )(info, mine, received)


def forward_kernel(group, places, info, entries, counts, tiles, *refs):
    pieces, refs = refs[: 2 * len(places)], refs[2 * len(places) :]
    if group < 2:
        before, refs = refs[0], refs[1:]
    if group == 0:
        sides, refs = refs[:4], refs[4:]
    if group == 0:
        out, total, feats, sems, ring, ring_sems = refs
    else:
        total, feats, sems, ring, ring_sems = refs
    core = info[0]
    copies = []
    for i, (first, nodes) in enumerate(places):
        for h in range(2):
            rows = pl.ds(pl.multiple_of(jnp.where(core == h, 0, HALF), HALF), HALF)
            copies.append(
                pltpu.make_async_copy(
                    pieces[2 * i + h], feats.at[rows, pl.ds(first, nodes)], sems.at[2 * i + h]
                )
            )
    for c in copies:
        c.start()
    if group == 2:
        total[...] = jnp.zeros_like(total)
    else:
        total[...] = before[...]
    if group == 0:
        for h in range(2):
            rows = pl.ds(pl.multiple_of(jnp.where(core == h, 0, HALF), HALF), HALF)
            cot, weight = sides[2 * h], sides[2 * h + 1]
            for g in range(8):
                nodes = pl.ds(pl.multiple_of(1024 * g + 512 * core, 512), 512)
                out[g, rows, 512:1024] = cot[:, nodes]
                out[g, rows, 1024:] = weight[...]
    for c in copies:
        c.wait()

    def work(i, slot):
        for t in range(CHUNK):
            entry = entries[i * CHUNK + t]
            local = entry // 65536
            left = feats[:, lanes_of(lax.rem(entry, 256))]
            total[local] += lax.dot_general(
                left, ring[slot, t], (((1,), (1,)), ((), ())), preferred_element_type=F32
            )

    each_chunk(core, entries, counts[group], tiles, ring, ring_sems, work)
    if group == 0:
        for g in range(8):
            for i in range(4):
                out[g, :, 128 * i : 128 * (i + 1)] = total[4 * g + i].astype(BF16)


def forward(group, info, entries, counts, tiles, pieces, before=None, sides=()):
    widths = [p.shape[1] for p in pieces[::2]]
    places = tuple((sum(widths[:i]), n) for i, n in enumerate(widths))
    total = (ROWS + 1, PAIR, 128)
    args = [info, entries, counts, tiles, *pieces]
    specs = [SMEM, SMEM, SMEM, ANY] + [ANY] * len(pieces)
    if before is not None:
        args.append(before)
        specs.append(VMEM)
    args += sides
    specs += [VMEM] * len(sides)
    scratch = [
        pltpu.VMEM((PAIR, sum(widths)), BF16),
        pltpu.SemaphoreType.DMA((len(pieces),)),
        *RING_SCRATCH,
    ]
    if group == 0:
        out = jax.ShapeDtypeStruct((8, PAIR, WIDE), BF16)
        scratch = [pltpu.VMEM(total, F32)] + scratch
    else:
        out = jax.ShapeDtypeStruct(total, F32)
    return pl.pallas_call(
        functools.partial(forward_kernel, group, places),
        out_shape=out,
        in_specs=specs,
        out_specs=VMEM,
        scratch_shapes=scratch,
        compiler_params=pltpu.CompilerParams(vmem_limit_bytes=16 << 20),
        cost_estimate=pl.CostEstimate(flops=1 << 20, bytes_accessed=1 << 20, transcendentals=0),
        name="forward_" + ("corner", "middle", "near")[group],
    )(*args)


def dense_kernel(message, out):
    agg = message[:, :512]
    weight = message[:, 1024:]
    pre = lax.dot_general(weight, agg, (((0,), (0,)), ((), ())), preferred_element_type=F32)
    sig = 1.0 / (1.0 + jnp.exp(-pre))
    out[:, 512:1024] = (pre * sig).astype(BF16)
    cot = message[:, 512:1024].astype(F32)
    pre_grad = (cot * sig * (1.0 + pre * (1.0 - sig))).astype(BF16)
    out[:, :512] = jnp.dot(weight, pre_grad, preferred_element_type=F32).astype(BF16)
    wgrad = lax.dot_general(agg, pre_grad, (((1,), (1,)), ((), ())), preferred_element_type=F32)
    out[:, 1024:] = wgrad.astype(BF16)


def dense(message):
    return pl.pallas_call(
        dense_kernel,
        out_shape=jax.ShapeDtypeStruct((256, WIDE), BF16),
        in_specs=[VMEM],
        out_specs=VMEM,
        compiler_params=pltpu.CompilerParams(vmem_limit_bytes=8 << 20),
        cost_estimate=pl.CostEstimate(
            flops=3 * 2 * 256 * 256 * 512, bytes_accessed=2 << 20, transcendentals=256 * 512
        ),
        name="dense",
    )(message)


def backward_kernel(group, info, entries, counts, tiles, message, own_out, other_out, *scratch):
    total, grad, ring, sems = scratch
    core = info[0]
    lanes_in_all = LOCAL * len(GROUPS[group])

    def clear(i, carry):
        total[:, pl.ds(pl.multiple_of(i * 2048, 2048), 2048)] = jnp.zeros((PAIR, 2048), F32)
        return carry

    lax.fori_loop(0, lanes_in_all // 2048, clear, 0)
    for g in range(8):
        for i in range(4):
            grad[4 * g + i] = message[g, :, 128 * i : 128 * (i + 1)]
    grad[ROWS] = jnp.zeros((PAIR, 128), BF16)

    def work(i, slot):
        for t in range(CHUNK):
            entry = entries[i * CHUNK + t]
            lanes = lanes_of(lax.rem(entry, 256))
            total[:, lanes] += jnp.dot(
                grad[entry // 65536], ring[slot, t], preferred_element_type=F32
            )

    each_chunk(core, entries, counts[group], tiles, ring, sems, work)
    own = pl.ds(pl.multiple_of(HALF * core, HALF), HALF)
    other = pl.ds(pl.multiple_of(HALF * (1 - core), HALF), HALF)
    own_out[...] = total[own, :].astype(BF16)
    other_out[...] = total[other, :].astype(BF16)


def backward(group, info, entries, counts, tiles, message):
    nodes = LOCAL * len(GROUPS[group])
    return pl.pallas_call(
        functools.partial(backward_kernel, group),
        out_shape=[jax.ShapeDtypeStruct((HALF, nodes), BF16)] * 2,
        in_specs=[SMEM, SMEM, SMEM, ANY, VMEM],
        out_specs=[VMEM] * 2,
        scratch_shapes=[
            pltpu.VMEM((PAIR, nodes), F32),
            pltpu.VMEM((ROWS + 1, PAIR, 128), BF16),
            *RING_SCRATCH,
        ],
        compiler_params=pltpu.CompilerParams(vmem_limit_bytes=16 << 20),
        cost_estimate=pl.CostEstimate(flops=1 << 20, bytes_accessed=1 << 20, transcendentals=0),
        name="backward_" + ("corner", "middle", "near")[group],
    )(info, entries, counts, tiles, message)


def cut_kernel(across_up, across_down, far, total, up_half, down_half):
    up_half[...] = across_up[:, :4096]
    down_half[...] = across_down[:, 4096:]


def cut(across_up, across_down, far, total):
    return pl.pallas_call(
        cut_kernel,
        out_shape=[jax.ShapeDtypeStruct((HALF, 4096), BF16)] * 2,
        in_specs=[VMEM, VMEM, ANY, ANY],
        out_specs=[VMEM] * 2,
        compiler_params=pltpu.CompilerParams(vmem_limit_bytes=4 << 20),
        cost_estimate=pl.CostEstimate(flops=0, bytes_accessed=1 << 19, transcendentals=0),
        name="cut",
    )(across_up, across_down, far, total)


def sum_call(kernel, shapes, args, name, before=()):
    def body(*refs):
        kernel(*refs[: len(args)], *refs[len(args) + len(before) :])

    return pl.pallas_call(
        body,
        out_shape=[jax.ShapeDtypeStruct(s, t) for s, t in shapes],
        in_specs=[VMEM] * len(args) + [ANY] * len(before),
        out_specs=[VMEM] * len(shapes),
        compiler_params=pltpu.CompilerParams(vmem_limit_bytes=8 << 20),
        cost_estimate=pl.CostEstimate(flops=0, bytes_accessed=2 << 20, transcendentals=0),
        name=name,
    )(*args, *before)


def corner_kernel(own, other, low, high):
    total = own[...].astype(F32) + other[...].astype(F32)
    low[...] = total[:, :4096].astype(BF16)
    high[...] = total[:, 4096:].astype(BF16)


def middle_kernel(own, other, low, high, across_up, across_down, far):
    def mine(i, first, count):
        lanes = slice(LOCAL * i + first, LOCAL * i + first + count)
        return own[:, lanes].astype(F32) + other[:, lanes].astype(F32)

    across_up[:, :4096] = (mine(0, 0, 4096) + low[...].astype(F32)).astype(BF16)
    across_up[:, 4096:] = mine(0, 4096, 4096).astype(BF16)
    across_down[:, :4096] = mine(1, 0, 4096).astype(BF16)
    across_down[:, 4096:] = (mine(1, 4096, 4096) + high[...].astype(F32)).astype(BF16)
    far[...] = mine(2, 0, LOCAL).astype(BF16)


def near_kernel(own, other, from_across, from_up, from_down, up, across, down, base):
    def mine(i):
        lanes = slice(LOCAL * i, LOCAL * (i + 1))
        return own[:, lanes].astype(F32) + other[:, lanes].astype(F32)

    up[...] = (mine(0) + from_across[...].astype(F32) + from_down[...].astype(F32)).astype(BF16)
    across[...] = (mine(1) + from_up[...].astype(F32)).astype(BF16)
    down[...] = mine(2).astype(BF16)
    base[...] = mine(3)


def last_kernel(base, a, b, c, out):
    total = base[...] + a[...].astype(F32) + b[...].astype(F32) + c[...].astype(F32)
    out[...] = total.astype(BF16)


def per_device(node_feats, weight, tiles, block_cols, cotangent):
    core = lax.axis_index("feat") % 2
    slab = lax.axis_index("blk")
    x, y = slab // 4, slab % 4
    info = jnp.stack([core] + [(x ^ dx) * 4 + (y + dy) % 4 for dx, dy in STEPS]).astype(jnp.int32)
    cols = block_cols.T

    up, down, across = (receive(node_feats, s) for s in (UP, DOWN, ACROSS))
    lists, counts = make_lists(info, cols)
    feats_swapped, cot_swapped = swap(node_feats), swap(cotangent)
    up, down, across, lists, counts, feats_swapped, cot_swapped = lax.optimization_barrier(
        (up, down, across, lists, counts, feats_swapped, cot_swapped)
    )
    far = receive(up, UP)
    across_up = receive(up, ACROSS)
    across_down = receive(across, DOWN)
    pieces = [up, swap(up), across, swap(across), down, swap(down), node_feats, feats_swapped]
    total = forward(2, info, lists[2], counts, tiles, pieces)
    far, across_up, across_down, total = lax.optimization_barrier(
        (far, across_up, across_down, total)
    )
    up_half, down_half = cut(across_up, across_down, far, total)
    corner = (receive(up_half, UP), receive(down_half, DOWN))
    weight_swapped = swap(weight)
    pieces = [across_up, swap(across_up), across_down, swap(across_down), far, swap(far)]
    total = forward(1, info, lists[1], counts, tiles, pieces, total)
    *corner, total = lax.optimization_barrier((*corner, total))
    pieces = [corner[0], swap(corner[0]), corner[1], swap(corner[1])]
    sides = (cotangent, weight, cot_swapped, weight_swapped)
    message = forward(0, info, lists[0], counts, tiles, pieces, total, sides)

    message = lax.all_to_all(message, "feat", 0, 0, axis_index_groups=SAME_CORE, tiled=True)
    message = dense(message.reshape(256, WIDE)).reshape(8, PAIR, WIDE)
    message = lax.all_to_all(message, "feat", 0, 0, axis_index_groups=SAME_CORE, tiled=True)

    own_a, other_a = backward(0, info, lists[0], counts, tiles, message)
    half, whole = ((HALF, 4096), BF16), ((HALF, LOCAL), BF16)
    low, high = sum_call(corner_kernel, [half] * 2, (own_a, swap(other_a)), "sum_corner")
    corner_up, corner_down = send(low, UP), send(high, DOWN)
    own_b, other_b = backward(1, info, lists[1], counts, tiles, after(message, low, high))
    hidden, hidden_other, wgrad, wgrad_other = unpack(info, after(message, low, high))
    wgrad_other, hidden_other = swap(wgrad_other), swap(hidden_other)
    other_b, corner_up, corner_down = lax.optimization_barrier((other_b, corner_up, corner_down))
    across_up, across_down, far = sum_call(
        middle_kernel,
        [whole] * 3,
        (own_b, swap(other_b), corner_up, corner_down),
        "sum_middle",
        before=(wgrad_other, hidden_other),
    )
    from_across = send(across_up, ACROSS)
    from_up = send(across_down, DOWN)
    from_down = send(far, UP)
    own_c, other_c = backward(2, info, lists[2], counts, tiles, after(message, far))
    wgrad = wgrad + after(wgrad_other, far)
    wgrad = wgrad + receive(wgrad, ACROSS)
    other_c, from_across, from_up, from_down = lax.optimization_barrier(
        (other_c, from_across, from_up, from_down)
    )
    up, across, down, base = sum_call(
        near_kernel,
        [whole] * 3 + [((HALF, LOCAL), F32)],
        (own_c, swap(other_c), from_across, from_up, from_down),
        "sum_near",
        before=(wgrad,),
    )
    last = [send(up, UP), send(across, ACROSS), send(down, DOWN)]
    wgrad = after(wgrad, down)
    wgrad = wgrad + lax.ppermute(wgrad, "blk", [(b, b ^ 1) for b in range(8)])
    weight_grad = wgrad + lax.ppermute(wgrad, "blk", [(b, b ^ 2) for b in range(8)])
    hidden = join(info, after(hidden, down), hidden_other)
    (feats_grad,) = sum_call(last_kernel, [whole], (base, *last), "sum_last")
    return hidden, weight_grad, feats_grad


def solution(mesh):
    placed = (
        P("feat", "blk"),
        P("feat", None),
        P("blk", None, None, None),
        P("blk", None),
        P("feat", "blk"),
    )
    return jax.shard_map(
        per_device,
        mesh=mesh,
        in_specs=placed,
        out_specs=(P("feat", "blk"), P("feat", None), P("feat", "blk")),
        check_vma=False,
    )
```

```python
import functools

import jax
import jax.numpy as jnp
from jax import lax
from jax.experimental import pallas as pl
from jax.experimental.pallas import tpu as pltpu
from jax.sharding import PartitionSpec as P

BF16 = jnp.bfloat16
F32 = jnp.float32
ANY = pl.BlockSpec(memory_space=pl.ANY)
VMEM = pl.BlockSpec(memory_space=pltpu.VMEM)
SMEM = pl.BlockSpec(memory_space=pltpu.SMEM)

STEPS = ((0, 0), (0, 1), (0, 3), (1, 0), (0, 2), (1, 1), (1, 3), (1, 2))
UP, DOWN, ACROSS, CORNER = (0, 1), (0, 3), (1, 0), (1, 2)
GROUPS = ((5, 6, 4, 7), (1, 3, 2, 0))
SLABS = 8
HALF = 16
PAIR = 32
LOCAL = 8192
NODES = 65536
SLOTS = 32
ROWS = 32
RING = 16


def _index(x, y):
    return x * 4 + y


def _from_step(step):
    dx, dy = step
    return [(_index(x ^ dx, (y + dy) % 4), _index(x, y)) for x in range(2) for y in range(4)]


def _to_step(step):
    return [(b, a) for a, b in _from_step(step)]


CORE_SWAP = [(f, f ^ 1) for f in range(16)]
SAME_CORE = [list(range(0, 16, 2)), list(range(1, 16, 2))]


def swap(a):
    return lax.ppermute(a, "feat", CORE_SWAP)


def receive(a, step):
    return lax.ppermute(a, "blk", _from_step(step))


def send(a, step):
    return lax.ppermute(a, "blk", _to_step(step))


def row_of(core, local):
    return 8 * (local // 4) + 4 * core + local % 4


def lanes_of(block):
    return pl.ds(pl.multiple_of(block * 128, 128), 128)


def load_kernel(info, tiles, low, high, token, sems):
    core = info[0]
    copies = []
    for g in range(8):
        half = (low, high)[g // 4]
        copies.append(
            pltpu.make_async_copy(
                tiles.at[pl.ds(8 * g + 4 * core, 4)], half.at[pl.ds(4 * (g % 4), 4)], sems.at[g]
            )
        )
    for c in copies:
        c.start()
    token[...] = jnp.zeros_like(token)
    for c in copies:
        c.wait()


def load_tiles(info, tiles):
    *held, token = pl.pallas_call(
        load_kernel,
        out_shape=(
            pltpu.VMEM((ROWS // 2, SLOTS, 128, 128), BF16),
            pltpu.VMEM((ROWS // 2, SLOTS, 128, 128), BF16),
            jax.ShapeDtypeStruct((8, 128), F32),
        ),
        in_specs=[SMEM, ANY],
        out_specs=(VMEM, VMEM, VMEM),
        scratch_shapes=[pltpu.SemaphoreType.DMA((8,))],
        compiler_params=pltpu.CompilerParams(vmem_limit_bytes=2 << 20),
        cost_estimate=pl.CostEstimate(flops=0, bytes_accessed=48 << 20, transcendentals=0),
        name="load_tiles",
    )(info, tiles)
    return [pltpu.with_memory_space_constraint(h, pltpu.VMEM) for h in held], token


def gate(arrays, before):
    n = len(arrays)
    return pl.pallas_call(
        lambda *refs: None,
        out_shape=[jax.ShapeDtypeStruct(a.shape, a.dtype) for a in arrays],
        in_specs=[ANY] * (n + len(before)),
        out_specs=[ANY] * n,
        input_output_aliases={i: i for i in range(n)},
        compiler_params=pltpu.CompilerParams(vmem_limit_bytes=1 << 20),
        cost_estimate=pl.CostEstimate(flops=0, bytes_accessed=1024, transcendentals=0),
        name="gate",
    )(*arrays, *before)


WIDE = 1280


def unpack_kernel(info, message, before, mine, other, wgrad_mine, wgrad_other):
    core = info[0]
    own = pl.ds(pl.multiple_of(HALF * core, HALF), HALF)
    sibling = pl.ds(pl.multiple_of(HALF * (1 - core), HALF), HALF)
    for rows, nodes, wgrad in ((own, mine, wgrad_mine), (sibling, other, wgrad_other)):
        total = jnp.zeros((HALF, 256), F32)
        for g in range(8):
            nodes[:, 512 * g : 512 * (g + 1)] = message[g, rows, 512:1024]
            total += message[g, rows, 1024:].astype(F32)
        wgrad[...] = total


def unpack(info, message, before):
    return pl.pallas_call(
        unpack_kernel,
        out_shape=(
            jax.ShapeDtypeStruct((HALF, 4096), BF16),
            jax.ShapeDtypeStruct((HALF, 4096), BF16),
            jax.ShapeDtypeStruct((HALF, 256), F32),
            jax.ShapeDtypeStruct((HALF, 256), F32),
        ),
        in_specs=[SMEM, VMEM, ANY],
        out_specs=(VMEM,) * 4,
        compiler_params=pltpu.CompilerParams(vmem_limit_bytes=4 << 20),
        cost_estimate=pl.CostEstimate(flops=0, bytes_accessed=1 << 20, transcendentals=0),
        name="unpack",
    )(info, message, before)


def join_kernel(info, mine, received, before, hidden):
    core = info[0]
    for g in range(8):
        chunk = slice(512 * g, 512 * (g + 1))
        a, b = mine[:, chunk], received[:, chunk]
        hidden[:, 1024 * g : 1024 * g + 512] = jnp.where(core == 0, a, b)
        hidden[:, 1024 * g + 512 : 1024 * (g + 1)] = jnp.where(core == 0, b, a)


def join(info, mine, received, before):
    return pl.pallas_call(
        join_kernel,
        out_shape=jax.ShapeDtypeStruct((HALF, LOCAL), BF16),
        in_specs=[SMEM, VMEM, VMEM, ANY],
        out_specs=VMEM,
        compiler_params=pltpu.CompilerParams(vmem_limit_bytes=4 << 20),
        cost_estimate=pl.CostEstimate(flops=0, bytes_accessed=1 << 20, transcendentals=0),
        name="join",
    )(info, mine, received, before)


def forward_kernel(info, cols, low_tiles, high_tiles, *refs):
    pieces, sides, (out, feats, sems) = refs[:16], refs[16:20], refs[20:]
    core = info[0]
    copies = []
    for i in range(SLABS):
        at = pl.multiple_of(info[1 + i] * LOCAL, LOCAL)
        for h in range(2):
            rows = pl.ds(pl.multiple_of(jnp.where(core == h, 0, HALF), HALF), HALF)
            copies.append(
                pltpu.make_async_copy(
                    pieces[2 * i + h], feats.at[rows, pl.ds(at, LOCAL)], sems.at[2 * i + h]
                )
            )
    for c in copies:
        c.start()
    for h in range(2):
        rows = pl.ds(pl.multiple_of(jnp.where(core == h, 0, HALF), HALF), HALF)
        cot, weight = sides[2 * h], sides[2 * h + 1]
        for g in range(8):
            nodes = pl.ds(pl.multiple_of(1024 * g + 512 * core, 512), 512)
            out[g, rows, 512:1024] = cot[:, nodes]
            out[g, rows, 1024:] = weight[...]
    for c in copies:
        c.wait()

    def four_rows(first, tiles, sums):
        rows = [row_of(core, first + k) for k in range(4)]

        def push(unit, p, register):
            right = [
                jnp.concatenate([tiles[lax.rem(first, 16) + k, p + e] for e in range(2)], axis=1)
                for k in (2 * unit, 2 * unit + 1)
            ]
            pltpu.matmul_push_rhs(
                jnp.concatenate(right, axis=0), register, unit, transpose=True
            )

        def multiply(unit, p, register):
            left = [
                jnp.concatenate([feats[:, lanes_of(cols[p + e, r])] for e in range(2)], axis=1)
                for r in rows[2 * unit : 2 * unit + 2]
            ]
            pltpu.matmul_acc_lhs(
                sums[unit], jnp.concatenate(left, axis=0), load_staged_rhs=register
            )

        for unit in range(2):
            push(unit, 0, 0)
        for p in range(0, SLOTS, 2):
            if p + 2 < SLOTS:
                for unit in range(2):
                    push(unit, p + 2, (p // 2 + 1) % 2)
            for unit in range(2):
                multiply(unit, p, (p // 2) % 2)
        for unit in range(2):
            got = pltpu.matmul_pop(sums[unit])
            for k in range(2):
                value = got[PAIR * k : PAIR * (k + 1), 128 * k : 128 * (k + 1)]
                j = 2 * unit + k
                out[first // 4, :, 128 * j : 128 * (j + 1)] = value.astype(BF16)

    for half, tiles in enumerate((low_tiles, high_tiles)):

        def step(i, carry, tiles=tiles):
            pl.run_scoped(
                lambda *sums: four_rows(4 * i, tiles, sums),
                *[pltpu.ACC(unit)((2 * PAIR, 256), F32) for unit in range(2)],
            )
            return carry

        lax.fori_loop(4 * half, 4 * half + 4, step, 0)


def forward(info, cols, held, pieces, sides):
    return pl.pallas_call(
        forward_kernel,
        out_shape=jax.ShapeDtypeStruct((8, PAIR, WIDE), BF16),
        in_specs=[SMEM, SMEM, VMEM, VMEM] + [ANY] * 16 + [VMEM] * 4,
        out_specs=VMEM,
        scratch_shapes=[
            pltpu.VMEM((PAIR, NODES), BF16),
            pltpu.SemaphoreType.DMA((16,)),
        ],
        compiler_params=pltpu.CompilerParams(vmem_limit_bytes=8 << 20),
        cost_estimate=pl.CostEstimate(
            flops=8 * 2 * 1024 * 128 * 128 * 32, bytes_accessed=8 << 20, transcendentals=0
        ),
        name="forward",
    )(info, cols, *held, *pieces, *sides)


def dense_kernel(message, out):
    agg = message[:, :512]
    weight = message[:, 1024:]
    pre = lax.dot_general(weight, agg, (((0,), (0,)), ((), ())), preferred_element_type=F32)
    sig = 1.0 / (1.0 + jnp.exp(-pre))
    out[:, 512:1024] = (pre * sig).astype(BF16)
    cot = message[:, 512:1024].astype(F32)
    pre_grad = (cot * sig * (1.0 + pre * (1.0 - sig))).astype(BF16)
    out[:, :512] = jnp.dot(weight, pre_grad, preferred_element_type=F32).astype(BF16)
    wgrad = lax.dot_general(agg, pre_grad, (((1,), (1,)), ((), ())), preferred_element_type=F32)
    out[:, 1024:] = wgrad.astype(BF16)


def dense(message):
    return pl.pallas_call(
        dense_kernel,
        out_shape=jax.ShapeDtypeStruct((256, WIDE), BF16),
        in_specs=[VMEM],
        out_specs=VMEM,
        compiler_params=pltpu.CompilerParams(vmem_limit_bytes=8 << 20),
        cost_estimate=pl.CostEstimate(
            flops=3 * 2 * 256 * 256 * 512, bytes_accessed=2 << 20, transcendentals=256 * 512
        ),
        name="dense",
    )(message)


def backward_kernel(info, cols, tiles, grad, *refs):
    outs, (total, ring, sems) = refs[:4], refs[4:]
    core = info[0]

    def copy(i):
        slot = lax.rem(i, RING)
        return pltpu.make_async_copy(tiles.at[row_of(core, i)], ring.at[slot], sems.at[slot])

    for i in range(RING):
        copy(jnp.int32(i)).start()

    def clear(i, carry):
        total[:, pl.ds(pl.multiple_of(i * 2048, 2048), 2048)] = jnp.zeros((PAIR, 2048), F32)
        return carry

    lax.fori_loop(0, NODES // 2048, clear, 0)

    def row(local):
        r = row_of(core, local)
        slot = lax.rem(local, RING)
        g = grad[local // 4, :, lanes_of(lax.rem(local, 4))]
        for first in range(0, SLOTS, 8):
            blocks = [lanes_of(cols[first + i, r]) for i in range(8)]
            terms = []
            for i in range(first, first + 8, 2):
                pair = jnp.concatenate([ring[slot, i], ring[slot, i + 1]], axis=1)
                both = jnp.dot(g, pair, preferred_element_type=F32)
                terms += [both[:, :128], both[:, 128:]]
            sums = [total[:, blocks[i]] + terms[i] for i in range(8)]
            for i in range(8):
                total[:, blocks[i]] = sums[i]

    def step(i, carry):
        for k in range(2):
            copy(2 * i + k).wait()
        for k in range(2):
            row(2 * i + k)

        @pl.when(2 * i + RING < ROWS)
        def _():
            for k in range(2):
                copy(2 * i + k + RING).start()

        return carry

    lax.fori_loop(0, ROWS // 2, step, 0)

    own = pl.ds(pl.multiple_of(HALF * core, HALF), HALF)
    other = pl.ds(pl.multiple_of(HALF * (1 - core), HALF), HALF)
    for phase, group in enumerate(GROUPS):
        for i, d in enumerate(group):
            lanes = pl.ds(pl.multiple_of(info[1 + d] * LOCAL, LOCAL), LOCAL)
            place = slice(LOCAL * i, LOCAL * (i + 1))
            outs[phase][:, place] = total[own, lanes].astype(BF16)
            outs[2 + phase][:, place] = total[other, lanes].astype(BF16)


def backward(info, cols, tiles, grad):
    return pl.pallas_call(
        backward_kernel,
        out_shape=[jax.ShapeDtypeStruct((HALF, LOCAL * len(g)), BF16) for g in GROUPS] * 2,
        in_specs=[SMEM, SMEM, ANY, VMEM],
        out_specs=[VMEM] * 4,
        scratch_shapes=[
            pltpu.VMEM((PAIR, NODES), F32),
            pltpu.VMEM((RING, SLOTS, 128, 128), BF16),
            pltpu.SemaphoreType.DMA((RING,)),
        ],
        compiler_params=pltpu.CompilerParams(vmem_limit_bytes=32 << 20),
        cost_estimate=pl.CostEstimate(
            flops=8 * 2 * 1024 * 128 * 128 * 32, bytes_accessed=8 << 20, transcendentals=0
        ),
        name="backward",
    )(info, cols, tiles, grad)


def sum_call(kernel, shapes, args, name, before=()):
    def body(*refs):
        kernel(*refs[: len(args)], *refs[len(args) + len(before) :])

    return pl.pallas_call(
        body,
        out_shape=[jax.ShapeDtypeStruct(s, t) for s, t in shapes],
        in_specs=[VMEM] * len(args) + [ANY] * len(before),
        out_specs=[VMEM] * len(shapes),
        compiler_params=pltpu.CompilerParams(vmem_limit_bytes=8 << 20),
        cost_estimate=pl.CostEstimate(flops=0, bytes_accessed=2 << 20, transcendentals=0),
        name=name,
    )(*args, *before)


def far_kernel(own, other, wgrad, wgrad_other, *outs):
    for i, out in enumerate(outs[:4]):
        lanes = slice(LOCAL * i, LOCAL * (i + 1))
        out[...] = (own[:, lanes].astype(F32) + other[:, lanes].astype(F32)).astype(BF16)
    outs[4][...] = wgrad[...] + wgrad_other[...]


def near_kernel(own, other, from_across, from_up, from_down, up, across, down, base):
    def mine(i):
        lanes = slice(LOCAL * i, LOCAL * (i + 1))
        return own[:, lanes].astype(F32) + other[:, lanes].astype(F32)

    up[...] = (mine(0) + from_across[...].astype(F32) + from_down[...].astype(F32)).astype(BF16)
    across[...] = (mine(1) + from_up[...].astype(F32)).astype(BF16)
    down[...] = mine(2).astype(BF16)
    base[...] = mine(3)


def last_kernel(base, *refs):
    *received, out = refs
    total = base[...]
    for a in received:
        total += a[...].astype(F32)
    out[...] = total.astype(BF16)


def per_device(node_feats, weight, tiles, block_cols, cotangent):
    core = lax.axis_index("feat") % 2
    slab = lax.axis_index("blk")
    x, y = slab // 4, slab % 4
    info = jnp.stack([core] + [(x ^ dx) * 4 + (y + dy) % 4 for dx, dy in STEPS]).astype(jnp.int32)
    cols = block_cols.T

    up, down, across, corner = (receive(node_feats, s) for s in (UP, DOWN, ACROSS, CORNER))
    held, token = load_tiles(info, tiles)
    feats_swapped, cot_swapped = swap(node_feats), swap(cotangent)
    up, down, across, corner = gate(
        (up, down, across, corner), (token, feats_swapped, cot_swapped)
    )
    far = receive(up, UP)
    across_up = receive(up, ACROSS)
    across_down = receive(across, DOWN)
    pieces = [node_feats, feats_swapped]
    for block in (up, down, across, far, across_up, across_down, corner):
        pieces += [block, swap(block)]
    sides = [cotangent, weight, cot_swapped, swap(weight)]

    message = forward(info, cols, held, pieces, sides)
    message = lax.all_to_all(message, "feat", 0, 0, axis_index_groups=SAME_CORE, tiled=True)
    message = dense(message.reshape(256, WIDE)).reshape(8, PAIR, WIDE)
    message = lax.all_to_all(message, "feat", 0, 0, axis_index_groups=SAME_CORE, tiled=True)

    own_a, own_c, other_a, other_c = backward(info, cols, tiles, message)
    whole = ((HALF, LOCAL), BF16)
    hidden, hidden_other, wgrad, wgrad_other = unpack(info, message, own_a)
    hidden_other, wgrad_other = swap(hidden_other), swap(wgrad_other)
    across_up, across_down, far, corner, wgrad = sum_call(
        far_kernel,
        [whole] * 4 + [((HALF, 256), F32)],
        (own_a, swap(other_a), wgrad, wgrad_other),
        "sum_far",
        (hidden_other,),
    )
    from_across = send(across_up, ACROSS)
    from_up = send(across_down, DOWN)
    from_down = send(far, UP)
    from_corner = send(corner, CORNER)
    (other_c,) = gate((other_c,), (far,))
    wgrad = wgrad + receive(wgrad, ACROSS)
    up, across, down, base = sum_call(
        near_kernel,
        [whole] * 3 + [((HALF, LOCAL), F32)],
        (own_c, swap(other_c), from_across, from_up, from_down),
        "sum_near",
        (wgrad,),
    )
    last = [send(up, UP), send(across, ACROSS), send(down, DOWN)]
    weight_grad = wgrad + receive(wgrad, UP) + receive(wgrad, DOWN) + receive(wgrad, (0, 2))
    hidden = join(info, hidden, hidden_other, down)
    (feats_grad,) = sum_call(last_kernel, [whole], (base, from_corner, *last), "sum_last")
    return hidden, weight_grad, feats_grad


def solution(mesh):
    placed = (
        P("feat", "blk"),
        P("feat", None),
        P("blk", None, None, None),
        P("blk", None),
        P("feat", "blk"),
    )
    return jax.shard_map(
        per_device,
        mesh=mesh,
        in_specs=placed,
        out_specs=(P("feat", "blk"), P("feat", None), P("feat", "blk")),
        check_vma=False,
    )
```

```python
import functools

import jax
import jax.numpy as jnp
from jax import lax
from jax.experimental import pallas as pl
from jax.experimental.pallas import tpu as pltpu
from jax.sharding import PartitionSpec as P

BF16 = jnp.bfloat16
F32 = jnp.float32
ANY = pl.BlockSpec(memory_space=pl.ANY)
VMEM = pl.BlockSpec(memory_space=pltpu.VMEM)
SMEM = pl.BlockSpec(memory_space=pltpu.SMEM)

STEPS = ((0, 0), (0, 1), (0, 3), (1, 0), (0, 2), (1, 1), (1, 3), (1, 2))
UP, DOWN, ACROSS, CORNER = (0, 1), (0, 3), (1, 0), (1, 2)
GROUPS = ((5, 6, 4, 7), (1, 3, 2, 0))
SLABS = 8
HALF = 16
PAIR = 32
LOCAL = 8192
NODES = 65536
SLOTS = 32
ROWS = 32
RING = 16


def _index(x, y):
    return x * 4 + y


def _from_step(step):
    dx, dy = step
    return [(_index(x ^ dx, (y + dy) % 4), _index(x, y)) for x in range(2) for y in range(4)]


def _to_step(step):
    return [(b, a) for a, b in _from_step(step)]


CORE_SWAP = [(f, f ^ 1) for f in range(16)]
SAME_CORE = [list(range(0, 16, 2)), list(range(1, 16, 2))]


def swap(a):
    return lax.ppermute(a, "feat", CORE_SWAP)


def receive(a, step):
    return lax.ppermute(a, "blk", _from_step(step))


def send(a, step):
    return lax.ppermute(a, "blk", _to_step(step))


def row_of(core, local):
    return 8 * (local // 4) + 4 * core + local % 4


def lanes_of(block):
    return pl.ds(pl.multiple_of(block * 128, 128), 128)


def load_kernel(info, tiles, low, high, token, sems):
    core = info[0]
    copies = []
    for g in range(8):
        half = (low, high)[g // 4]
        copies.append(
            pltpu.make_async_copy(
                tiles.at[pl.ds(8 * g + 4 * core, 4)], half.at[pl.ds(4 * (g % 4), 4)], sems.at[g]
            )
        )
    for c in copies:
        c.start()
    token[...] = jnp.zeros_like(token)
    for c in copies:
        c.wait()


def load_tiles(info, tiles):
    *held, token = pl.pallas_call(
        load_kernel,
        out_shape=(
            pltpu.VMEM((ROWS // 2, SLOTS, 128, 128), BF16),
            pltpu.VMEM((ROWS // 2, SLOTS, 128, 128), BF16),
            jax.ShapeDtypeStruct((8, 128), F32),
        ),
        in_specs=[SMEM, ANY],
        out_specs=(VMEM, VMEM, VMEM),
        scratch_shapes=[pltpu.SemaphoreType.DMA((8,))],
        compiler_params=pltpu.CompilerParams(vmem_limit_bytes=2 << 20),
        cost_estimate=pl.CostEstimate(flops=0, bytes_accessed=48 << 20, transcendentals=0),
        name="load_tiles",
    )(info, tiles)
    return [pltpu.with_memory_space_constraint(h, pltpu.VMEM) for h in held], token


def gate(arrays, before):
    n = len(arrays)
    return pl.pallas_call(
        lambda *refs: None,
        out_shape=[jax.ShapeDtypeStruct(a.shape, a.dtype) for a in arrays],
        in_specs=[ANY] * (n + len(before)),
        out_specs=[ANY] * n,
        input_output_aliases={i: i for i in range(n)},
        compiler_params=pltpu.CompilerParams(vmem_limit_bytes=1 << 20),
        cost_estimate=pl.CostEstimate(flops=0, bytes_accessed=1024, transcendentals=0),
        name="gate",
    )(*arrays, *before)


def bundle_kernel(up, across, down, corner, feats, cot, weight, token, up_out, across_out, out):
    for i, a in enumerate((up, across, down, corner, feats, cot)):
        out[:, LOCAL * i : LOCAL * (i + 1)] = a[...]
    out[:, 6 * LOCAL :] = weight[...]


def bundle(up, across, down, corner, feats, cot, weight, token):
    wide = 6 * LOCAL + 256
    return pl.pallas_call(
        bundle_kernel,
        out_shape=[
            jax.ShapeDtypeStruct(up.shape, BF16),
            jax.ShapeDtypeStruct(across.shape, BF16),
            jax.ShapeDtypeStruct((HALF, wide), BF16),
        ],
        in_specs=[VMEM] * 7 + [ANY],
        out_specs=[ANY, ANY, VMEM],
        input_output_aliases={0: 0, 1: 1},
        compiler_params=pltpu.CompilerParams(vmem_limit_bytes=8 << 20),
        cost_estimate=pl.CostEstimate(flops=0, bytes_accessed=3 << 20, transcendentals=0),
        name="bundle",
    )(up, across, down, corner, feats, cot, weight, token)


WIDE = 1280


def unpack_kernel(info, message, before, mine, other, wgrad_mine, wgrad_other):
    core = info[0]
    own = pl.ds(pl.multiple_of(HALF * core, HALF), HALF)
    sibling = pl.ds(pl.multiple_of(HALF * (1 - core), HALF), HALF)
    for rows, nodes, wgrad in ((own, mine, wgrad_mine), (sibling, other, wgrad_other)):
        total = jnp.zeros((HALF, 256), F32)
        for g in range(8):
            nodes[:, 512 * g : 512 * (g + 1)] = message[g, rows, 512:1024]
            total += message[g, rows, 1024:].astype(F32)
        wgrad[...] = total


def unpack(info, message, before):
    return pl.pallas_call(
        unpack_kernel,
        out_shape=(
            jax.ShapeDtypeStruct((HALF, 4096), BF16),
            jax.ShapeDtypeStruct((HALF, 4096), BF16),
            jax.ShapeDtypeStruct((HALF, 256), F32),
            jax.ShapeDtypeStruct((HALF, 256), F32),
        ),
        in_specs=[SMEM, VMEM, ANY],
        out_specs=(VMEM,) * 4,
        compiler_params=pltpu.CompilerParams(vmem_limit_bytes=4 << 20),
        cost_estimate=pl.CostEstimate(flops=0, bytes_accessed=1 << 20, transcendentals=0),
        name="unpack",
    )(info, message, before)


def join_kernel(info, mine, received, before, hidden):
    core = info[0]
    for g in range(8):
        chunk = slice(512 * g, 512 * (g + 1))
        a, b = mine[:, chunk], received[:, chunk]
        hidden[:, 1024 * g : 1024 * g + 512] = jnp.where(core == 0, a, b)
        hidden[:, 1024 * g + 512 : 1024 * (g + 1)] = jnp.where(core == 0, b, a)


def join(info, mine, received, before):
    return pl.pallas_call(
        join_kernel,
        out_shape=jax.ShapeDtypeStruct((HALF, LOCAL), BF16),
        in_specs=[SMEM, VMEM, VMEM, ANY],
        out_specs=VMEM,
        compiler_params=pltpu.CompilerParams(vmem_limit_bytes=4 << 20),
        cost_estimate=pl.CostEstimate(flops=0, bytes_accessed=1 << 20, transcendentals=0),
        name="join",
    )(info, mine, received, before)


def forward_kernel(places, info, cols, low_tiles, high_tiles, *refs):
    own, others, cot, weight, (out, feats, sems) = refs[:8], refs[8:12], refs[12], refs[13], refs[14:]
    core = info[0]
    mine = pl.ds(pl.multiple_of(HALF * core, HALF), HALF)
    sibling = pl.ds(pl.multiple_of(HALF * (1 - core), HALF), HALF)
    copies = []
    for i, (which, first) in enumerate(places):
        at = pl.ds(pl.multiple_of(info[1 + i] * LOCAL, LOCAL), LOCAL)
        other = others[which].at[:, pl.ds(first, LOCAL)]
        copies += [
            pltpu.make_async_copy(own[i], feats.at[mine, at], sems.at[2 * i]),
            pltpu.make_async_copy(other, feats.at[sibling, at], sems.at[2 * i + 1]),
        ]
    for c in copies:
        c.start()
    near = others[0]
    for g in range(8):
        at = 1024 * g + 512 * core
        out[g, mine, 512:1024] = cot[:, pl.ds(pl.multiple_of(at, 512), 512)]
        out[g, mine, 1024:] = weight[...]
        at = 5 * LOCAL + at
        out[g, sibling, 512:1024] = near[:, pl.ds(pl.multiple_of(at, 512), 512)]
        out[g, sibling, 1024:] = near[:, 6 * LOCAL :]
    for c in copies:
        c.wait()

    def four_rows(first, tiles, sums):
        rows = [row_of(core, first + k) for k in range(4)]

        def push(unit, p, register):
            right = [
                jnp.concatenate([tiles[lax.rem(first, 16) + k, p + e] for e in range(2)], axis=1)
                for k in (2 * unit, 2 * unit + 1)
            ]
            pltpu.matmul_push_rhs(
                jnp.concatenate(right, axis=0), register, unit, transpose=True
            )

        def multiply(unit, p, register):
            left = [
                jnp.concatenate([feats[:, lanes_of(cols[p + e, r])] for e in range(2)], axis=1)
                for r in rows[2 * unit : 2 * unit + 2]
            ]
            pltpu.matmul_acc_lhs(
                sums[unit], jnp.concatenate(left, axis=0), load_staged_rhs=register
            )

        for unit in range(2):
            push(unit, 0, 0)
        for p in range(0, SLOTS, 2):
            if p + 2 < SLOTS:
                for unit in range(2):
                    push(unit, p + 2, (p // 2 + 1) % 2)
            for unit in range(2):
                multiply(unit, p, (p // 2) % 2)
        for unit in range(2):
            got = pltpu.matmul_pop(sums[unit])
            for k in range(2):
                value = got[PAIR * k : PAIR * (k + 1), 128 * k : 128 * (k + 1)]
                j = 2 * unit + k
                out[first // 4, :, 128 * j : 128 * (j + 1)] = value.astype(BF16)

    for half, tiles in enumerate((low_tiles, high_tiles)):

        def step(i, carry, tiles=tiles):
            pl.run_scoped(
                lambda *sums: four_rows(4 * i, tiles, sums),
                *[pltpu.ACC(unit)((2 * PAIR, 256), F32) for unit in range(2)],
            )
            return carry

        lax.fori_loop(4 * half, 4 * half + 4, step, 0)


def forward(info, cols, held, pieces, cot, weight):
    own = [p[0] for p in pieces]
    others = []
    for _, other, _ in pieces:
        if not any(other is o for o in others):
            others.append(other)
    places = tuple((next(k for k, o in enumerate(others) if o is p[1]), p[2]) for p in pieces)
    return pl.pallas_call(
        functools.partial(forward_kernel, places),
        out_shape=jax.ShapeDtypeStruct((8, PAIR, WIDE), BF16),
        in_specs=[SMEM, SMEM, VMEM, VMEM] + [ANY] * 8 + [VMEM] + [ANY] * 3 + [VMEM] * 2,
        out_specs=VMEM,
        scratch_shapes=[
            pltpu.VMEM((PAIR, NODES), BF16),
            pltpu.SemaphoreType.DMA((16,)),
        ],
        compiler_params=pltpu.CompilerParams(vmem_limit_bytes=10 << 20),
        cost_estimate=pl.CostEstimate(
            flops=8 * 2 * 1024 * 128 * 128 * 32, bytes_accessed=8 << 20, transcendentals=0
        ),
        name="forward",
    )(info, cols, *held, *own, *others, cot, weight)


def dense_kernel(message, out):
    agg = message[:, :512]
    weight = message[:, 1024:]
    pre = lax.dot_general(weight, agg, (((0,), (0,)), ((), ())), preferred_element_type=F32)
    sig = 1.0 / (1.0 + jnp.exp(-pre))
    out[:, 512:1024] = (pre * sig).astype(BF16)
    cot = message[:, 512:1024].astype(F32)
    pre_grad = (cot * sig * (1.0 + pre * (1.0 - sig))).astype(BF16)
    out[:, :512] = jnp.dot(weight, pre_grad, preferred_element_type=F32).astype(BF16)
    wgrad = lax.dot_general(agg, pre_grad, (((1,), (1,)), ((), ())), preferred_element_type=F32)
    out[:, 1024:] = wgrad.astype(BF16)


def dense(message):
    return pl.pallas_call(
        dense_kernel,
        out_shape=jax.ShapeDtypeStruct((256, WIDE), BF16),
        in_specs=[VMEM],
        out_specs=VMEM,
        compiler_params=pltpu.CompilerParams(vmem_limit_bytes=8 << 20),
        cost_estimate=pl.CostEstimate(
            flops=3 * 2 * 256 * 256 * 512, bytes_accessed=2 << 20, transcendentals=256 * 512
        ),
        name="dense",
    )(message)


def backward_kernel(info, cols, tiles, grad, *refs):
    outs, (total, ring, sems) = refs[:4], refs[4:]
    core = info[0]

    def copy(i):
        slot = lax.rem(i, RING)
        return pltpu.make_async_copy(tiles.at[row_of(core, i)], ring.at[slot], sems.at[slot])

    for i in range(RING):
        copy(jnp.int32(i)).start()

    def clear(i, carry):
        total[:, pl.ds(pl.multiple_of(i * 2048, 2048), 2048)] = jnp.zeros((PAIR, 2048), F32)
        return carry

    lax.fori_loop(0, NODES // 2048, clear, 0)

    def row(local):
        r = row_of(core, local)
        slot = lax.rem(local, RING)
        g = grad[local // 4, :, lanes_of(lax.rem(local, 4))]
        for first in range(0, SLOTS, 8):
            blocks = [lanes_of(cols[first + i, r]) for i in range(8)]
            terms = []
            for i in range(first, first + 8, 2):
                pair = jnp.concatenate([ring[slot, i], ring[slot, i + 1]], axis=1)
                both = jnp.dot(g, pair, preferred_element_type=F32)
                terms += [both[:, :128], both[:, 128:]]
            sums = [total[:, blocks[i]] + terms[i] for i in range(8)]
            for i in range(8):
                total[:, blocks[i]] = sums[i]

    def step(i, carry):
        for k in range(2):
            copy(2 * i + k).wait()
        for k in range(2):
            row(2 * i + k)

        @pl.when(2 * i + RING < ROWS)
        def _():
            for k in range(2):
                copy(2 * i + k + RING).start()

        return carry

    lax.fori_loop(0, ROWS // 2, step, 0)

    own = pl.ds(pl.multiple_of(HALF * core, HALF), HALF)
    other = pl.ds(pl.multiple_of(HALF * (1 - core), HALF), HALF)
    for phase, group in enumerate(GROUPS):
        for i, d in enumerate(group):
            lanes = pl.ds(pl.multiple_of(info[1 + d] * LOCAL, LOCAL), LOCAL)
            place = slice(LOCAL * i, LOCAL * (i + 1))
            outs[phase][:, place] = total[own, lanes].astype(BF16)
            outs[2 + phase][:, place] = total[other, lanes].astype(BF16)


def backward(info, cols, tiles, grad):
    return pl.pallas_call(
        backward_kernel,
        out_shape=[jax.ShapeDtypeStruct((HALF, LOCAL * len(g)), BF16) for g in GROUPS] * 2,
        in_specs=[SMEM, SMEM, ANY, VMEM],
        out_specs=[VMEM] * 4,
        scratch_shapes=[
            pltpu.VMEM((PAIR, NODES), F32),
            pltpu.VMEM((RING, SLOTS, 128, 128), BF16),
            pltpu.SemaphoreType.DMA((RING,)),
        ],
        compiler_params=pltpu.CompilerParams(vmem_limit_bytes=32 << 20),
        cost_estimate=pl.CostEstimate(
            flops=8 * 2 * 1024 * 128 * 128 * 32, bytes_accessed=8 << 20, transcendentals=0
        ),
        name="backward",
    )(info, cols, tiles, grad)


def sum_call(kernel, shapes, args, name, before=()):
    def body(*refs):
        kernel(*refs[: len(args)], *refs[len(args) + len(before) :])

    return pl.pallas_call(
        body,
        out_shape=[jax.ShapeDtypeStruct(s, t) for s, t in shapes],
        in_specs=[VMEM] * len(args) + [ANY] * len(before),
        out_specs=[VMEM] * len(shapes),
        compiler_params=pltpu.CompilerParams(vmem_limit_bytes=8 << 20),
        cost_estimate=pl.CostEstimate(flops=0, bytes_accessed=2 << 20, transcendentals=0),
        name=name,
    )(*args, *before)


def far_kernel(own, other, wgrad, wgrad_other, *outs):
    for i, out in enumerate(outs[:4]):
        lanes = slice(LOCAL * i, LOCAL * (i + 1))
        out[:, :LOCAL] = (own[:, lanes].astype(F32) + other[:, lanes].astype(F32)).astype(BF16)
        out[:, LOCAL:] = (wgrad[...] + wgrad_other[...]).astype(BF16)
    outs[4][...] = wgrad[...] + wgrad_other[...]


def near_kernel(own, other, wgrad, from_across, from_up, from_down, up, across, down, base):
    def mine(i):
        lanes = slice(LOCAL * i, LOCAL * (i + 1))
        return own[:, lanes].astype(F32) + other[:, lanes].astype(F32)

    for i, (out, received) in enumerate(
        ((up, (from_across, from_down)), (across, (from_up,)), (down, ()), (base, ()))
    ):
        piece, terms = mine(i), wgrad[...]
        for r in received:
            piece += r[:, :LOCAL].astype(F32)
            terms += r[:, LOCAL:].astype(F32)
        out[:, :LOCAL] = piece.astype(out.dtype)
        out[:, LOCAL:] = terms.astype(out.dtype)


def last_kernel(base, *refs):
    *received, feats_grad, weight_grad = refs
    total = base[...]
    for a in received:
        total += a[...].astype(F32)
    feats_grad[...] = total[:, :LOCAL].astype(BF16)
    weight_grad[...] = total[:, LOCAL:]


def per_device(node_feats, weight, tiles, block_cols, cotangent):
    core = lax.axis_index("feat") % 2
    slab = lax.axis_index("blk")
    x, y = slab // 4, slab % 4
    info = jnp.stack([core] + [(x ^ dx) * 4 + (y + dy) % 4 for dx, dy in STEPS]).astype(jnp.int32)
    cols = block_cols.T

    up, down, across, corner = (receive(node_feats, s) for s in (UP, DOWN, ACROSS, CORNER))
    held, token = load_tiles(info, tiles)
    up, across, near = bundle(up, across, down, corner, node_feats, cotangent, weight, token)
    far = receive(up, UP)
    across_up = receive(up, ACROSS)
    across_down = receive(across, DOWN)
    near = swap(near)
    pieces = [
        (node_feats, near, 4 * LOCAL),
        (up, near, 0),
        (down, near, 2 * LOCAL),
        (across, near, LOCAL),
        (far, swap(far), 0),
        (across_up, swap(across_up), 0),
        (across_down, swap(across_down), 0),
        (corner, near, 3 * LOCAL),
    ]
    message = forward(info, cols, held, pieces, cotangent, weight)
    message = lax.all_to_all(message, "feat", 0, 0, axis_index_groups=SAME_CORE, tiled=True)
    message = dense(message.reshape(256, WIDE)).reshape(8, PAIR, WIDE)
    message = lax.all_to_all(message, "feat", 0, 0, axis_index_groups=SAME_CORE, tiled=True)

    own_a, own_c, other_a, other_c = backward(info, cols, tiles, message)
    piece = ((HALF, LOCAL + 256), BF16)
    hidden, hidden_other, wgrad, wgrad_other = unpack(info, message, own_a)
    hidden_other = swap(hidden_other)
    across_up, across_down, far, corner, wgrad = sum_call(
        far_kernel,
        [piece] * 4 + [((HALF, 256), F32)],
        (own_a, swap(other_a), wgrad, swap(wgrad_other)),
        "sum_far",
    )
    from_across = send(across_up, ACROSS)
    from_up = send(across_down, DOWN)
    from_down = send(far, UP)
    from_corner = send(corner, CORNER)
    (other_c,) = gate((other_c,), (far,))
    up, across, down, base = sum_call(
        near_kernel,
        [piece] * 3 + [((HALF, LOCAL + 256), F32)],
        (own_c, swap(other_c), wgrad, from_across, from_up, from_down),
        "sum_near",
    )
    hidden = join(info, hidden, hidden_other, down)
    last = [send(up, UP), send(across, ACROSS), send(down, DOWN)]
    feats_grad, weight_grad = sum_call(
        last_kernel,
        [((HALF, LOCAL), BF16), ((HALF, 256), F32)],
        (base, from_corner, *last),
        "sum_last",
    )
    return hidden, weight_grad, feats_grad


def solution(mesh):
    placed = (
        P("feat", "blk"),
        P("feat", None),
        P("blk", None, None, None),
        P("blk", None),
        P("feat", "blk"),
    )
    return jax.shard_map(
        per_device,
        mesh=mesh,
        in_specs=placed,
        out_specs=(P("feat", "blk"), P("feat", None), P("feat", "blk")),
        check_vma=False,
    )
```

```python
import functools

import jax
import jax.numpy as jnp
from jax import lax
from jax.experimental import pallas as pl
from jax.experimental.pallas import tpu as pltpu
from jax.sharding import PartitionSpec as P

BF16 = jnp.bfloat16
F32 = jnp.float32
ANY = pl.BlockSpec(memory_space=pl.ANY)
VMEM = pl.BlockSpec(memory_space=pltpu.VMEM)
SMEM = pl.BlockSpec(memory_space=pltpu.SMEM)

STEPS = ((0, 0), (0, 1), (0, 3), (1, 0), (0, 2), (1, 1), (1, 3), (1, 2))
UP, DOWN, ACROSS, CORNER = (0, 1), (0, 3), (1, 0), (1, 2)
GROUPS = ((5, 6, 4, 7), (1, 3, 2, 0))
SLABS = 8
HALF = 16
PAIR = 32
LOCAL = 8192
NODES = 65536
SLOTS = 32
ROWS = 32


def _index(x, y):
    return x * 4 + y


def _from_step(step):
    dx, dy = step
    return [(_index(x ^ dx, (y + dy) % 4), _index(x, y)) for x in range(2) for y in range(4)]


def _to_step(step):
    return [(b, a) for a, b in _from_step(step)]


CORE_SWAP = [(f, f ^ 1) for f in range(16)]
SAME_CORE = [list(range(0, 16, 2)), list(range(1, 16, 2))]


def swap(a):
    return lax.ppermute(a, "feat", CORE_SWAP)


def receive(a, step):
    return lax.ppermute(a, "blk", _from_step(step))


def send(a, step):
    return lax.ppermute(a, "blk", _to_step(step))


def row_of(core, local):
    return 8 * (local // 4) + 4 * core + local % 4


def lanes_of(block):
    return pl.ds(pl.multiple_of(block * 128, 128), 128)


def load_kernel(info, tiles, held, token, sems):
    core = info[0]
    copies = []
    for g in range(4):
        copies.append(
            pltpu.make_async_copy(
                tiles.at[pl.ds(8 * g + 4 * core, 4)], held.at[pl.ds(4 * g, 4)], sems.at[g]
            )
        )
    for c in copies:
        c.start()
    token[...] = jnp.zeros_like(token)
    for c in copies:
        c.wait()


def load_tiles(info, tiles):
    held, token = pl.pallas_call(
        load_kernel,
        out_shape=(
            pltpu.VMEM((ROWS // 2, SLOTS, 128, 128), BF16),
            jax.ShapeDtypeStruct((8, 128), F32),
        ),
        in_specs=[SMEM, ANY],
        out_specs=(VMEM, VMEM),
        scratch_shapes=[pltpu.SemaphoreType.DMA((4,))],
        compiler_params=pltpu.CompilerParams(vmem_limit_bytes=2 << 20),
        cost_estimate=pl.CostEstimate(flops=0, bytes_accessed=48 << 20, transcendentals=0),
        name="load_tiles",
    )(info, tiles)
    return pltpu.with_memory_space_constraint(held, pltpu.VMEM), token


def gate(arrays, before):
    n = len(arrays)
    return pl.pallas_call(
        lambda *refs: None,
        out_shape=[jax.ShapeDtypeStruct(a.shape, a.dtype) for a in arrays],
        in_specs=[ANY] * (n + len(before)),
        out_specs=[ANY] * n,
        input_output_aliases={i: i for i in range(n)},
        compiler_params=pltpu.CompilerParams(vmem_limit_bytes=1 << 20),
        cost_estimate=pl.CostEstimate(flops=0, bytes_accessed=1024, transcendentals=0),
        name="gate",
    )(*arrays, *before)


def bundle_kernel(up, across, down, corner, feats, cot, weight, token, up_out, across_out, out):
    for i, a in enumerate((up, across, down, corner, feats, cot)):
        out[:, LOCAL * i : LOCAL * (i + 1)] = a[...]
    out[:, 6 * LOCAL :] = weight[...]


def bundle(up, across, down, corner, feats, cot, weight, token):
    wide = 6 * LOCAL + 256
    return pl.pallas_call(
        bundle_kernel,
        out_shape=[
            jax.ShapeDtypeStruct(up.shape, BF16),
            jax.ShapeDtypeStruct(across.shape, BF16),
            jax.ShapeDtypeStruct((HALF, wide), BF16),
        ],
        in_specs=[VMEM] * 7 + [ANY],
        out_specs=[ANY, ANY, VMEM],
        input_output_aliases={0: 0, 1: 1},
        compiler_params=pltpu.CompilerParams(vmem_limit_bytes=8 << 20),
        cost_estimate=pl.CostEstimate(flops=0, bytes_accessed=3 << 20, transcendentals=0),
        name="bundle",
    )(up, across, down, corner, feats, cot, weight, token)


WIDE = 1280


def unpack_kernel(info, message, before, mine, other, wgrad_mine, wgrad_other):
    core = info[0]
    own = pl.ds(pl.multiple_of(HALF * core, HALF), HALF)
    sibling = pl.ds(pl.multiple_of(HALF * (1 - core), HALF), HALF)
    for rows, nodes, wgrad in ((own, mine, wgrad_mine), (sibling, other, wgrad_other)):
        total = jnp.zeros((HALF, 256), F32)
        for g in range(8):
            nodes[:, 512 * g : 512 * (g + 1)] = message[g, rows, 512:1024]
            total += message[g, rows, 1024:].astype(F32)
        wgrad[...] = total


def unpack(info, message, before):
    return pl.pallas_call(
        unpack_kernel,
        out_shape=(
            jax.ShapeDtypeStruct((HALF, 4096), BF16),
            jax.ShapeDtypeStruct((HALF, 4096), BF16),
            jax.ShapeDtypeStruct((HALF, 256), F32),
            jax.ShapeDtypeStruct((HALF, 256), F32),
        ),
        in_specs=[SMEM, VMEM, ANY],
        out_specs=(VMEM,) * 4,
        compiler_params=pltpu.CompilerParams(vmem_limit_bytes=4 << 20),
        cost_estimate=pl.CostEstimate(flops=0, bytes_accessed=1 << 20, transcendentals=0),
        name="unpack",
    )(info, message, before)


def join_kernel(info, mine, received, before, hidden):
    core = info[0]
    for g in range(8):
        chunk = slice(512 * g, 512 * (g + 1))
        a, b = mine[:, chunk], received[:, chunk]
        hidden[:, 1024 * g : 1024 * g + 512] = jnp.where(core == 0, a, b)
        hidden[:, 1024 * g + 512 : 1024 * (g + 1)] = jnp.where(core == 0, b, a)


def join(info, mine, received, before):
    return pl.pallas_call(
        join_kernel,
        out_shape=jax.ShapeDtypeStruct((HALF, LOCAL), BF16),
        in_specs=[SMEM, VMEM, VMEM, ANY],
        out_specs=VMEM,
        compiler_params=pltpu.CompilerParams(vmem_limit_bytes=4 << 20),
        cost_estimate=pl.CostEstimate(flops=0, bytes_accessed=1 << 20, transcendentals=0),
        name="join",
    )(info, mine, received, before)


def forward_kernel(places, info, cols, low_tiles, tiles, *refs):
    own, others, cot, weight = refs[:8], refs[8:12], refs[12], refs[13]
    out, high_tiles, feats, sems, stream_sems = refs[14:]
    core = info[0]
    mine = pl.ds(pl.multiple_of(HALF * core, HALF), HALF)
    sibling = pl.ds(pl.multiple_of(HALF * (1 - core), HALF), HALF)
    copies = []
    for i, (which, first) in enumerate(places):
        at = pl.ds(pl.multiple_of(info[1 + i] * LOCAL, LOCAL), LOCAL)
        other = others[which].at[:, pl.ds(first, LOCAL)]
        copies += [
            pltpu.make_async_copy(own[i], feats.at[mine, at], sems.at[2 * i]),
            pltpu.make_async_copy(other, feats.at[sibling, at], sems.at[2 * i + 1]),
        ]
    stream = [
        pltpu.make_async_copy(
            tiles.at[pl.ds(8 * (4 + g) + 4 * core, 4)],
            high_tiles.at[pl.ds(4 * g, 4)],
            stream_sems.at[g],
        )
        for g in range(4)
    ]
    for c in copies + stream:
        c.start()
    near = others[0]
    for g in range(8):
        at = 1024 * g + 512 * core
        out[g, mine, 512:1024] = cot[:, pl.ds(pl.multiple_of(at, 512), 512)]
        out[g, mine, 1024:] = weight[...]
        at = 5 * LOCAL + at
        out[g, sibling, 512:1024] = near[:, pl.ds(pl.multiple_of(at, 512), 512)]
        out[g, sibling, 1024:] = near[:, 6 * LOCAL :]
    for c in copies:
        c.wait()

    def four_rows(first, tiles, sums):
        rows = [row_of(core, first + k) for k in range(4)]

        def push(unit, p, register):
            right = [
                jnp.concatenate([tiles[lax.rem(first, 16) + k, p + e] for e in range(2)], axis=1)
                for k in (2 * unit, 2 * unit + 1)
            ]
            pltpu.matmul_push_rhs(
                jnp.concatenate(right, axis=0), register, unit, transpose=True
            )

        def multiply(unit, p, register):
            left = [
                jnp.concatenate([feats[:, lanes_of(cols[p + e, r])] for e in range(2)], axis=1)
                for r in rows[2 * unit : 2 * unit + 2]
            ]
            pltpu.matmul_acc_lhs(
                sums[unit], jnp.concatenate(left, axis=0), load_staged_rhs=register
            )

        for unit in range(2):
            push(unit, 0, 0)
        for p in range(0, SLOTS, 2):
            if p + 2 < SLOTS:
                for unit in range(2):
                    push(unit, p + 2, (p // 2 + 1) % 2)
            for unit in range(2):
                multiply(unit, p, (p // 2) % 2)
        for unit in range(2):
            got = pltpu.matmul_pop(sums[unit])
            for k in range(2):
                value = got[PAIR * k : PAIR * (k + 1), 128 * k : 128 * (k + 1)]
                j = 2 * unit + k
                out[first // 4, :, 128 * j : 128 * (j + 1)] = value.astype(BF16)

    for half, tiles in enumerate((low_tiles, high_tiles)):

        def step(i, carry, tiles=tiles):
            pl.run_scoped(
                lambda *sums: four_rows(4 * i, tiles, sums),
                *[pltpu.ACC(unit)((2 * PAIR, 256), F32) for unit in range(2)],
            )
            return carry

        if half:
            for c in stream:
                c.wait()
        lax.fori_loop(4 * half, 4 * half + 4, step, 0)


def forward(info, cols, held, tiles, pieces, cot, weight):
    own = [p[0] for p in pieces]
    others = []
    for _, other, _ in pieces:
        if not any(other is o for o in others):
            others.append(other)
    places = tuple((next(k for k, o in enumerate(others) if o is p[1]), p[2]) for p in pieces)
    message, streamed = pl.pallas_call(
        functools.partial(forward_kernel, places),
        out_shape=(
            jax.ShapeDtypeStruct((8, PAIR, WIDE), BF16),
            pltpu.VMEM((ROWS // 2, SLOTS, 128, 128), BF16),
        ),
        in_specs=[SMEM, SMEM, VMEM, ANY] + [ANY] * 8 + [VMEM] + [ANY] * 3 + [VMEM] * 2,
        out_specs=(VMEM, VMEM),
        scratch_shapes=[
            pltpu.VMEM((PAIR, NODES), BF16),
            pltpu.SemaphoreType.DMA((16,)),
            pltpu.SemaphoreType.DMA((4,)),
        ],
        compiler_params=pltpu.CompilerParams(vmem_limit_bytes=10 << 20),
        cost_estimate=pl.CostEstimate(
            flops=8 * 2 * 1024 * 128 * 128 * 32, bytes_accessed=8 << 20, transcendentals=0
        ),
        name="forward",
    )(info, cols, held, tiles, *own, *others, cot, weight)
    return message, pltpu.with_memory_space_constraint(streamed, pltpu.VMEM)


def dense_kernel(message, out):
    agg = message[:, :512]
    weight = message[:, 1024:]
    pre = lax.dot_general(weight, agg, (((0,), (0,)), ((), ())), preferred_element_type=F32)
    sig = 1.0 / (1.0 + jnp.exp(-pre))
    out[:, 512:1024] = (pre * sig).astype(BF16)
    cot = message[:, 512:1024].astype(F32)
    pre_grad = (cot * sig * (1.0 + pre * (1.0 - sig))).astype(BF16)
    out[:, :512] = jnp.dot(weight, pre_grad, preferred_element_type=F32).astype(BF16)
    wgrad = lax.dot_general(agg, pre_grad, (((1,), (1,)), ((), ())), preferred_element_type=F32)
    out[:, 1024:] = wgrad.astype(BF16)


def dense(message):
    return pl.pallas_call(
        dense_kernel,
        out_shape=jax.ShapeDtypeStruct((256, WIDE), BF16),
        in_specs=[VMEM],
        out_specs=VMEM,
        compiler_params=pltpu.CompilerParams(vmem_limit_bytes=8 << 20),
        cost_estimate=pl.CostEstimate(
            flops=3 * 2 * 256 * 256 * 512, bytes_accessed=2 << 20, transcendentals=256 * 512
        ),
        name="dense",
    )(message)


def backward_kernel(info, cols, low_tiles, high_tiles, grad, *refs):
    outs, total = refs[:4], refs[4]
    core = info[0]

    def clear(i, carry):
        total[:, pl.ds(pl.multiple_of(i * 2048, 2048), 2048)] = jnp.zeros((PAIR, 2048), F32)
        return carry

    lax.fori_loop(0, NODES // 2048, clear, 0)

    def row(local, tiles):
        r = row_of(core, local)
        g = grad[local // 4, :, lanes_of(lax.rem(local, 4))]
        at = lax.rem(local, 16)
        for first in range(0, SLOTS, 8):
            blocks = [lanes_of(cols[first + i, r]) for i in range(8)]
            terms = []
            for i in range(first, first + 8, 2):
                pair = jnp.concatenate([tiles[at, i], tiles[at, i + 1]], axis=1)
                both = jnp.dot(g, pair, preferred_element_type=F32)
                terms += [both[:, :128], both[:, 128:]]
            sums = [total[:, blocks[i]] + terms[i] for i in range(8)]
            for i in range(8):
                total[:, blocks[i]] = sums[i]

    for half, tiles in enumerate((low_tiles, high_tiles)):

        def step(i, carry, tiles=tiles):
            for k in range(4):
                row(4 * i + k, tiles)
            return carry

        lax.fori_loop(4 * half, 4 * half + 4, step, 0)

    own = pl.ds(pl.multiple_of(HALF * core, HALF), HALF)
    other = pl.ds(pl.multiple_of(HALF * (1 - core), HALF), HALF)
    for phase, group in enumerate(GROUPS):
        for i, d in enumerate(group):
            lanes = pl.ds(pl.multiple_of(info[1 + d] * LOCAL, LOCAL), LOCAL)
            place = slice(LOCAL * i, LOCAL * (i + 1))
            outs[phase][:, place] = total[own, lanes].astype(BF16)
            outs[2 + phase][:, place] = total[other, lanes].astype(BF16)


def backward(info, cols, held, grad):
    return pl.pallas_call(
        backward_kernel,
        out_shape=[jax.ShapeDtypeStruct((HALF, LOCAL * len(g)), BF16) for g in GROUPS] * 2,
        in_specs=[SMEM, SMEM, VMEM, VMEM, VMEM],
        out_specs=[VMEM] * 4,
        scratch_shapes=[
            pltpu.VMEM((PAIR, NODES), F32),
        ],
        compiler_params=pltpu.CompilerParams(vmem_limit_bytes=10 << 20),
        cost_estimate=pl.CostEstimate(
            flops=8 * 2 * 1024 * 128 * 128 * 32, bytes_accessed=8 << 20, transcendentals=0
        ),
        name="backward",
    )(info, cols, *held, grad)


def sum_call(kernel, shapes, args, name, before=()):
    def body(*refs):
        kernel(*refs[: len(args)], *refs[len(args) + len(before) :])

    return pl.pallas_call(
        body,
        out_shape=[jax.ShapeDtypeStruct(s, t) for s, t in shapes],
        in_specs=[VMEM] * len(args) + [ANY] * len(before),
        out_specs=[VMEM] * len(shapes),
        compiler_params=pltpu.CompilerParams(vmem_limit_bytes=8 << 20),
        cost_estimate=pl.CostEstimate(flops=0, bytes_accessed=2 << 20, transcendentals=0),
        name=name,
    )(*args, *before)


def far_kernel(own, other, wgrad, wgrad_other, *outs):
    for i, out in enumerate(outs[:4]):
        lanes = slice(LOCAL * i, LOCAL * (i + 1))
        out[:, :LOCAL] = (own[:, lanes].astype(F32) + other[:, lanes].astype(F32)).astype(BF16)
        out[:, LOCAL:] = (wgrad[...] + wgrad_other[...]).astype(BF16)
    outs[4][...] = wgrad[...] + wgrad_other[...]


def near_kernel(own, other, wgrad, from_across, from_up, from_down, up, across, down, base):
    def mine(i):
        lanes = slice(LOCAL * i, LOCAL * (i + 1))
        return own[:, lanes].astype(F32) + other[:, lanes].astype(F32)

    for i, (out, received) in enumerate(
        ((up, (from_across, from_down)), (across, (from_up,)), (down, ()), (base, ()))
    ):
        piece, terms = mine(i), wgrad[...]
        for r in received:
            piece += r[:, :LOCAL].astype(F32)
            terms += r[:, LOCAL:].astype(F32)
        out[:, :LOCAL] = piece.astype(out.dtype)
        out[:, LOCAL:] = terms.astype(out.dtype)


def last_kernel(base, *refs):
    *received, feats_grad, weight_grad = refs
    total = base[...]
    for a in received:
        total += a[...].astype(F32)
    feats_grad[...] = total[:, :LOCAL].astype(BF16)
    weight_grad[...] = total[:, LOCAL:]


def per_device(node_feats, weight, tiles, block_cols, cotangent):
    core = lax.axis_index("feat") % 2
    slab = lax.axis_index("blk")
    x, y = slab // 4, slab % 4
    info = jnp.stack([core] + [(x ^ dx) * 4 + (y + dy) % 4 for dx, dy in STEPS]).astype(jnp.int32)
    cols = block_cols.T

    up, down, across, corner = (receive(node_feats, s) for s in (UP, DOWN, ACROSS, CORNER))
    held, token = load_tiles(info, tiles)
    up, across, near = bundle(up, across, down, corner, node_feats, cotangent, weight, token)
    far = receive(up, UP)
    across_up = receive(up, ACROSS)
    across_down = receive(across, DOWN)
    near = swap(near)
    pieces = [
        (node_feats, near, 4 * LOCAL),
        (up, near, 0),
        (down, near, 2 * LOCAL),
        (across, near, LOCAL),
        (far, swap(far), 0),
        (across_up, swap(across_up), 0),
        (across_down, swap(across_down), 0),
        (corner, near, 3 * LOCAL),
    ]
    message, streamed = forward(info, cols, held, tiles, pieces, cotangent, weight)
    message = lax.all_to_all(message, "feat", 0, 0, axis_index_groups=SAME_CORE, tiled=True)
    message = dense(message.reshape(256, WIDE)).reshape(8, PAIR, WIDE)
    message = lax.all_to_all(message, "feat", 0, 0, axis_index_groups=SAME_CORE, tiled=True)

    own_a, own_c, other_a, other_c = backward(info, cols, (held, streamed), message)
    piece = ((HALF, LOCAL + 256), BF16)
    hidden, hidden_other, wgrad, wgrad_other = unpack(info, message, own_a)
    hidden_other = swap(hidden_other)
    across_up, across_down, far, corner, wgrad = sum_call(
        far_kernel,
        [piece] * 4 + [((HALF, 256), F32)],
        (own_a, swap(other_a), wgrad, swap(wgrad_other)),
        "sum_far",
    )
    from_across = send(across_up, ACROSS)
    from_up = send(across_down, DOWN)
    from_down = send(far, UP)
    from_corner = send(corner, CORNER)
    (other_c,) = gate((other_c,), (far,))
    up, across, down, base = sum_call(
        near_kernel,
        [piece] * 3 + [((HALF, LOCAL + 256), F32)],
        (own_c, swap(other_c), wgrad, from_across, from_up, from_down),
        "sum_near",
    )
    hidden = join(info, hidden, hidden_other, down)
    last = [send(up, UP), send(across, ACROSS), send(down, DOWN)]
    feats_grad, weight_grad = sum_call(
        last_kernel,
        [((HALF, LOCAL), BF16), ((HALF, 256), F32)],
        (base, from_corner, *last),
        "sum_last",
    )
    return hidden, weight_grad, feats_grad


def solution(mesh):
    placed = (
        P("feat", "blk"),
        P("feat", None),
        P("blk", None, None, None),
        P("blk", None),
        P("feat", "blk"),
    )
    return jax.shard_map(
        per_device,
        mesh=mesh,
        in_specs=placed,
        out_specs=(P("feat", "blk"), P("feat", None), P("feat", "blk")),
        check_vma=False,
    )
```

```python
import functools

import jax
import jax.numpy as jnp
from jax import lax
from jax.experimental import pallas as pl
from jax.experimental.pallas import tpu as pltpu
from jax.sharding import PartitionSpec as P

BF16 = jnp.bfloat16
F32 = jnp.float32
ANY = pl.BlockSpec(memory_space=pl.ANY)
VMEM = pl.BlockSpec(memory_space=pltpu.VMEM)
SMEM = pl.BlockSpec(memory_space=pltpu.SMEM)

STEPS = ((0, 0), (0, 1), (0, 3), (1, 0), (0, 2), (1, 1), (1, 3), (1, 2))
UP, DOWN, ACROSS, CORNER = (0, 1), (0, 3), (1, 0), (1, 2)
GROUPS = ((5, 6, 4, 7), (1, 3, 2, 0))
SLABS = 8
HALF = 16
PAIR = 32
LOCAL = 8192
NODES = 65536
SLOTS = 32
ROWS = 32


def _index(x, y):
    return x * 4 + y


def _from_step(step):
    dx, dy = step
    return [(_index(x ^ dx, (y + dy) % 4), _index(x, y)) for x in range(2) for y in range(4)]


def _to_step(step):
    return [(b, a) for a, b in _from_step(step)]


CORE_SWAP = [(f, f ^ 1) for f in range(16)]
SAME_CORE = [list(range(0, 16, 2)), list(range(1, 16, 2))]


def swap(a):
    return lax.ppermute(a, "feat", CORE_SWAP)


def receive(a, step):
    return lax.ppermute(a, "blk", _from_step(step))


def send(a, step):
    return lax.ppermute(a, "blk", _to_step(step))


def row_of(core, local):
    return 8 * (local // 4) + 4 * core + local % 4


def lanes_of(block):
    return pl.ds(pl.multiple_of(block * 128, 128), 128)


def load_kernel(info, tiles, held, token, sems):
    core = info[0]
    copies = []
    for g in range(4):
        copies.append(
            pltpu.make_async_copy(
                tiles.at[pl.ds(8 * g + 4 * core, 4)], held.at[pl.ds(4 * g, 4)], sems.at[g]
            )
        )
    for c in copies:
        c.start()
    token[...] = jnp.zeros_like(token)
    for c in copies:
        c.wait()


def load_tiles(info, tiles):
    held, token = pl.pallas_call(
        load_kernel,
        out_shape=(
            pltpu.VMEM((ROWS // 2, SLOTS, 128, 128), BF16),
            jax.ShapeDtypeStruct((8, 128), F32),
        ),
        in_specs=[SMEM, ANY],
        out_specs=(VMEM, VMEM),
        scratch_shapes=[pltpu.SemaphoreType.DMA((4,))],
        compiler_params=pltpu.CompilerParams(vmem_limit_bytes=2 << 20),
        cost_estimate=pl.CostEstimate(flops=0, bytes_accessed=48 << 20, transcendentals=0),
        name="load_tiles",
    )(info, tiles)
    return pltpu.with_memory_space_constraint(held, pltpu.VMEM), token


def gate(arrays, before):
    n = len(arrays)
    return pl.pallas_call(
        lambda *refs: None,
        out_shape=[jax.ShapeDtypeStruct(a.shape, a.dtype) for a in arrays],
        in_specs=[ANY] * (n + len(before)),
        out_specs=[ANY] * n,
        input_output_aliases={i: i for i in range(n)},
        compiler_params=pltpu.CompilerParams(vmem_limit_bytes=1 << 20),
        cost_estimate=pl.CostEstimate(flops=0, bytes_accessed=1024, transcendentals=0),
        name="gate",
    )(*arrays, *before)


def bundle_kernel(feats, cot, weight, up, across, down, corner, token, local, first, second):
    for out, parts in ((local, (feats, cot)), (first, (up, across)), (second, (down, corner))):
        for i, a in enumerate(parts):
            out[:, LOCAL * i : LOCAL * (i + 1)] = a[...]
    local[:, 2 * LOCAL :] = weight[...]


def bundle(*args):
    return pl.pallas_call(
        bundle_kernel,
        out_shape=[
            jax.ShapeDtypeStruct((HALF, 2 * LOCAL + n), BF16) for n in (256, 0, 0)
        ],
        in_specs=[VMEM] * 7 + [ANY],
        out_specs=[VMEM] * 3,
        compiler_params=pltpu.CompilerParams(vmem_limit_bytes=8 << 20),
        cost_estimate=pl.CostEstimate(flops=0, bytes_accessed=3 << 20, transcendentals=0),
        name="bundle",
    )(*args)


WIDE = 1280


def unpack_kernel(info, message, before, mine, other):
    core = info[0]
    own = pl.ds(pl.multiple_of(HALF * core, HALF), HALF)
    sibling = pl.ds(pl.multiple_of(HALF * (1 - core), HALF), HALF)
    for rows, nodes in ((own, mine), (sibling, other)):
        for g in range(8):
            nodes[:, 512 * g : 512 * (g + 1)] = message[g, rows, 512:1024]


def unpack(info, message, before):
    return pl.pallas_call(
        unpack_kernel,
        out_shape=[jax.ShapeDtypeStruct((HALF, 4096), BF16)] * 2,
        in_specs=[SMEM, VMEM, ANY],
        out_specs=[VMEM] * 2,
        compiler_params=pltpu.CompilerParams(vmem_limit_bytes=4 << 20),
        cost_estimate=pl.CostEstimate(flops=0, bytes_accessed=1 << 20, transcendentals=0),
        name="unpack",
    )(info, message, before)


def join_kernel(info, mine, received, before, hidden):
    core = info[0]
    for g in range(8):
        chunk = slice(512 * g, 512 * (g + 1))
        a, b = mine[:, chunk], received[:, chunk]
        hidden[:, 1024 * g : 1024 * g + 512] = jnp.where(core == 0, a, b)
        hidden[:, 1024 * g + 512 : 1024 * (g + 1)] = jnp.where(core == 0, b, a)


def join(info, mine, received, before):
    return pl.pallas_call(
        join_kernel,
        out_shape=jax.ShapeDtypeStruct((HALF, LOCAL), BF16),
        in_specs=[SMEM, VMEM, VMEM, ANY],
        out_specs=VMEM,
        compiler_params=pltpu.CompilerParams(vmem_limit_bytes=4 << 20),
        cost_estimate=pl.CostEstimate(flops=0, bytes_accessed=1 << 20, transcendentals=0),
        name="join",
    )(info, mine, received, before)


def forward_kernel(places, info, cols, low_tiles, tiles, *refs):
    own, others, cot, weight = refs[:8], refs[8:14], refs[14], refs[15]
    out, high_tiles, feats, sems, stream_sems = refs[16:]
    core = info[0]
    mine = pl.ds(pl.multiple_of(HALF * core, HALF), HALF)
    sibling = pl.ds(pl.multiple_of(HALF * (1 - core), HALF), HALF)
    copies = []
    for i, (which, first) in enumerate(places):
        at = pl.ds(pl.multiple_of(info[1 + i] * LOCAL, LOCAL), LOCAL)
        other = others[which].at[:, pl.ds(first, LOCAL)]
        copies += [
            pltpu.make_async_copy(own[i], feats.at[mine, at], sems.at[2 * i]),
            pltpu.make_async_copy(other, feats.at[sibling, at], sems.at[2 * i + 1]),
        ]
    stream = [
        pltpu.make_async_copy(
            tiles.at[pl.ds(8 * (4 + g) + 4 * core, 4)],
            high_tiles.at[pl.ds(4 * g, 4)],
            stream_sems.at[g],
        )
        for g in range(4)
    ]
    for c in copies + stream:
        c.start()
    local = others[0]
    for g in range(8):
        at = 1024 * g + 512 * core
        out[g, mine, 512:1024] = cot[:, pl.ds(pl.multiple_of(at, 512), 512)]
        out[g, mine, 1024:] = weight[...]
        at = LOCAL + at
        out[g, sibling, 512:1024] = local[:, pl.ds(pl.multiple_of(at, 512), 512)]
        out[g, sibling, 1024:] = local[:, 2 * LOCAL :]
    for c in copies:
        c.wait()

    def four_rows(first, tiles, sums):
        rows = [row_of(core, first + k) for k in range(4)]

        def push(unit, p, register):
            right = [
                jnp.concatenate([tiles[lax.rem(first, 16) + k, p + e] for e in range(2)], axis=1)
                for k in (2 * unit, 2 * unit + 1)
            ]
            pltpu.matmul_push_rhs(
                jnp.concatenate(right, axis=0), register, unit, transpose=True
            )

        def multiply(unit, p, register):
            left = [
                jnp.concatenate([feats[:, lanes_of(cols[p + e, r])] for e in range(2)], axis=1)
                for r in rows[2 * unit : 2 * unit + 2]
            ]
            pltpu.matmul_acc_lhs(
                sums[unit], jnp.concatenate(left, axis=0), load_staged_rhs=register
            )

        for unit in range(2):
            push(unit, 0, 0)
        for p in range(0, SLOTS, 2):
            if p + 2 < SLOTS:
                for unit in range(2):
                    push(unit, p + 2, (p // 2 + 1) % 2)
            for unit in range(2):
                multiply(unit, p, (p // 2) % 2)
        for unit in range(2):
            got = pltpu.matmul_pop(sums[unit])
            for k in range(2):
                value = got[PAIR * k : PAIR * (k + 1), 128 * k : 128 * (k + 1)]
                j = 2 * unit + k
                out[first // 4, :, 128 * j : 128 * (j + 1)] = value.astype(BF16)

    for half, tiles in enumerate((low_tiles, high_tiles)):

        def step(i, carry, tiles=tiles):
            pl.run_scoped(
                lambda *sums: four_rows(4 * i, tiles, sums),
                *[pltpu.ACC(unit)((2 * PAIR, 256), F32) for unit in range(2)],
            )
            return carry

        if half:
            for c in stream:
                c.wait()
        lax.fori_loop(4 * half, 4 * half + 4, step, 0)


def forward(info, cols, held, tiles, pieces, cot, weight):
    own = [p[0] for p in pieces]
    others = []
    for _, other, _ in pieces:
        if not any(other is o for o in others):
            others.append(other)
    places = tuple((next(k for k, o in enumerate(others) if o is p[1]), p[2]) for p in pieces)
    message, streamed = pl.pallas_call(
        functools.partial(forward_kernel, places),
        out_shape=(
            jax.ShapeDtypeStruct((8, PAIR, WIDE), BF16),
            pltpu.VMEM((ROWS // 2, SLOTS, 128, 128), BF16),
        ),
        in_specs=[SMEM, SMEM, VMEM, ANY] + [ANY] * 8 + [VMEM] + [ANY] * 5 + [VMEM] * 2,
        out_specs=(VMEM, VMEM),
        scratch_shapes=[
            pltpu.VMEM((PAIR, NODES), BF16),
            pltpu.SemaphoreType.DMA((16,)),
            pltpu.SemaphoreType.DMA((4,)),
        ],
        compiler_params=pltpu.CompilerParams(vmem_limit_bytes=10 << 20),
        cost_estimate=pl.CostEstimate(
            flops=8 * 2 * 1024 * 128 * 128 * 32, bytes_accessed=8 << 20, transcendentals=0
        ),
        name="forward",
    )(info, cols, held, tiles, *own, *others, cot, weight)
    return message, pltpu.with_memory_space_constraint(streamed, pltpu.VMEM)


def dense_kernel(message, out):
    agg = message[:, :512]
    weight = message[:, 1024:]
    pre = lax.dot_general(weight, agg, (((0,), (0,)), ((), ())), preferred_element_type=F32)
    sig = 1.0 / (1.0 + jnp.exp(-pre))
    out[:, 512:1024] = (pre * sig).astype(BF16)
    cot = message[:, 512:1024].astype(F32)
    pre_grad = (cot * sig * (1.0 + pre * (1.0 - sig))).astype(BF16)
    out[:, :512] = jnp.dot(weight, pre_grad, preferred_element_type=F32).astype(BF16)
    wgrad = lax.dot_general(agg, pre_grad, (((1,), (1,)), ((), ())), preferred_element_type=F32)
    out[:, 1024:] = wgrad.astype(BF16)


def dense(message):
    return pl.pallas_call(
        dense_kernel,
        out_shape=jax.ShapeDtypeStruct((256, WIDE), BF16),
        in_specs=[VMEM],
        out_specs=VMEM,
        compiler_params=pltpu.CompilerParams(vmem_limit_bytes=8 << 20),
        cost_estimate=pl.CostEstimate(
            flops=3 * 2 * 256 * 256 * 512, bytes_accessed=2 << 20, transcendentals=256 * 512
        ),
        name="dense",
    )(message)


def backward_kernel(info, cols, low_tiles, high_tiles, grad, *refs):
    outs, wgrad, total = refs[:4], refs[4], refs[5]
    core = info[0]

    def clear(i, carry):
        total[:, pl.ds(pl.multiple_of(i * 2048, 2048), 2048)] = jnp.zeros((PAIR, 2048), F32)
        return carry

    lax.fori_loop(0, NODES // 2048, clear, 0)

    def row(local, tiles):
        r = row_of(core, local)
        g = grad[local // 4, :, lanes_of(lax.rem(local, 4))]
        at = lax.rem(local, 16)
        for first in range(0, SLOTS, 8):
            blocks = [lanes_of(cols[first + i, r]) for i in range(8)]
            terms = []
            for i in range(first, first + 8, 2):
                pair = jnp.concatenate([tiles[at, i], tiles[at, i + 1]], axis=1)
                both = jnp.dot(g, pair, preferred_element_type=F32)
                terms += [both[:, :128], both[:, 128:]]
            sums = [total[:, blocks[i]] + terms[i] for i in range(8)]
            for i in range(8):
                total[:, blocks[i]] = sums[i]

    for half, tiles in enumerate((low_tiles, high_tiles)):

        def step(i, carry, tiles=tiles):
            for k in range(4):
                row(4 * i + k, tiles)
            return carry

        lax.fori_loop(4 * half, 4 * half + 4, step, 0)

    own = pl.ds(pl.multiple_of(HALF * core, HALF), HALF)
    other = pl.ds(pl.multiple_of(HALF * (1 - core), HALF), HALF)
    for phase, group in enumerate(GROUPS):
        for i, d in enumerate(group):
            lanes = pl.ds(pl.multiple_of(info[1 + d] * LOCAL, LOCAL), LOCAL)
            place = slice(LOCAL * i, LOCAL * (i + 1))
            outs[phase][:, place] = total[own, lanes].astype(BF16)
            outs[2 + phase][:, place] = total[other, lanes].astype(BF16)
    for rows, keep in ((own, True), (other, False)):
        terms = grad[0, rows, 1024:].astype(F32)
        for g in range(1, 8):
            terms += grad[g, rows, 1024:].astype(F32)
        if keep:
            wgrad[...] = terms
        else:
            outs[2][:, LOCAL * len(GROUPS[0]) :] = terms.astype(BF16)


def backward(info, cols, held, grad):
    widths = [LOCAL * len(g) for g in GROUPS]
    return pl.pallas_call(
        backward_kernel,
        out_shape=[
            jax.ShapeDtypeStruct((HALF, n), BF16) for n in (*widths, widths[0] + 256, widths[1])
        ]
        + [jax.ShapeDtypeStruct((HALF, 256), F32)],
        in_specs=[SMEM, SMEM, VMEM, VMEM, VMEM],
        out_specs=[VMEM] * 5,
        scratch_shapes=[
            pltpu.VMEM((PAIR, NODES), F32),
        ],
        compiler_params=pltpu.CompilerParams(vmem_limit_bytes=10 << 20),
        cost_estimate=pl.CostEstimate(
            flops=8 * 2 * 1024 * 128 * 128 * 32, bytes_accessed=8 << 20, transcendentals=0
        ),
        name="backward",
    )(info, cols, *held, grad)


def sum_call(kernel, shapes, args, name, before=()):
    def body(*refs):
        kernel(*refs[: len(args)], *refs[len(args) + len(before) :])

    return pl.pallas_call(
        body,
        out_shape=[jax.ShapeDtypeStruct(s, t) for s, t in shapes],
        in_specs=[VMEM] * len(args) + [ANY] * len(before),
        out_specs=[VMEM] * len(shapes),
        compiler_params=pltpu.CompilerParams(vmem_limit_bytes=8 << 20),
        cost_estimate=pl.CostEstimate(flops=0, bytes_accessed=2 << 20, transcendentals=0),
        name=name,
    )(*args, *before)


def far_kernel(own, other, wgrad, *outs):
    terms = wgrad[...] + other[:, 4 * LOCAL :].astype(F32)
    for i, out in enumerate(outs[:4]):
        lanes = slice(LOCAL * i, LOCAL * (i + 1))
        out[:, :LOCAL] = (own[:, lanes].astype(F32) + other[:, lanes].astype(F32)).astype(BF16)
        out[:, LOCAL:] = terms.astype(BF16)
    outs[4][...] = terms


def near_kernel(own, other, wgrad, from_across, from_up, from_down, up, across, down, base):
    def mine(i):
        lanes = slice(LOCAL * i, LOCAL * (i + 1))
        return own[:, lanes].astype(F32) + other[:, lanes].astype(F32)

    for i, (out, received) in enumerate(
        ((up, (from_across, from_down)), (across, (from_up,)), (down, ()), (base, ()))
    ):
        piece, terms = mine(i), wgrad[...]
        for r in received:
            piece += r[:, :LOCAL].astype(F32)
            terms += r[:, LOCAL:].astype(F32)
        out[:, :LOCAL] = piece.astype(out.dtype)
        out[:, LOCAL:] = terms.astype(out.dtype)


def last_kernel(base, *refs):
    *received, feats_grad, weight_grad = refs
    total = base[...]
    for a in received:
        total += a[...].astype(F32)
    feats_grad[...] = total[:, :LOCAL].astype(BF16)
    weight_grad[...] = total[:, LOCAL:]


def per_device(node_feats, weight, tiles, block_cols, cotangent):
    core = lax.axis_index("feat") % 2
    slab = lax.axis_index("blk")
    x, y = slab // 4, slab % 4
    info = jnp.stack([core] + [(x ^ dx) * 4 + (y + dy) % 4 for dx, dy in STEPS]).astype(jnp.int32)
    cols = block_cols.T

    up, down, across, corner = (receive(node_feats, s) for s in (UP, DOWN, ACROSS, CORNER))
    held, token = load_tiles(info, tiles)
    up, across = gate((up, across), (token,))
    far = receive(up, UP)
    across_up = receive(up, ACROSS)
    across_down = receive(across, DOWN)
    near = bundle(node_feats, cotangent, weight, up, across, down, corner, token)
    local, first, second = (swap(n) for n in near)
    pieces = [
        (node_feats, local, 0),
        (up, first, 0),
        (down, second, 0),
        (across, first, LOCAL),
        (far, swap(far), 0),
        (across_up, swap(across_up), 0),
        (across_down, swap(across_down), 0),
        (corner, second, LOCAL),
    ]
    message, streamed = forward(info, cols, held, tiles, pieces, cotangent, weight)
    message = lax.all_to_all(message, "feat", 0, 0, axis_index_groups=SAME_CORE, tiled=True)
    message = dense(message.reshape(256, WIDE)).reshape(8, PAIR, WIDE)
    message = lax.all_to_all(message, "feat", 0, 0, axis_index_groups=SAME_CORE, tiled=True)

    own_a, own_c, other_a, other_c, wgrad = backward(info, cols, (held, streamed), message)
    piece = ((HALF, LOCAL + 256), BF16)
    across_up, across_down, far, corner, wgrad = sum_call(
        far_kernel,
        [piece] * 4 + [((HALF, 256), F32)],
        (own_a, swap(other_a), wgrad),
        "sum_far",
    )
    from_across = send(across_up, ACROSS)
    from_up = send(across_down, DOWN)
    from_down = send(far, UP)
    from_corner = send(corner, CORNER)
    (other_c,) = gate((other_c,), (far,))
    up, across, down, base = sum_call(
        near_kernel,
        [piece] * 3 + [((HALF, LOCAL + 256), F32)],
        (own_c, swap(other_c), wgrad, from_across, from_up, from_down),
        "sum_near",
    )
    hidden, hidden_other = unpack(info, message, far)
    hidden = join(info, hidden, swap(hidden_other), down)
    last = [send(up, UP), send(across, ACROSS), send(down, DOWN)]
    feats_grad, weight_grad = sum_call(
        last_kernel,
        [((HALF, LOCAL), BF16), ((HALF, 256), F32)],
        (base, from_corner, *last),
        "sum_last",
    )
    return hidden, weight_grad, feats_grad


def solution(mesh):
    placed = (
        P("feat", "blk"),
        P("feat", None),
        P("blk", None, None, None),
        P("blk", None),
        P("feat", "blk"),
    )
    return jax.shard_map(
        per_device,
        mesh=mesh,
        in_specs=placed,
        out_specs=(P("feat", "blk"), P("feat", None), P("feat", "blk")),
        check_vma=False,
    )
```

```python
import functools

import jax
import jax.numpy as jnp
from jax import lax
from jax.experimental import pallas as pl
from jax.experimental.pallas import tpu as pltpu
from jax.sharding import PartitionSpec as P

BF16 = jnp.bfloat16
F32 = jnp.float32
ANY = pl.BlockSpec(memory_space=pl.ANY)
VMEM = pl.BlockSpec(memory_space=pltpu.VMEM)
SMEM = pl.BlockSpec(memory_space=pltpu.SMEM)

STEPS = ((0, 0), (0, 1), (0, 3), (1, 0), (0, 2), (1, 1), (1, 3), (1, 2))
UP, DOWN, ACROSS, CORNER = (0, 1), (0, 3), (1, 0), (1, 2)
GROUPS = ((5, 6, 4, 7), (1, 3, 2, 0))
SLABS = 8
HALF = 16
PAIR = 32
LOCAL = 8192
NODES = 65536
SLOTS = 32
ROWS = 32


def _index(x, y):
    return x * 4 + y


def _from_step(step):
    dx, dy = step
    return [(_index(x ^ dx, (y + dy) % 4), _index(x, y)) for x in range(2) for y in range(4)]


def _to_step(step):
    return [(b, a) for a, b in _from_step(step)]


CORE_SWAP = [(f, f ^ 1) for f in range(16)]
SAME_CORE = [list(range(0, 16, 2)), list(range(1, 16, 2))]


def swap(a):
    return lax.ppermute(a, "feat", CORE_SWAP)


def receive(a, step):
    return lax.ppermute(a, "blk", _from_step(step))


def send(a, step):
    return lax.ppermute(a, "blk", _to_step(step))


def row_of(core, local):
    return 8 * (local // 4) + 4 * core + local % 4


def lanes_of(block):
    return pl.ds(pl.multiple_of(block * 128, 128), 128)


def load_kernel(info, tiles, held, token, sems):
    core = info[0]
    copies = []
    for g in range(4):
        copies.append(
            pltpu.make_async_copy(
                tiles.at[pl.ds(8 * g + 4 * core, 4)], held.at[pl.ds(4 * g, 4)], sems.at[g]
            )
        )
    for c in copies:
        c.start()
    token[...] = jnp.zeros_like(token)
    for c in copies:
        c.wait()


def load_tiles(info, tiles):
    held, token = pl.pallas_call(
        load_kernel,
        out_shape=(
            pltpu.VMEM((ROWS // 2, SLOTS, 128, 128), BF16),
            jax.ShapeDtypeStruct((8, 128), F32),
        ),
        in_specs=[SMEM, ANY],
        out_specs=(VMEM, VMEM),
        scratch_shapes=[pltpu.SemaphoreType.DMA((4,))],
        compiler_params=pltpu.CompilerParams(vmem_limit_bytes=2 << 20),
        cost_estimate=pl.CostEstimate(flops=0, bytes_accessed=48 << 20, transcendentals=0),
        name="load_tiles",
    )(info, tiles)
    return pltpu.with_memory_space_constraint(held, pltpu.VMEM), token


def gate(arrays, before):
    n = len(arrays)
    return pl.pallas_call(
        lambda *refs: None,
        out_shape=[jax.ShapeDtypeStruct(a.shape, a.dtype) for a in arrays],
        in_specs=[ANY] * (n + len(before)),
        out_specs=[ANY] * n,
        input_output_aliases={i: i for i in range(n)},
        compiler_params=pltpu.CompilerParams(vmem_limit_bytes=1 << 20),
        cost_estimate=pl.CostEstimate(flops=0, bytes_accessed=1024, transcendentals=0),
        name="gate",
    )(*arrays, *before)


def bundle_kernel(widths, before, *refs):
    parts, outs = refs[: sum(widths)], refs[sum(widths) + before :]
    parts = list(parts)
    for count, out in zip(widths, outs):
        at = 0
        for a in parts[:count]:
            out[:, at : at + a.shape[1]] = a[...]
            at += a.shape[1]
        parts = parts[count:]


def bundle(groups, before=()):
    arrays = [a for g in groups for a in g]
    return pl.pallas_call(
        functools.partial(bundle_kernel, [len(g) for g in groups], len(before)),
        out_shape=[jax.ShapeDtypeStruct((HALF, sum(a.shape[1] for a in g)), BF16) for g in groups],
        in_specs=[VMEM] * len(arrays) + [ANY] * len(before),
        out_specs=[VMEM] * len(groups),
        compiler_params=pltpu.CompilerParams(vmem_limit_bytes=8 << 20),
        cost_estimate=pl.CostEstimate(flops=0, bytes_accessed=2 << 20, transcendentals=0),
        name="bundle",
    )(*arrays, *before)


WIDE = 1280


def unpack_kernel(info, message, before, mine, other):
    core = info[0]
    own = pl.ds(pl.multiple_of(HALF * core, HALF), HALF)
    sibling = pl.ds(pl.multiple_of(HALF * (1 - core), HALF), HALF)
    for rows, nodes in ((own, mine), (sibling, other)):
        for g in range(8):
            nodes[:, 512 * g : 512 * (g + 1)] = message[g, rows, 512:1024]


def unpack(info, message, before):
    return pl.pallas_call(
        unpack_kernel,
        out_shape=[jax.ShapeDtypeStruct((HALF, 4096), BF16)] * 2,
        in_specs=[SMEM, VMEM, ANY],
        out_specs=[VMEM] * 2,
        compiler_params=pltpu.CompilerParams(vmem_limit_bytes=4 << 20),
        cost_estimate=pl.CostEstimate(flops=0, bytes_accessed=1 << 20, transcendentals=0),
        name="unpack",
    )(info, message, before)


def join_kernel(info, mine, received, before, hidden):
    core = info[0]
    for g in range(8):
        chunk = slice(512 * g, 512 * (g + 1))
        a, b = mine[:, chunk], received[:, chunk]
        hidden[:, 1024 * g : 1024 * g + 512] = jnp.where(core == 0, a, b)
        hidden[:, 1024 * g + 512 : 1024 * (g + 1)] = jnp.where(core == 0, b, a)


def join(info, mine, received, before):
    return pl.pallas_call(
        join_kernel,
        out_shape=jax.ShapeDtypeStruct((HALF, LOCAL), BF16),
        in_specs=[SMEM, VMEM, VMEM, ANY],
        out_specs=VMEM,
        compiler_params=pltpu.CompilerParams(vmem_limit_bytes=4 << 20),
        cost_estimate=pl.CostEstimate(flops=0, bytes_accessed=1 << 20, transcendentals=0),
        name="join",
    )(info, mine, received, before)


def forward_kernel(places, info, cols, low_tiles, tiles, *refs):
    own, others, cot, weight = refs[:8], refs[8:14], refs[14], refs[15]
    out, high_tiles, feats, sems, stream_sems = refs[16:]
    core = info[0]
    mine = pl.ds(pl.multiple_of(HALF * core, HALF), HALF)
    sibling = pl.ds(pl.multiple_of(HALF * (1 - core), HALF), HALF)
    copies = []
    for i, (which, first) in enumerate(places):
        at = pl.ds(pl.multiple_of(info[1 + i] * LOCAL, LOCAL), LOCAL)
        other = others[which].at[:, pl.ds(first, LOCAL)]
        copies += [
            pltpu.make_async_copy(own[i], feats.at[mine, at], sems.at[2 * i]),
            pltpu.make_async_copy(other, feats.at[sibling, at], sems.at[2 * i + 1]),
        ]
    stream = [
        pltpu.make_async_copy(
            tiles.at[pl.ds(8 * (4 + g) + 4 * core, 4)],
            high_tiles.at[pl.ds(4 * g, 4)],
            stream_sems.at[g],
        )
        for g in range(4)
    ]
    for c in copies + stream:
        c.start()
    local = others[0]
    for g in range(8):
        at = 1024 * g + 512 * core
        out[g, mine, 512:1024] = cot[:, pl.ds(pl.multiple_of(at, 512), 512)]
        out[g, mine, 1024:] = weight[...]
        at = LOCAL + at
        out[g, sibling, 512:1024] = local[:, pl.ds(pl.multiple_of(at, 512), 512)]
        out[g, sibling, 1024:] = local[:, 2 * LOCAL :]
    for c in copies:
        c.wait()

    def four_rows(first, tiles, sums):
        rows = [row_of(core, first + k) for k in range(4)]

        def push(unit, p, register):
            right = [
                jnp.concatenate([tiles[lax.rem(first, 16) + k, p + e] for e in range(2)], axis=1)
                for k in (2 * unit, 2 * unit + 1)
            ]
            pltpu.matmul_push_rhs(
                jnp.concatenate(right, axis=0), register, unit, transpose=True
            )

        def multiply(unit, p, register):
            left = [
                jnp.concatenate([feats[:, lanes_of(cols[p + e, r])] for e in range(2)], axis=1)
                for r in rows[2 * unit : 2 * unit + 2]
            ]
            pltpu.matmul_acc_lhs(
                sums[unit], jnp.concatenate(left, axis=0), load_staged_rhs=register
            )

        for unit in range(2):
            push(unit, 0, 0)
        for p in range(0, SLOTS, 2):
            if p + 2 < SLOTS:
                for unit in range(2):
                    push(unit, p + 2, (p // 2 + 1) % 2)
            for unit in range(2):
                multiply(unit, p, (p // 2) % 2)
        for unit in range(2):
            got = pltpu.matmul_pop(sums[unit])
            for k in range(2):
                value = got[PAIR * k : PAIR * (k + 1), 128 * k : 128 * (k + 1)]
                j = 2 * unit + k
                out[first // 4, :, 128 * j : 128 * (j + 1)] = value.astype(BF16)

    for half, tiles in enumerate((low_tiles, high_tiles)):

        def step(i, carry, tiles=tiles):
            pl.run_scoped(
                lambda *sums: four_rows(4 * i, tiles, sums),
                *[pltpu.ACC(unit)((2 * PAIR, 256), F32) for unit in range(2)],
            )
            return carry

        if half:
            for c in stream:
                c.wait()
        lax.fori_loop(4 * half, 4 * half + 4, step, 0)


def forward(info, cols, held, tiles, pieces, cot, weight):
    own = [p[0] for p in pieces]
    others = []
    for _, other, _ in pieces:
        if not any(other is o for o in others):
            others.append(other)
    places = tuple((next(k for k, o in enumerate(others) if o is p[1]), p[2]) for p in pieces)
    message, streamed = pl.pallas_call(
        functools.partial(forward_kernel, places),
        out_shape=(
            jax.ShapeDtypeStruct((8, PAIR, WIDE), BF16),
            pltpu.VMEM((ROWS // 2, SLOTS, 128, 128), BF16),
        ),
        in_specs=[SMEM, SMEM, VMEM, ANY] + [ANY] * 8 + [VMEM] + [ANY] * 5 + [VMEM] * 2,
        out_specs=(VMEM, VMEM),
        scratch_shapes=[
            pltpu.VMEM((PAIR, NODES), BF16),
            pltpu.SemaphoreType.DMA((16,)),
            pltpu.SemaphoreType.DMA((4,)),
        ],
        compiler_params=pltpu.CompilerParams(vmem_limit_bytes=10 << 20),
        cost_estimate=pl.CostEstimate(
            flops=8 * 2 * 1024 * 128 * 128 * 32, bytes_accessed=8 << 20, transcendentals=0
        ),
        name="forward",
    )(info, cols, held, tiles, *own, *others, cot, weight)
    return message, pltpu.with_memory_space_constraint(streamed, pltpu.VMEM)


def dense_kernel(message, out):
    agg = message[:, :512]
    weight = message[:, 1024:]
    pre = lax.dot_general(weight, agg, (((0,), (0,)), ((), ())), preferred_element_type=F32)
    sig = 1.0 / (1.0 + jnp.exp(-pre))
    out[:, 512:1024] = (pre * sig).astype(BF16)
    cot = message[:, 512:1024].astype(F32)
    pre_grad = (cot * sig * (1.0 + pre * (1.0 - sig))).astype(BF16)
    out[:, :512] = jnp.dot(weight, pre_grad, preferred_element_type=F32).astype(BF16)
    wgrad = lax.dot_general(agg, pre_grad, (((1,), (1,)), ((), ())), preferred_element_type=F32)
    out[:, 1024:] = wgrad.astype(BF16)


def dense(message):
    return pl.pallas_call(
        dense_kernel,
        out_shape=jax.ShapeDtypeStruct((256, WIDE), BF16),
        in_specs=[VMEM],
        out_specs=VMEM,
        compiler_params=pltpu.CompilerParams(vmem_limit_bytes=8 << 20),
        cost_estimate=pl.CostEstimate(
            flops=3 * 2 * 256 * 256 * 512, bytes_accessed=2 << 20, transcendentals=256 * 512
        ),
        name="dense",
    )(message)


def backward_kernel(info, cols, low_tiles, high_tiles, grad, *refs):
    outs, wgrad, total = refs[:4], refs[4], refs[5]
    core = info[0]

    def clear(i, carry):
        total[:, pl.ds(pl.multiple_of(i * 2048, 2048), 2048)] = jnp.zeros((PAIR, 2048), F32)
        return carry

    lax.fori_loop(0, NODES // 2048, clear, 0)

    def row(local, tiles):
        r = row_of(core, local)
        g = grad[local // 4, :, lanes_of(lax.rem(local, 4))]
        at = lax.rem(local, 16)
        for first in range(0, SLOTS, 8):
            blocks = [lanes_of(cols[first + i, r]) for i in range(8)]
            terms = []
            for i in range(first, first + 8, 2):
                pair = jnp.concatenate([tiles[at, i], tiles[at, i + 1]], axis=1)
                both = jnp.dot(g, pair, preferred_element_type=F32)
                terms += [both[:, :128], both[:, 128:]]
            sums = [total[:, blocks[i]] + terms[i] for i in range(8)]
            for i in range(8):
                total[:, blocks[i]] = sums[i]

    for half, tiles in enumerate((low_tiles, high_tiles)):

        def step(i, carry, tiles=tiles):
            for k in range(4):
                row(4 * i + k, tiles)
            return carry

        lax.fori_loop(4 * half, 4 * half + 4, step, 0)

    own = pl.ds(pl.multiple_of(HALF * core, HALF), HALF)
    other = pl.ds(pl.multiple_of(HALF * (1 - core), HALF), HALF)
    for phase, group in enumerate(GROUPS):
        for i, d in enumerate(group):
            lanes = pl.ds(pl.multiple_of(info[1 + d] * LOCAL, LOCAL), LOCAL)
            place = slice(LOCAL * i, LOCAL * (i + 1))
            outs[phase][:, place] = total[own, lanes].astype(BF16)
            outs[2 + phase][:, place] = total[other, lanes].astype(BF16)
    for rows, keep in ((own, True), (other, False)):
        terms = grad[0, rows, 1024:].astype(F32)
        for g in range(1, 8):
            terms += grad[g, rows, 1024:].astype(F32)
        if keep:
            wgrad[...] = terms
        else:
            outs[2][:, LOCAL * len(GROUPS[0]) :] = terms.astype(BF16)


def backward(info, cols, held, grad):
    widths = [LOCAL * len(g) for g in GROUPS]
    return pl.pallas_call(
        backward_kernel,
        out_shape=[
            jax.ShapeDtypeStruct((HALF, n), BF16) for n in (*widths, widths[0] + 256, widths[1])
        ]
        + [jax.ShapeDtypeStruct((HALF, 256), F32)],
        in_specs=[SMEM, SMEM, VMEM, VMEM, VMEM],
        out_specs=[VMEM] * 5,
        scratch_shapes=[
            pltpu.VMEM((PAIR, NODES), F32),
        ],
        compiler_params=pltpu.CompilerParams(vmem_limit_bytes=10 << 20),
        cost_estimate=pl.CostEstimate(
            flops=8 * 2 * 1024 * 128 * 128 * 32, bytes_accessed=8 << 20, transcendentals=0
        ),
        name="backward",
    )(info, cols, *held, grad)


def sum_call(kernel, shapes, args, name, before=()):
    def body(*refs):
        kernel(*refs[: len(args)], *refs[len(args) + len(before) :])

    return pl.pallas_call(
        body,
        out_shape=[jax.ShapeDtypeStruct(s, t) for s, t in shapes],
        in_specs=[VMEM] * len(args) + [ANY] * len(before),
        out_specs=[VMEM] * len(shapes),
        compiler_params=pltpu.CompilerParams(vmem_limit_bytes=8 << 20),
        cost_estimate=pl.CostEstimate(flops=0, bytes_accessed=2 << 20, transcendentals=0),
        name=name,
    )(*args, *before)


def far_kernel(own, other, wgrad, *outs):
    terms = wgrad[...] + other[:, 4 * LOCAL :].astype(F32)
    for i, out in enumerate(outs[:4]):
        lanes = slice(LOCAL * i, LOCAL * (i + 1))
        out[:, :LOCAL] = (own[:, lanes].astype(F32) + other[:, lanes].astype(F32)).astype(BF16)
        out[:, LOCAL:] = terms.astype(BF16)
    outs[4][...] = terms


def near_kernel(own, other, wgrad, from_across, from_up, from_down, up, across, down, base):
    def mine(i):
        lanes = slice(LOCAL * i, LOCAL * (i + 1))
        return own[:, lanes].astype(F32) + other[:, lanes].astype(F32)

    for i, (out, received) in enumerate(
        ((up, (from_across, from_down)), (across, (from_up,)), (down, ()), (base, ()))
    ):
        piece, terms = mine(i), wgrad[...]
        for r in received:
            piece += r[:, :LOCAL].astype(F32)
            terms += r[:, LOCAL:].astype(F32)
        out[:, :LOCAL] = piece.astype(out.dtype)
        out[:, LOCAL:] = terms.astype(out.dtype)


def last_kernel(base, *refs):
    *received, feats_grad, weight_grad = refs
    total = base[...]
    for a in received:
        total += a[...].astype(F32)
    feats_grad[...] = total[:, :LOCAL].astype(BF16)
    weight_grad[...] = total[:, LOCAL:]


def per_device(node_feats, weight, tiles, block_cols, cotangent):
    core = lax.axis_index("feat") % 2
    slab = lax.axis_index("blk")
    x, y = slab // 4, slab % 4
    info = jnp.stack([core] + [(x ^ dx) * 4 + (y + dy) % 4 for dx, dy in STEPS]).astype(jnp.int32)
    cols = block_cols.T

    up, down, across, corner = (receive(node_feats, s) for s in (UP, DOWN, ACROSS, CORNER))
    held, token = load_tiles(info, tiles)
    (local,) = bundle(((node_feats, cotangent, weight),), (token,))
    local = swap(local)
    up, across = gate((up, across), (token, local))
    far = receive(up, UP)
    across_up = receive(up, ACROSS)
    across_down = receive(across, DOWN)
    first, second = bundle(((up, across), (down, corner)))
    first, second = swap(first), swap(second)
    pieces = [
        (node_feats, local, 0),
        (up, first, 0),
        (down, second, 0),
        (across, first, LOCAL),
        (far, swap(far), 0),
        (across_up, swap(across_up), 0),
        (across_down, swap(across_down), 0),
        (corner, second, LOCAL),
    ]
    message, streamed = forward(info, cols, held, tiles, pieces, cotangent, weight)
    message = lax.all_to_all(message, "feat", 0, 0, axis_index_groups=SAME_CORE, tiled=True)
    message = dense(message.reshape(256, WIDE)).reshape(8, PAIR, WIDE)
    message = lax.all_to_all(message, "feat", 0, 0, axis_index_groups=SAME_CORE, tiled=True)

    own_a, own_c, other_a, other_c, wgrad = backward(info, cols, (held, streamed), message)
    piece = ((HALF, LOCAL + 256), BF16)
    across_up, across_down, far, corner, wgrad = sum_call(
        far_kernel,
        [piece] * 4 + [((HALF, 256), F32)],
        (own_a, swap(other_a), wgrad),
        "sum_far",
    )
    from_across = send(across_up, ACROSS)
    from_up = send(across_down, DOWN)
    from_down = send(far, UP)
    from_corner = send(corner, CORNER)
    (other_c,) = gate((other_c,), (far,))
    up, across, down, base = sum_call(
        near_kernel,
        [piece] * 3 + [((HALF, LOCAL + 256), F32)],
        (own_c, swap(other_c), wgrad, from_across, from_up, from_down),
        "sum_near",
    )
    hidden, hidden_other = unpack(info, message, far)
    hidden = join(info, hidden, swap(hidden_other), down)
    last = [send(up, UP), send(across, ACROSS), send(down, DOWN)]
    feats_grad, weight_grad = sum_call(
        last_kernel,
        [((HALF, LOCAL), BF16), ((HALF, 256), F32)],
        (base, from_corner, *last),
        "sum_last",
    )
    return hidden, weight_grad, feats_grad


def solution(mesh):
    placed = (
        P("feat", "blk"),
        P("feat", None),
        P("blk", None, None, None),
        P("blk", None),
        P("feat", "blk"),
    )
    return jax.shard_map(
        per_device,
        mesh=mesh,
        in_specs=placed,
        out_specs=(P("feat", "blk"), P("feat", None), P("feat", "blk")),
        check_vma=False,
    )
```

```python
import functools

import jax
import jax.numpy as jnp
from jax import lax
from jax.experimental import pallas as pl
from jax.experimental.pallas import tpu as pltpu
from jax.sharding import PartitionSpec as P

BF16 = jnp.bfloat16
F32 = jnp.float32
ANY = pl.BlockSpec(memory_space=pl.ANY)
VMEM = pl.BlockSpec(memory_space=pltpu.VMEM)
SMEM = pl.BlockSpec(memory_space=pltpu.SMEM)

STEPS = ((0, 0), (0, 1), (0, 3), (1, 0), (0, 2), (1, 1), (1, 3), (1, 2))
UP, DOWN, ACROSS, CORNER = (0, 1), (0, 3), (1, 0), (1, 2)
GROUPS = ((5, 6, 4, 7), (1, 3, 2, 0))
SLABS = 8
HALF = 16
PAIR = 32
LOCAL = 8192
NODES = 65536
SLOTS = 32
ROWS = 32


def _index(x, y):
    return x * 4 + y


def _from_step(step):
    dx, dy = step
    return [(_index(x ^ dx, (y + dy) % 4), _index(x, y)) for x in range(2) for y in range(4)]


def _to_step(step):
    return [(b, a) for a, b in _from_step(step)]


CORE_SWAP = [(f, f ^ 1) for f in range(16)]
SAME_CORE = [list(range(0, 16, 2)), list(range(1, 16, 2))]


def swap(a):
    return lax.ppermute(a, "feat", CORE_SWAP)


def receive(a, step):
    return lax.ppermute(a, "blk", _from_step(step))


def send(a, step):
    return lax.ppermute(a, "blk", _to_step(step))


def row_of(core, local):
    return 8 * (local // 4) + 4 * core + local % 4


def lanes_of(block):
    return pl.ds(pl.multiple_of(block * 128, 128), 128)


def load_kernel(info, tiles, held, token, sems):
    core = info[0]
    copies = []
    for g in range(4):
        copies.append(
            pltpu.make_async_copy(
                tiles.at[pl.ds(8 * g + 4 * core, 4)], held.at[pl.ds(4 * g, 4)], sems.at[g]
            )
        )
    for c in copies:
        c.start()
    token[...] = jnp.zeros_like(token)
    for c in copies:
        c.wait()


def load_tiles(info, tiles):
    held, token = pl.pallas_call(
        load_kernel,
        out_shape=(
            pltpu.VMEM((ROWS // 2, SLOTS, 128, 128), BF16),
            jax.ShapeDtypeStruct((8, 128), F32),
        ),
        in_specs=[SMEM, ANY],
        out_specs=(VMEM, VMEM),
        scratch_shapes=[pltpu.SemaphoreType.DMA((4,))],
        compiler_params=pltpu.CompilerParams(vmem_limit_bytes=2 << 20),
        cost_estimate=pl.CostEstimate(flops=0, bytes_accessed=48 << 20, transcendentals=0),
        name="load_tiles",
    )(info, tiles)
    return pltpu.with_memory_space_constraint(held, pltpu.VMEM), token


def gate(arrays, before):
    n = len(arrays)
    return pl.pallas_call(
        lambda *refs: None,
        out_shape=[jax.ShapeDtypeStruct(a.shape, a.dtype) for a in arrays],
        in_specs=[ANY] * (n + len(before)),
        out_specs=[ANY] * n,
        input_output_aliases={i: i for i in range(n)},
        compiler_params=pltpu.CompilerParams(vmem_limit_bytes=1 << 20),
        cost_estimate=pl.CostEstimate(flops=0, bytes_accessed=1024, transcendentals=0),
        name="gate",
    )(*arrays, *before)


def bundle_kernel(widths, before, *refs):
    parts, outs = refs[: sum(widths)], refs[sum(widths) + before :]
    parts = list(parts)
    for count, out in zip(widths, outs):
        at = 0
        for a in parts[:count]:
            out[:, at : at + a.shape[1]] = a[...]
            at += a.shape[1]
        parts = parts[count:]


def bundle(groups, before=()):
    arrays = [a for g in groups for a in g]
    return pl.pallas_call(
        functools.partial(bundle_kernel, [len(g) for g in groups], len(before)),
        out_shape=[jax.ShapeDtypeStruct((HALF, sum(a.shape[1] for a in g)), BF16) for g in groups],
        in_specs=[VMEM] * len(arrays) + [ANY] * len(before),
        out_specs=[VMEM] * len(groups),
        compiler_params=pltpu.CompilerParams(vmem_limit_bytes=8 << 20),
        cost_estimate=pl.CostEstimate(flops=0, bytes_accessed=2 << 20, transcendentals=0),
        name="bundle",
    )(*arrays, *before)


WIDE = 1280


def unpack_kernel(info, message, before, mine, other):
    core = info[0]
    own = pl.ds(pl.multiple_of(HALF * core, HALF), HALF)
    sibling = pl.ds(pl.multiple_of(HALF * (1 - core), HALF), HALF)
    for rows, nodes in ((own, mine), (sibling, other)):
        for g in range(8):
            nodes[:, 512 * g : 512 * (g + 1)] = message[g, rows, 512:1024]


def unpack(info, message, before):
    return pl.pallas_call(
        unpack_kernel,
        out_shape=[jax.ShapeDtypeStruct((HALF, 4096), BF16)] * 2,
        in_specs=[SMEM, VMEM, ANY],
        out_specs=[VMEM] * 2,
        compiler_params=pltpu.CompilerParams(vmem_limit_bytes=4 << 20),
        cost_estimate=pl.CostEstimate(flops=0, bytes_accessed=1 << 20, transcendentals=0),
        name="unpack",
    )(info, message, before)


def join_kernel(info, mine, received, before, hidden):
    core = info[0]
    for g in range(8):
        chunk = slice(512 * g, 512 * (g + 1))
        a, b = mine[:, chunk], received[:, chunk]
        hidden[:, 1024 * g : 1024 * g + 512] = jnp.where(core == 0, a, b)
        hidden[:, 1024 * g + 512 : 1024 * (g + 1)] = jnp.where(core == 0, b, a)


def join(info, mine, received, before):
    return pl.pallas_call(
        join_kernel,
        out_shape=jax.ShapeDtypeStruct((HALF, LOCAL), BF16),
        in_specs=[SMEM, VMEM, VMEM, ANY],
        out_specs=VMEM,
        compiler_params=pltpu.CompilerParams(vmem_limit_bytes=4 << 20),
        cost_estimate=pl.CostEstimate(flops=0, bytes_accessed=1 << 20, transcendentals=0),
        name="join",
    )(info, mine, received, before)


def forward_kernel(places, info, cols, low_tiles, tiles, *refs):
    own, others, (cot, weight, sides) = refs[:8], refs[8:14], refs[14:17]
    out, high_tiles, feats, sems, stream_sems = refs[17:]
    core = info[0]
    mine = pl.ds(pl.multiple_of(HALF * core, HALF), HALF)
    sibling = pl.ds(pl.multiple_of(HALF * (1 - core), HALF), HALF)
    copies = []
    for i, (which, first) in enumerate(places):
        at = pl.ds(pl.multiple_of(info[1 + i] * LOCAL, LOCAL), LOCAL)
        other = others[which].at[:, pl.ds(first, LOCAL)]
        copies += [
            pltpu.make_async_copy(own[i], feats.at[mine, at], sems.at[2 * i]),
            pltpu.make_async_copy(other, feats.at[sibling, at], sems.at[2 * i + 1]),
        ]
    stream = [
        pltpu.make_async_copy(
            tiles.at[pl.ds(8 * (4 + g) + 4 * core, 4)],
            high_tiles.at[pl.ds(4 * g, 4)],
            stream_sems.at[g],
        )
        for g in range(4)
    ]
    for c in copies + stream:
        c.start()
    for g in range(8):
        at = 1024 * g + 512 * core
        out[g, mine, 512:1024] = cot[:, pl.ds(pl.multiple_of(at, 512), 512)]
        out[g, mine, 1024:] = weight[...]
        out[g, sibling, 512:1024] = sides[:, pl.ds(pl.multiple_of(at, 512), 512)]
        out[g, sibling, 1024:] = sides[:, LOCAL:]
    for c in copies:
        c.wait()

    def four_rows(first, tiles, sums):
        rows = [row_of(core, first + k) for k in range(4)]

        def push(unit, p, register):
            right = [
                jnp.concatenate([tiles[lax.rem(first, 16) + k, p + e] for e in range(2)], axis=1)
                for k in (2 * unit, 2 * unit + 1)
            ]
            pltpu.matmul_push_rhs(
                jnp.concatenate(right, axis=0), register, unit, transpose=True
            )

        def multiply(unit, p, register):
            left = [
                jnp.concatenate([feats[:, lanes_of(cols[p + e, r])] for e in range(2)], axis=1)
                for r in rows[2 * unit : 2 * unit + 2]
            ]
            pltpu.matmul_acc_lhs(
                sums[unit], jnp.concatenate(left, axis=0), load_staged_rhs=register
            )

        for unit in range(2):
            push(unit, 0, 0)
        for p in range(0, SLOTS, 2):
            if p + 2 < SLOTS:
                for unit in range(2):
                    push(unit, p + 2, (p // 2 + 1) % 2)
            for unit in range(2):
                multiply(unit, p, (p // 2) % 2)
        for unit in range(2):
            got = pltpu.matmul_pop(sums[unit])
            for k in range(2):
                value = got[PAIR * k : PAIR * (k + 1), 128 * k : 128 * (k + 1)]
                j = 2 * unit + k
                out[first // 4, :, 128 * j : 128 * (j + 1)] = value.astype(BF16)

    for half, tiles in enumerate((low_tiles, high_tiles)):

        def step(i, carry, tiles=tiles):
            pl.run_scoped(
                lambda *sums: four_rows(4 * i, tiles, sums),
                *[pltpu.ACC(unit)((2 * PAIR, 256), F32) for unit in range(2)],
            )
            return carry

        if half:
            for c in stream:
                c.wait()
        lax.fori_loop(4 * half, 4 * half + 4, step, 0)


def forward(info, cols, held, tiles, pieces, sides):
    own = [p[0] for p in pieces]
    others = []
    for _, other, _ in pieces:
        if not any(other is o for o in others):
            others.append(other)
    places = tuple((next(k for k, o in enumerate(others) if o is p[1]), p[2]) for p in pieces)
    message, streamed = pl.pallas_call(
        functools.partial(forward_kernel, places),
        out_shape=(
            jax.ShapeDtypeStruct((8, PAIR, WIDE), BF16),
            pltpu.VMEM((ROWS // 2, SLOTS, 128, 128), BF16),
        ),
        in_specs=[SMEM, SMEM, VMEM, ANY] + [ANY] * 14 + [VMEM] * 3,
        out_specs=(VMEM, VMEM),
        scratch_shapes=[
            pltpu.VMEM((PAIR, NODES), BF16),
            pltpu.SemaphoreType.DMA((16,)),
            pltpu.SemaphoreType.DMA((4,)),
        ],
        compiler_params=pltpu.CompilerParams(vmem_limit_bytes=10 << 20),
        cost_estimate=pl.CostEstimate(
            flops=8 * 2 * 1024 * 128 * 128 * 32, bytes_accessed=8 << 20, transcendentals=0
        ),
        name="forward",
    )(info, cols, held, tiles, *own, *others, *sides)
    return message, pltpu.with_memory_space_constraint(streamed, pltpu.VMEM)


def dense_kernel(message, out):
    agg = message[:, :512]
    weight = message[:, 1024:]
    pre = lax.dot_general(weight, agg, (((0,), (0,)), ((), ())), preferred_element_type=F32)
    sig = 1.0 / (1.0 + jnp.exp(-pre))
    out[:, 512:1024] = (pre * sig).astype(BF16)
    cot = message[:, 512:1024].astype(F32)
    pre_grad = (cot * sig * (1.0 + pre * (1.0 - sig))).astype(BF16)
    out[:, :512] = jnp.dot(weight, pre_grad, preferred_element_type=F32).astype(BF16)
    wgrad = lax.dot_general(agg, pre_grad, (((1,), (1,)), ((), ())), preferred_element_type=F32)
    out[:, 1024:] = wgrad.astype(BF16)


def dense(message):
    return pl.pallas_call(
        dense_kernel,
        out_shape=jax.ShapeDtypeStruct((256, WIDE), BF16),
        in_specs=[VMEM],
        out_specs=VMEM,
        compiler_params=pltpu.CompilerParams(vmem_limit_bytes=8 << 20),
        cost_estimate=pl.CostEstimate(
            flops=3 * 2 * 256 * 256 * 512, bytes_accessed=2 << 20, transcendentals=256 * 512
        ),
        name="dense",
    )(message)


def backward_kernel(info, cols, low_tiles, high_tiles, grad, *refs):
    outs, wgrad, total = refs[:4], refs[4], refs[5]
    core = info[0]

    def clear(i, carry):
        total[:, pl.ds(pl.multiple_of(i * 2048, 2048), 2048)] = jnp.zeros((PAIR, 2048), F32)
        return carry

    lax.fori_loop(0, NODES // 2048, clear, 0)

    def row(local, tiles):
        r = row_of(core, local)
        g = grad[local // 4, :, lanes_of(lax.rem(local, 4))]
        at = lax.rem(local, 16)
        for first in range(0, SLOTS, 8):
            blocks = [lanes_of(cols[first + i, r]) for i in range(8)]
            terms = []
            for i in range(first, first + 8, 2):
                pair = jnp.concatenate([tiles[at, i], tiles[at, i + 1]], axis=1)
                both = jnp.dot(g, pair, preferred_element_type=F32)
                terms += [both[:, :128], both[:, 128:]]
            sums = [total[:, blocks[i]] + terms[i] for i in range(8)]
            for i in range(8):
                total[:, blocks[i]] = sums[i]

    for half, tiles in enumerate((low_tiles, high_tiles)):

        def step(i, carry, tiles=tiles):
            for k in range(4):
                row(4 * i + k, tiles)
            return carry

        lax.fori_loop(4 * half, 4 * half + 4, step, 0)

    own = pl.ds(pl.multiple_of(HALF * core, HALF), HALF)
    other = pl.ds(pl.multiple_of(HALF * (1 - core), HALF), HALF)
    for phase, group in enumerate(GROUPS):
        for i, d in enumerate(group):
            lanes = pl.ds(pl.multiple_of(info[1 + d] * LOCAL, LOCAL), LOCAL)
            place = slice(LOCAL * i, LOCAL * (i + 1))
            outs[phase][:, place] = total[own, lanes].astype(BF16)
            outs[2 + phase][:, place] = total[other, lanes].astype(BF16)
    for rows, keep in ((own, True), (other, False)):
        terms = grad[0, rows, 1024:].astype(F32)
        for g in range(1, 8):
            terms += grad[g, rows, 1024:].astype(F32)
        if keep:
            wgrad[...] = terms
        else:
            outs[2][:, LOCAL * len(GROUPS[0]) :] = terms.astype(BF16)


def backward(info, cols, held, grad):
    widths = [LOCAL * len(g) for g in GROUPS]
    return pl.pallas_call(
        backward_kernel,
        out_shape=[
            jax.ShapeDtypeStruct((HALF, n), BF16) for n in (*widths, widths[0] + 256, widths[1])
        ]
        + [jax.ShapeDtypeStruct((HALF, 256), F32)],
        in_specs=[SMEM, SMEM, VMEM, VMEM, VMEM],
        out_specs=[VMEM] * 5,
        scratch_shapes=[
            pltpu.VMEM((PAIR, NODES), F32),
        ],
        compiler_params=pltpu.CompilerParams(vmem_limit_bytes=10 << 20),
        cost_estimate=pl.CostEstimate(
            flops=8 * 2 * 1024 * 128 * 128 * 32, bytes_accessed=8 << 20, transcendentals=0
        ),
        name="backward",
    )(info, cols, *held, grad)


def sum_call(kernel, shapes, args, name, before=()):
    def body(*refs):
        kernel(*refs[: len(args)], *refs[len(args) + len(before) :])

    return pl.pallas_call(
        body,
        out_shape=[jax.ShapeDtypeStruct(s, t) for s, t in shapes],
        in_specs=[VMEM] * len(args) + [ANY] * len(before),
        out_specs=[VMEM] * len(shapes),
        compiler_params=pltpu.CompilerParams(vmem_limit_bytes=8 << 20),
        cost_estimate=pl.CostEstimate(flops=0, bytes_accessed=2 << 20, transcendentals=0),
        name=name,
    )(*args, *before)


def far_kernel(own, other, wgrad, *outs):
    terms = wgrad[...] + other[:, 4 * LOCAL :].astype(F32)
    for i, out in enumerate(outs[:4]):
        lanes = slice(LOCAL * i, LOCAL * (i + 1))
        out[:, :LOCAL] = (own[:, lanes].astype(F32) + other[:, lanes].astype(F32)).astype(BF16)
        out[:, LOCAL:] = terms.astype(BF16)
    outs[4][...] = terms


def near_kernel(own, other, wgrad, from_across, from_up, from_down, up, across, down, base):
    def mine(i):
        lanes = slice(LOCAL * i, LOCAL * (i + 1))
        return own[:, lanes].astype(F32) + other[:, lanes].astype(F32)

    for i, (out, received) in enumerate(
        ((up, (from_across, from_down)), (across, (from_up,)), (down, ()), (base, ()))
    ):
        piece, terms = mine(i), wgrad[...]
        for r in received:
            piece += r[:, :LOCAL].astype(F32)
            terms += r[:, LOCAL:].astype(F32)
        out[:, :LOCAL] = piece.astype(out.dtype)
        out[:, LOCAL:] = terms.astype(out.dtype)


def last_kernel(base, *refs):
    *received, feats_grad, weight_grad = refs
    total = base[...]
    for a in received:
        total += a[...].astype(F32)
    feats_grad[...] = total[:, :LOCAL].astype(BF16)
    weight_grad[...] = total[:, LOCAL:]


def per_device(node_feats, weight, tiles, block_cols, cotangent):
    core = lax.axis_index("feat") % 2
    slab = lax.axis_index("blk")
    x, y = slab // 4, slab % 4
    info = jnp.stack([core] + [(x ^ dx) * 4 + (y + dy) % 4 for dx, dy in STEPS]).astype(jnp.int32)
    cols = block_cols.T

    up, down, across, corner = (receive(node_feats, s) for s in (UP, DOWN, ACROSS, CORNER))
    held, token = load_tiles(info, tiles)
    local = swap(node_feats)
    up, across = gate((up, across), (token, local))
    far = receive(up, UP)
    across_up = receive(up, ACROSS)
    across_down = receive(across, DOWN)
    first, second = bundle(((up, across), (down, corner)))
    first, second = swap(first), swap(second)
    (sides,) = bundle(((cotangent, weight),), (far,))
    sides = swap(sides)
    pieces = [
        (node_feats, local, 0),
        (up, first, 0),
        (down, second, 0),
        (across, first, LOCAL),
        (far, swap(far), 0),
        (across_up, swap(across_up), 0),
        (across_down, swap(across_down), 0),
        (corner, second, LOCAL),
    ]
    message, streamed = forward(
        info, cols, held, tiles, pieces, (cotangent, weight, sides)
    )
    message = lax.all_to_all(message, "feat", 0, 0, axis_index_groups=SAME_CORE, tiled=True)
    message = dense(message.reshape(256, WIDE)).reshape(8, PAIR, WIDE)
    message = lax.all_to_all(message, "feat", 0, 0, axis_index_groups=SAME_CORE, tiled=True)

    own_a, own_c, other_a, other_c, wgrad = backward(info, cols, (held, streamed), message)
    piece = ((HALF, LOCAL + 256), BF16)
    across_up, across_down, far, corner, wgrad = sum_call(
        far_kernel,
        [piece] * 4 + [((HALF, 256), F32)],
        (own_a, swap(other_a), wgrad),
        "sum_far",
    )
    from_across = send(across_up, ACROSS)
    from_up = send(across_down, DOWN)
    from_down = send(far, UP)
    from_corner = send(corner, CORNER)
    (other_c,) = gate((other_c,), (far,))
    up, across, down, base = sum_call(
        near_kernel,
        [piece] * 3 + [((HALF, LOCAL + 256), F32)],
        (own_c, swap(other_c), wgrad, from_across, from_up, from_down),
        "sum_near",
    )
    hidden, hidden_other = unpack(info, message, far)
    hidden = join(info, hidden, swap(hidden_other), down)
    last = [send(up, UP), send(across, ACROSS), send(down, DOWN)]
    feats_grad, weight_grad = sum_call(
        last_kernel,
        [((HALF, LOCAL), BF16), ((HALF, 256), F32)],
        (base, from_corner, *last),
        "sum_last",
    )
    return hidden, weight_grad, feats_grad


def solution(mesh):
    placed = (
        P("feat", "blk"),
        P("feat", None),
        P("blk", None, None, None),
        P("blk", None),
        P("feat", "blk"),
    )
    return jax.shard_map(
        per_device,
        mesh=mesh,
        in_specs=placed,
        out_specs=(P("feat", "blk"), P("feat", None), P("feat", "blk")),
        check_vma=False,
    )
```
